32 devices in a mesh: dp: 2 (over core), expert: 4 (over z), tensor: 4 (over y, x).
Axes of the slice: x: 2, y: 2, z: 4, core: 2. Of those that a mesh axis runs over, the one named last changes fastest.
Arguments:
- layer_input: float32 [16384, 768], P(('dp', 'expert')), may hold values from -6 to 6
- cotangent: bfloat16 [16384, 768], P(('dp', 'expert')), may hold values from -6 to 6
- norm1_gain: bfloat16 [768], replicated, may hold values from 0.099609375 to 1.8984375
- w_query: bfloat16 [768, 768], P(None, 'tensor'), may hold values from -0.21875 to 0.21875
- w_key: bfloat16 [768, 768], P(None, 'tensor'), may hold values from -0.21875 to 0.21875
- w_value: bfloat16 [768, 768], P(None, 'tensor'), may hold values from -0.21875 to 0.21875
- w_output: bfloat16 [768, 768], P('tensor'), may hold values from -2.5 to 2.5
- bias_table: bfloat16 [32, 12], P(None, 'tensor'), may hold values from -6 to 6
- bucket: int32 [2047], replicated, may hold values from 0 to 31
- norm2_gain: bfloat16 [768], replicated, may hold values from 0.099609375 to 1.8984375
- router: bfloat16 [768, 4], replicated, may hold values from -0.15625 to 0.15625
- expert_index: int32 [16384, 1], P(('dp', 'expert')), may hold values from 0 to 3; in each aligned block of 512 rows (0 to 511, 512 to 1023, ...) at most 256 rows name the same one
- w_in: bfloat16 [4, 768, 3072], P('expert', None, 'tensor'), may hold values from -0.21875 to 0.21875
- w_out: bfloat16 [4, 3072, 768], P('expert', 'tensor'), may hold values from -0.4375 to 0.4375
Outputs:
- output: float32 [16384, 768], P(('dp', 'expert', 'tensor'))
- input_grad: float32 [16384, 768], P(('dp', 'expert', 'tensor'))
- grad_query: float32 [768, 768], P(None, 'tensor')
- grad_key: float32 [768, 768], P(None, 'tensor')
- grad_value: float32 [768, 768], P(None, 'tensor')
- grad_output_proj: float32 [768, 768], P('tensor')
- grad_bias_table: float32 [32, 12], P(None, 'tensor')
- grad_norm1: float32 [768], replicated
- grad_norm2: float32 [768], replicated
- grad_router: float32 [768, 4], replicated
- grad_w_in: float32 [4, 768, 3072], P('expert', None, 'tensor')
- grad_w_out: float32 [4, 3072, 768], P('expert', 'tensor')
The draws below stay inside these ranges and needn't reach their ends.
Inputs may be any that keep to these rules, and one draw needn't show every extreme that they name: `expert_index`: in each aligned block of 512 rows (the rows of one device) no expert is named by more than 256 rows.
All inputs are finite; a program needn't handle non-finite values.
Results may differ from the reference program's by a relative error of at most 0.015.
Values may be sent and summed in bfloat16 or wider, within the bound.
No kernel may reach another device: no remote copies, remote signals or barrier semaphores. Data moves between devices by JAX's collectives and lax.ppermute only.
A program may use at most 320 MiB of HBM per device.

```python
import math
import jax
import jax.numpy as jnp
import numpy as np
from jax import lax

D = 768
HEADS = 12
HEAD_DIM = 64
FF = 3072
NUM_BUCKETS = 32
SEQ_LEN = 1024
EXPERTS = 4
TOK_SRC = 512
CAP = 256
TOKENS = 16384


def place_ends(array, rng, smallest, high):
    longest = array.shape.index(max(array.shape))
    spots = []
    for shift in (0, 1):
        where = [jax.random.randint(jax.random.fold_in(rng, axis), (), 0, length) for axis, length in enumerate(array.shape)]
        where[longest] = (where[longest] + shift) % array.shape[longest]
        spots.append(tuple(where))
    return array.at[spots[0]].set(smallest).at[spots[1]].set(high)


def shard_levels(own_key, shape, shards, smallest, high):
    def one(dim, blocks):
        draws = jax.random.uniform(jax.random.fold_in(jax.random.fold_in(own_key, 6), dim), (blocks,), jnp.float32, smallest / len(shards), high / len(shards))
        return jnp.repeat(jnp.exp(draws), shape[dim] // blocks).reshape((-1,) + (1,) * (len(shape) - dim - 1))

    factor_of = one(*shards[0])
    for cut in shards[1:]:
        factor_of = factor_of * one(*cut)
    return factor_of


def assign_block(key, own, number, rows, number_of, top, most, slope):
    ranking = jax.random.permutation(key, number_of)
    heavy_load, usual = shares(number_of, rows * top, most, slope, True), shares(number_of, rows * top, most, slope, False)
    places = jnp.arange(number_of)

    def named(sizes, offset_by):
        used = int((sizes > 0).sum())
        fixed = max(1, used // 4)
        shifted = fixed + (places - fixed + offset_by * (used - fixed)) % max(1, number_of - fixed)
        return jnp.zeros((number_of,), jnp.int32).at[ranking[jnp.where(places < fixed, places, shifted)]].set(jnp.asarray(sizes, jnp.int32))

    sizes = jnp.where(number % 4 == 0, named(heavy_load, number // 4), named(usual, number - number // 4 - 1))
    mixed = jax.random.permutation(jax.random.fold_in(own, 3), number_of)
    source_of, taker = mixed[0:number_of // 2 * 2:2], mixed[1:number_of // 2 * 2:2]
    room = jnp.minimum(sizes[source_of] - 1, most - sizes[taker]) // 2
    room = jnp.where((source_of == ranking[0]) | (taker == ranking[0]) | (sizes[taker] == 0), 0, jnp.maximum(room, 0))
    shifted = jax.random.randint(jax.random.fold_in(own, 4), (number_of // 2,), 0, 1 << 20) % (room + 1)
    sizes = sizes.at[source_of].add(-shifted).at[taker].add(shifted)
    items = jnp.searchsorted(jnp.cumsum(sizes), jnp.arange(rows * top), side="right").astype(jnp.int32)
    grid = items.reshape(top, rows).T
    grid = grid[jax.random.permutation(jax.random.fold_in(own, 1), rows)]
    offset_by = jax.random.randint(jax.random.fold_in(own, 2), (rows, 1), 0, top)
    return jnp.take_along_axis(grid, (jnp.arange(top)[None, :] + offset_by) % top, axis=1)


def shares(number_of, total, limit, skew, full):
    portions = [(1 << 20) // math.isqrt(rank ** skew) + 1 for rank in range(1, number_of + 1)]
    largest = limit if full else min(limit, max(-(-total // number_of), total * portions[0] // sum(portions)))
    least = 1 if total - largest >= number_of - 1 else 0
    holding, spare = [largest] + [least] * (number_of - 1), total - largest - least * (number_of - 1)
    while spare > 0:
        candidates = [i for i in range(1, number_of) if holding[i] < largest] or [i for i in range(1, number_of) if holding[i] < limit]
        mass, remaining = sum([portions[i] for i in candidates]), spare
        for i in candidates:
            extra = min(limit - holding[i], max(1, remaining * portions[i] // mass), spare)
            holding[i] = holding[i] + extra
            spare = spare - extra
    return np.array(holding)


def scatter_about(key, extent, scale, limit, pieces=(), kind=jnp.bfloat16):
    level = shard_levels(key, extent, pieces, -0.22, 0.18) if pieces else 1.0
    array = jax.random.normal(key, extent, jnp.float32) * scale * level
    return jnp.minimum(jnp.maximum(array, -limit), limit).astype(kind)


def setup_inputs(seed: int = 0) -> dict:
    splits = jax.random.split(jax.random.key(seed), 15)
    layer_input = scatter_about(splits[0], (TOKENS, D), 1.0, 6.0, ((0, 8),), jnp.float32)
    cotangent = scatter_about(splits[1], (TOKENS, D), 1.0, 6.0, ((0, 8),))
    norm1_gain = jnp.clip(1.0 + 0.18 * jax.random.normal(splits[2], (D,), jnp.float32), 0.099609375, 1.8984375).astype(jnp.bfloat16)
    w_query = scatter_about(splits[3], (D, HEADS * HEAD_DIM), D ** -0.5, 0.21875, ((1, 4),))
    w_key = scatter_about(splits[4], (D, HEADS * HEAD_DIM), D ** -0.5, 0.21875, ((1, 4),))
    w_value = scatter_about(splits[5], (D, HEADS * HEAD_DIM), D ** -0.5, 0.21875, ((1, 4),))
    w_output = scatter_about(splits[6], (HEADS * HEAD_DIM, D), (max(1, HEADS * HEAD_DIM // 128)) ** -0.5, 2.5, ((0, 4),))
    bias_table = scatter_about(splits[7], (NUM_BUCKETS, HEADS), 1.0, 6.0, ((1, 4),))
    bucket = place_ends(jax.random.randint(splits[8], (2 * SEQ_LEN - 1,), 0, NUM_BUCKETS), jax.random.fold_in(splits[8], 1), 0, NUM_BUCKETS - 1).astype(jnp.int32)
    norm2_gain = jnp.clip(1.0 + 0.18 * jax.random.normal(splits[9], (D,), jnp.float32), 0.099609375, 1.8984375).astype(jnp.bfloat16)
    router = scatter_about(splits[10], (D, EXPERTS), (2 * D) ** -0.5, 0.15625)
    expert_index_keys = jax.random.split(jax.random.fold_in(splits[11], 1), TOKENS // TOK_SRC)
    expert_index_turns = jax.random.permutation(jax.random.fold_in(splits[11], 3), TOKENS // TOK_SRC)
    expert_index = jax.vmap(lambda own, number: assign_block(jax.random.fold_in(splits[11], 2), own, number, TOK_SRC, EXPERTS, 1, CAP, 1))(expert_index_keys, expert_index_turns).reshape((TOKENS, 1))
    w_in = scatter_about(splits[12], (EXPERTS, D, FF), D ** -0.5, 0.21875, ((0, 4), (2, 4)))
    w_out = scatter_about(splits[13], (EXPERTS, FF, D), (max(1, FF // (EXPERTS * EXPERTS))) ** -0.5, 0.4375, ((0, 4), (1, 4)))
    return dict(layer_input=layer_input, cotangent=cotangent, norm1_gain=norm1_gain, w_query=w_query, w_key=w_key, w_value=w_value, w_output=w_output, bias_table=bias_table, bucket=bucket, norm2_gain=norm2_gain, router=router, expert_index=expert_index, w_in=w_in, w_out=w_out)


EPSILON = 1e-06
HIGHEST = lax.Precision.HIGHEST

@jax.custom_vjp
def low(v):
    return lax.optimization_barrier(v.astype(jnp.bfloat16)).astype(jnp.float32)

@jax.custom_vjp
def low_back(v):
    return v

def low_keep(v):
    return (low(v), None)

def low_pass(kept, grad):
    return (grad,)

def back_keep(v):
    return (v, None)

def back_low(kept, grad):
    return (low(grad),)
low.defvjp(low_keep, low_pass)
low_back.defvjp(back_keep, back_low)

def matmul(left, right):
    return jnp.dot(left, right, precision=HIGHEST)

def rms_norm(rows, gain):
    return rows * lax.rsqrt(lax.optimization_barrier(jnp.mean(rows * rows, axis=-1, keepdims=True)) + EPSILON) * gain

def dispatch_index(routes):
    blocks = routes.reshape(-1, TOK_SRC)
    onehot = (blocks[:, :, None] == jnp.arange(EXPERTS, dtype=jnp.int32)[None, None, :]).astype(jnp.int32)
    slots = lax.optimization_barrier(jnp.sum((jnp.cumsum(onehot, axis=1) - onehot) * onehot, axis=-1))
    block_ids = jnp.arange(blocks.shape[0], dtype=jnp.int32)[:, None]
    return ((block_ids * EXPERTS + blocks) * CAP + slots).reshape(-1).astype(jnp.int32)

def layer_forward(inputs, norm_one, wquery, wkey, wvalue, woutput, table, norm_two, router_w, expert_first, expert_second, bucket, routes):
    token_count = inputs.shape[0]
    inner = HEADS * HEAD_DIM
    normed = low(rms_norm(inputs, norm_one))
    queries = low_back(low(matmul(normed, wquery)))
    keys_all = low_back(low(matmul(normed, wkey)))
    values_all = low_back(low(matmul(normed, wvalue)))
    positions = jnp.arange(SEQ_LEN, dtype=jnp.int32)
    offsets = (positions[None, :] - positions[:, None] + SEQ_LEN - 1).astype(jnp.int32)
    relative = jnp.transpose(table[bucket][offsets], (2, 0, 1))
    seq_count = token_count // SEQ_LEN
    head_shape = (seq_count, SEQ_LEN, HEADS, HEAD_DIM)

    def attend(blocks):
        query_blk, key_blk, value_blk = blocks
        scores = jnp.einsum('qhd,khd->hqk', query_blk, key_blk, precision=HIGHEST) * HEAD_DIM ** (-0.5)
        scores = low_back(scores + relative)
        weights = low(jax.nn.softmax(scores, axis=-1))
        mixed_rows = jnp.einsum('hqk,khd->qhd', weights, value_blk, precision=HIGHEST)
        return low_back(low(mixed_rows)).reshape(SEQ_LEN, inner)
    heads_out = lax.map(jax.checkpoint(attend), (queries.reshape(head_shape), keys_all.reshape(head_shape), values_all.reshape(head_shape)))
    attention = low_back(matmul(heads_out.reshape(token_count, inner), woutput))
    residual = inputs + attention
    normed_two = rms_norm(residual, norm_two)
    router_probs = jax.nn.softmax(matmul(normed_two, router_w), axis=-1)
    chosen = routes[:, None] == jnp.arange(EXPERTS, dtype=jnp.int32)[None, :]
    gate_value = low(lax.optimization_barrier(jnp.sum(jnp.where(chosen, router_probs, 0.0), axis=-1)))
    expert_rows = low_back(low(normed_two))
    flat = dispatch_index(routes)
    block_count = token_count // TOK_SRC
    buffer = jnp.zeros((block_count * EXPERTS * CAP, D), expert_rows.dtype).at[flat].set(expert_rows)
    buffer = jnp.transpose(buffer.reshape(block_count, EXPERTS, CAP, D), (1, 0, 2, 3)).reshape(EXPERTS, block_count * CAP, D)

    def expert_apply(blocks):
        rows, first, second = blocks
        hidden = low_back(matmul(rows, first))
        activated = low(jax.nn.gelu(hidden, approximate=True))
        return low_back(low(matmul(activated, second)))
    results = lax.map(jax.checkpoint(expert_apply), (buffer, expert_first, expert_second))
    results = jnp.transpose(results.reshape(EXPERTS, block_count, CAP, D), (1, 0, 2, 3)).reshape(-1, D)
    return residual + gate_value[:, None] * results[flat]

def reference(layer_input, cotangent, norm1_gain, w_query, w_key, w_value, w_output, bias_table, bucket, norm2_gain, router, expert_index, w_in, w_out):
    routes = expert_index[:, 0].astype(jnp.int32)

    def forward(inputs, norm_one, wquery, wkey, wvalue, woutput, table, norm_two, router_w, expert_first, expert_second):
        return layer_forward(inputs, norm_one, wquery, wkey, wvalue, woutput, table, norm_two, router_w, expert_first, expert_second, bucket, routes)
    output, backward = jax.vjp(forward, layer_input.astype(jnp.float32), norm1_gain.astype(jnp.float32), w_query.astype(jnp.float32), w_key.astype(jnp.float32), w_value.astype(jnp.float32), w_output.astype(jnp.float32), bias_table.astype(jnp.float32), norm2_gain.astype(jnp.float32), router.astype(jnp.float32), w_in.astype(jnp.float32), w_out.astype(jnp.float32))
    grads = backward(cotangent.astype(jnp.float32))
    return (output, grads[0], grads[2], grads[3], grads[4], grads[5], grads[6], grads[1], grads[7], grads[8], grads[9], grads[10])
```

```python
import functools
import jax
import jax.numpy as jnp
from jax import lax
from jax.sharding import PartitionSpec as P
from jax.experimental import pallas as pl
from jax.experimental.pallas import tpu as pltpu

HEAD_DIM = 64
NUM_BUCKETS = 32
EPSILON = 1e-06
HIGHEST = lax.Precision.HIGHEST
CHUNK = 512
BAND = 128


def dot_nt(a, b):
    return lax.dot_general(a, b, (((1,), (1,)), ((), ())), preferred_element_type=jnp.float32)


def dot_nn(a, b):
    return lax.dot_general(a, b, (((1,), (0,)), ((), ())), preferred_element_type=jnp.float32)


def dot_tn(a, b):
    return lax.dot_general(a, b, (((0,), (0,)), ((), ())), preferred_element_type=jnp.float32)


def fill_band(band, vector):
    span = vector.shape[1]
    rows = jnp.broadcast_to(vector, (8, span))
    rows = pltpu.roll(rows, span - (BAND - 1), 1)
    index = lax.broadcasted_iota(jnp.int32, (8, span), 0)
    for step in (1, 2, 4):
        rows = jnp.where((index & step) != 0, pltpu.roll(rows, step, 1), rows)
    band[0:8, :] = rows
    step = 8
    while step < BAND:
        band[step : 2 * step, :] = pltpu.roll(band[0:step, :], step, 1)
        step *= 2


def fold_band(band):
    span = band.shape[1]
    step = BAND // 2
    while step >= 8:
        band[0:step, :] += pltpu.roll(band[step : 2 * step, :], span - step, 1)
        step //= 2
    rows = band[0:8, :]
    index = lax.broadcasted_iota(jnp.int32, (8, span), 0)
    for step in (1, 2, 4):
        rows = jnp.where((index & step) != 0, pltpu.roll(rows, span - step, 1), rows)
    total = jnp.sum(rows, axis=0, keepdims=True)
    return pltpu.roll(total, BAND - 1, 1)


def attend_kernel(q_ref, k_ref, v_ref, vec_ref, out_ref, log_ref, band):
    seq = k_ref.shape[3]
    own = out_ref.shape[3]

    @pl.when(pl.program_id(1) == 0)
    def _():
        fill_band(band, vec_ref[0])

    keys = k_ref[0, 0].T
    values = v_ref[0, 0]
    for start in range(0, seq, CHUNK):
        queries = q_ref[0, 0, :, start : start + CHUNK] * jnp.bfloat16(HEAD_DIM ** -0.5)
        raw = dot_nn(keys, queries)
        parts = []
        for low in range(0, seq, BAND):
            at = start - low + seq - BAND
            parts.append(raw[low : low + BAND] + band[:, at : at + CHUNK])
        peak = functools.reduce(jnp.maximum, parts)
        peak = jnp.max(peak, axis=0, keepdims=True)
        parts = [jnp.exp(part - peak) for part in parts]
        total = jnp.sum(functools.reduce(jnp.add, parts), axis=0, keepdims=True)
        weights = jnp.concatenate([part.astype(jnp.bfloat16) for part in parts], axis=0)
        mixed = dot_nn(values, weights) / total
        out_ref[start // own, 0, :, start % own : start % own + CHUNK] = mixed.astype(jnp.bfloat16)
        log_ref[0, 0, :, start : start + CHUNK] = peak + jnp.log(total)


def attend(projected, vectors, own):
    heads, seq = vectors.shape[0], vectors.shape[2] // 2
    seqs = projected.shape[1] // seq
    blocks = seq // own
    part = lambda p: pl.BlockSpec((1, 1, HEAD_DIM, seq), lambda h, s, p=p: (p, h, 0, s))
    proj = projected.reshape(3, heads, HEAD_DIM, seqs * seq)
    return pl.pallas_call(
        attend_kernel,
        grid=(heads, seqs),
        in_specs=[part(0), part(1), part(2), pl.BlockSpec((1, 1, 2 * seq), lambda h, s: (h, 0, 0))],
        out_specs=[
            pl.BlockSpec((blocks, 1, HEAD_DIM, own), lambda h, s: (s, h, 0, 0)),
            pl.BlockSpec((1, 1, 1, seq), lambda h, s: (h, s, 0, 0)),
        ],
        out_shape=[
            jax.ShapeDtypeStruct((seqs * blocks, heads, HEAD_DIM, own), jnp.bfloat16),
            jax.ShapeDtypeStruct((heads, seqs, 1, seq), jnp.float32),
        ],
        scratch_shapes=[pltpu.VMEM((BAND, 2 * seq), jnp.float32)],
        compiler_params=pltpu.CompilerParams(vmem_limit_bytes=48 * 2**20),
        cost_estimate=pl.CostEstimate(
            flops=4 * heads * seqs * seq * seq * HEAD_DIM * 4,
            bytes_accessed=4 * heads * seqs * seq * HEAD_DIM * 2,
            transcendentals=heads * seqs * seq * seq,
        ),
    )(proj, proj, proj, vectors)


def attend_back_kernel(q_ref, k_ref, v_ref, o_ref, g_ref, log_ref, vec_ref, out_ref, diag_ref, band, fold, dk, dv):
    seq = k_ref.shape[3]
    own = out_ref.shape[4]
    scale = HEAD_DIM ** -0.5

    @pl.when(pl.program_id(1) == 0)
    def _():
        fill_band(band, vec_ref[0])
        fold[...] = jnp.zeros_like(fold)

    keys_t = k_ref[0, 0]
    keys = keys_t.T
    values = v_ref[0, 0].T
    for start in range(0, seq, CHUNK):
        block, inner = start // own, start % own
        queries = q_ref[0, 0, :, start : start + CHUNK] * jnp.bfloat16(scale)
        grads = g_ref[block, 0, :, inner : inner + CHUNK]
        mixed = o_ref[block, 0, :, inner : inner + CHUNK]
        delta = jnp.sum(grads.astype(jnp.float32) * mixed.astype(jnp.float32), axis=0, keepdims=True)
        logs = log_ref[0, 0, :, start : start + CHUNK]
        raw = dot_nn(keys, queries)
        grad_weights = dot_nn(values, grads)
        low_weights, low_scores = [], []
        for low in range(0, seq, BAND):
            at = start - low + seq - BAND
            weights = jnp.exp(raw[low : low + BAND] + band[:, at : at + CHUNK] - logs)
            scores = weights * (grad_weights[low : low + BAND] - delta)
            fold[:, at : at + CHUNK] += scores
            low_weights.append(weights.astype(jnp.bfloat16))
            low_scores.append(scores.astype(jnp.bfloat16))
        weights = jnp.concatenate(low_weights, axis=0)
        scores = jnp.concatenate(low_scores, axis=0)
        grad_q = dot_nn(keys_t, scores) * scale
        out_ref[block, 0, 0, :, inner : inner + CHUNK] = grad_q.astype(jnp.bfloat16)
        if start == 0:
            dk[...] = dot_nt(queries, scores)
            dv[...] = dot_nt(grads, weights)
        else:
            dk[...] += dot_nt(queries, scores)
            dv[...] += dot_nt(grads, weights)
    for block in range(seq // own):
        out_ref[block, 1, 0] = dk[:, block * own : (block + 1) * own].astype(jnp.bfloat16)
        out_ref[block, 2, 0] = dv[:, block * own : (block + 1) * own].astype(jnp.bfloat16)

    @pl.when(pl.program_id(1) == pl.num_programs(1) - 1)
    def _():
        diag_ref[0] = fold_band(fold)


def attend_back(projected, vectors, mixed, grads, logs):
    heads, seq = vectors.shape[0], vectors.shape[2] // 2
    seqs = projected.shape[1] // seq
    own = mixed.shape[3]
    blocks = seq // own
    part = lambda p: pl.BlockSpec((1, 1, HEAD_DIM, seq), lambda h, s, p=p: (p, h, 0, s))
    side = pl.BlockSpec((blocks, 1, HEAD_DIM, own), lambda h, s: (s, h, 0, 0))
    vec = pl.BlockSpec((1, 1, 2 * seq), lambda h, s: (h, 0, 0))
    proj = projected.reshape(3, heads, HEAD_DIM, seqs * seq)
    return pl.pallas_call(
        attend_back_kernel,
        grid=(heads, seqs),
        in_specs=[part(0), part(1), part(2), side, side,
                  pl.BlockSpec((1, 1, 1, seq), lambda h, s: (h, s, 0, 0)), vec],
        out_specs=[
            pl.BlockSpec((blocks, 3, 1, HEAD_DIM, own), lambda h, s: (s, 0, h, 0, 0)),
            vec,
        ],
        out_shape=[
            jax.ShapeDtypeStruct((seqs * blocks, 3, heads, HEAD_DIM, own), jnp.bfloat16),
            jax.ShapeDtypeStruct((heads, 1, 2 * seq), jnp.float32),
        ],
        scratch_shapes=[
            pltpu.VMEM((BAND, 2 * seq), jnp.float32),
            pltpu.VMEM((BAND, 2 * seq), jnp.float32),
            pltpu.VMEM((HEAD_DIM, seq), jnp.float32),
            pltpu.VMEM((HEAD_DIM, seq), jnp.float32),
        ],
        compiler_params=pltpu.CompilerParams(vmem_limit_bytes=48 * 2**20),
        cost_estimate=pl.CostEstimate(
            flops=10 * heads * seqs * seq * seq * HEAD_DIM * 4,
            bytes_accessed=8 * heads * seqs * seq * HEAD_DIM * 2,
            transcendentals=heads * seqs * seq * seq,
        ),
    )(proj, proj, proj, mixed, grads, logs, vectors)


def gelu_parts(values):
    root = 0.7978845608028654
    square = values * values
    bend = jnp.tanh(root * values * (1.0 + 0.044715 * square))
    half = 0.5 * (1.0 + bend)
    slope = half + 0.5 * values * (1.0 - bend * bend) * (root * (1.0 + 3.0 * 0.044715 * square))
    return values * half, slope


def expert_kernel(x_ref, g_ref, gate_ref, in_ref, out_ref, act_ref, pre_ref, low_ref, res_ref, back_ref, gg_ref, res_sum, back_sum):
    step = pl.program_id(0)
    rows = x_ref.shape[0]
    tile = min(rows, 256)

    @pl.when(step == 0)
    def _():
        low_ref[...] = (gate_ref[...] * g_ref[...].astype(jnp.float32)).astype(jnp.bfloat16)
        res_sum[...] = jnp.zeros_like(res_sum)
        back_sum[...] = jnp.zeros_like(back_sum)

    first = in_ref[0]
    second = out_ref[0]
    for start in range(0, rows, tile):
        span = pl.ds(start, tile)
        active, slope = gelu_parts(dot_nn(x_ref[span, :], first))
        active = active.astype(jnp.bfloat16)
        act_ref[0, span, :] = active
        res_sum[span, :] += dot_nn(active, second)
        pre = (dot_nt(low_ref[span, :], second) * slope).astype(jnp.bfloat16)
        pre_ref[0, span, :] = pre
        back_sum[span, :] += dot_nt(pre, first)

    @pl.when(step == pl.num_programs(0) - 1)
    def _():
        res_ref[...] = res_sum[...].astype(jnp.bfloat16)
        back_ref[...] = back_sum[...].astype(jnp.bfloat16)
        gg_ref[...] = jnp.sum(res_sum[...] * g_ref[...].astype(jnp.float32), axis=1, keepdims=True)


def expert_apply(rows, grads, gates, first, second):
    count, width = rows.shape
    steps, _, hidden = first.shape
    whole = pl.BlockSpec((count, width), lambda i: (0, 0))
    column = pl.BlockSpec((count, 1), lambda i: (0, 0))
    kept = pl.BlockSpec((1, count, hidden), lambda i: (i, 0, 0))
    return pl.pallas_call(
        expert_kernel,
        grid=(steps,),
        in_specs=[
            whole,
            whole,
            column,
            pl.BlockSpec((1, width, hidden), lambda i: (i, 0, 0)),
            pl.BlockSpec((1, hidden, width), lambda i: (i, 0, 0)),
        ],
        out_specs=[kept, kept, whole, whole, whole, column],
        out_shape=[
            jax.ShapeDtypeStruct((steps, count, hidden), jnp.bfloat16),
            jax.ShapeDtypeStruct((steps, count, hidden), jnp.bfloat16),
            jax.ShapeDtypeStruct((count, width), jnp.bfloat16),
            jax.ShapeDtypeStruct((count, width), jnp.bfloat16),
            jax.ShapeDtypeStruct((count, width), jnp.bfloat16),
            jax.ShapeDtypeStruct((count, 1), jnp.float32),
        ],
        scratch_shapes=[
            pltpu.VMEM((count, width), jnp.float32),
            pltpu.VMEM((count, width), jnp.float32),
        ],
        compiler_params=pltpu.CompilerParams(vmem_limit_bytes=50 * 2**20),
        cost_estimate=pl.CostEstimate(
            flops=8 * count * width * hidden * steps,
            bytes_accessed=4 * (count + width) * hidden * steps,
            transcendentals=count * hidden * steps,
        ),
    )(rows, grads, gates, first, second)


def weight_kernel(x_ref, low_ref, act_ref, pre_ref, out_ref, x_turned, low_turned):
    @pl.when(pl.program_id(0) == 0)
    def _():
        x_turned[...] = x_ref[...].T
        low_turned[...] = low_ref[...].T

    out_ref[0, 0] = dot_nn(x_turned[...], pre_ref[0]).astype(jnp.bfloat16)
    out_ref[0, 1] = dot_nn(low_turned[...], act_ref[0]).astype(jnp.bfloat16)


def expert_weights(rows, low, act, pre):
    count, width = rows.shape
    steps, _, hidden = act.shape
    whole = pl.BlockSpec((count, width), lambda i: (0, 0))
    kept = pl.BlockSpec((1, count, hidden), lambda i: (i, 0, 0))
    return pl.pallas_call(
        weight_kernel,
        grid=(steps,),
        in_specs=[whole, whole, kept, kept],
        out_specs=pl.BlockSpec((1, 2, width, hidden), lambda i: (i, 0, 0, 0)),
        out_shape=jax.ShapeDtypeStruct((steps, 2, width, hidden), jnp.bfloat16),
        scratch_shapes=[
            pltpu.VMEM((width, count), jnp.bfloat16),
            pltpu.VMEM((width, count), jnp.bfloat16),
        ],
        compiler_params=pltpu.CompilerParams(vmem_limit_bytes=50 * 2**20),
        cost_estimate=pl.CostEstimate(
            flops=4 * count * width * hidden * steps,
            bytes_accessed=4 * (count + width) * hidden * steps,
            transcendentals=0,
        ),
    )(rows, low, act, pre)


def inverse_rms(rows):
    return lax.rsqrt(jnp.mean(rows * rows, axis=-1, keepdims=True) + EPSILON)


def norm_backward(grad_normed, gain, normed_hat, inv_scale):
    scaled = grad_normed * gain
    return inv_scale * (scaled - normed_hat * jnp.mean(scaled * normed_hat, axis=-1, keepdims=True))


def swap(array, axis, offset):
    count = lax.axis_size(axis)
    return lax.ppermute(array, axis, [(i, i ^ offset) for i in range(count)])


def trade(array, axis):
    return lax.all_to_all(array, axis, 0, 0, tiled=True)


def spread(array, axis):
    return trade(jnp.broadcast_to(array[None], (lax.axis_size(axis),) + array.shape), axis)


def split_low(values):
    high = values.astype(jnp.bfloat16)
    return high, (values - high.astype(jnp.float32)).astype(jnp.bfloat16)


def sum_copies(partial):
    rows, columns = partial.shape
    experts = lax.axis_size("expert")
    rank = lax.axis_index("dp")
    half = rows // 2
    mine = lax.dynamic_slice_in_dim(partial, rank * half, half, 0)
    other = lax.dynamic_slice_in_dim(partial, (1 - rank) * half, half, 0).astype(jnp.bfloat16)
    mine = (mine + swap(other, "dp", 1).astype(jnp.float32)).astype(jnp.bfloat16)
    shares = trade(mine.reshape(experts, half // experts, columns), "expert")
    share = jnp.sum(shares.astype(jnp.float32), axis=0).astype(jnp.bfloat16)
    mine = spread(share, "expert").reshape(half, columns)
    other = swap(mine, "dp", 1)
    first = rank == 0
    return jnp.concatenate(
        [jnp.where(first, mine, other), jnp.where(first, other, mine)], axis=0
    ).astype(jnp.float32)


def on_device(
    layer_input,
    cotangent,
    norm1_gain,
    w_query,
    w_key,
    w_value,
    w_output,
    bias_table,
    bucket,
    norm2_gain,
    router,
    expert_index,
    w_in,
    w_out,
):
    group_rows, width = layer_input.shape
    tensor_count = lax.axis_size("tensor")
    tensor_rank = lax.axis_index("tensor")
    dp_rank = lax.axis_index("dp")
    own_rows = group_rows // tensor_count
    own_start = tensor_rank * own_rows
    local_heads = bias_table.shape[1]
    inner = local_heads * HEAD_DIM
    experts = router.shape[1]
    capacity = 2 * own_rows // experts
    slots = experts * capacity

    hidden = w_in.shape[2]
    half = hidden // 2
    first_mine = lax.dynamic_slice_in_dim(w_in[0], dp_rank * half, half, 1)
    first_other = lax.dynamic_slice_in_dim(w_in[0], (1 - dp_rank) * half, half, 1)
    second_mine = lax.dynamic_slice_in_dim(w_out[0], dp_rank * half, half, 0)
    second_other = lax.dynamic_slice_in_dim(w_out[0], (1 - dp_rank) * half, half, 0)
    w_joined = jnp.concatenate([w_query, w_key, w_value], axis=1)
    w_joined_t = w_joined.T
    output_full = spread(w_output, "tensor").reshape(tensor_count * inner, width)

    routes = lax.dynamic_slice_in_dim(expert_index[:, 0], own_start, own_rows, 0)
    own_hot = routes[:, None] == jnp.arange(experts, dtype=jnp.int32)[None, :]
    row_ids = jnp.arange(own_rows, dtype=jnp.int32)
    earlier = (row_ids[None, :] < row_ids[:, None]).astype(jnp.bfloat16)
    before = jnp.dot(earlier, own_hot.astype(jnp.bfloat16), preferred_element_type=jnp.float32)
    own_hot = own_hot.astype(jnp.float32)
    slot = jnp.sum(before * own_hot, axis=-1).astype(jnp.int32)
    flat = routes * capacity + slot
    place_hot = (jnp.arange(slots, dtype=jnp.int32)[:, None] == flat[None, :]).astype(jnp.bfloat16)
    cot_low = lax.dynamic_slice_in_dim(cotangent, own_start, own_rows, 0)
    cot_own = cot_low.astype(jnp.float32)
    grad_send = jnp.dot(place_hot, cot_low, preferred_element_type=jnp.float32).astype(jnp.bfloat16)
    grad_in = trade(grad_send.reshape(experts, capacity, width), "expert").reshape(slots, width)

    gain_one = norm1_gain.astype(jnp.float32)
    inv_one = inverse_rms(layer_input)
    hat_one = layer_input * inv_one
    normed_one = (hat_one * gain_one).astype(jnp.bfloat16)
    projected = dot_nt(w_joined_t, normed_one).astype(jnp.bfloat16)
    turned = jnp.concatenate([bucket[::-1], jnp.full((1,), -1, jnp.int32)])
    bucket_hot = jnp.arange(NUM_BUCKETS, dtype=jnp.int32)[:, None] == turned[None, :]
    vectors = dot_tn(bias_table, bucket_hot.astype(jnp.bfloat16))[:, None, :]
    mixed, logs = attend(projected, vectors, own_rows)
    mixed_own = trade(mixed.reshape(tensor_count, inner, own_rows), "tensor").reshape(
        tensor_count * inner, own_rows
    )

    input_own = lax.dynamic_slice_in_dim(layer_input, own_start, own_rows, 0)
    residual = input_own + dot_tn(mixed_own, output_full)
    gain_two = norm2_gain.astype(jnp.float32)
    inv_two = inverse_rms(residual)
    hat_two = residual * inv_two
    normed_two = hat_two * gain_two
    router_wide = router.astype(jnp.float32)
    router_probs = jax.nn.softmax(jnp.dot(normed_two, router_wide, precision=HIGHEST), axis=-1)
    gate_full = jnp.sum(router_probs * own_hot, axis=-1)
    gate_low = gate_full.astype(jnp.bfloat16)
    send_rows = dot_nn(place_hot, normed_two.astype(jnp.bfloat16)).astype(jnp.bfloat16)
    send_gates = dot_nn(place_hot, gate_low[:, None]).astype(jnp.bfloat16)
    gate_rows = jnp.pad(send_gates.reshape(experts, 1, capacity), ((0, 0), (0, 7), (0, width - capacity)))
    sent = jnp.concatenate([send_rows.reshape(experts, capacity, width), gate_rows], axis=1)
    arrived = trade(sent, "expert")
    rows_in = arrived[:, :capacity].reshape(slots, width)
    gates_in = arrived[:, capacity, :capacity].reshape(slots, 1).astype(jnp.float32)

    first_parts, second_parts = [first_mine], [second_mine]
    for offset in range(1, tensor_count):
        first_parts.append(swap(first_mine, "tensor", offset))
        second_parts.append(swap(second_mine, "tensor", offset))
    first_rest = [first_other] + [swap(part, "dp", 1) for part in first_parts[1:]]
    second_rest = [second_other] + [swap(part, "dp", 1) for part in second_parts[1:]]
    first_all = jnp.stack(first_parts + first_rest)
    second_all = jnp.stack(second_parts + second_rest)

    act, pre, low_grads, result, back, grad_gates = expert_apply(
        rows_in, grad_in, gates_in, first_all, second_all
    )
    gate_high, gate_rest = split_low(grad_gates[:, 0])
    gate_pair = jnp.stack(
        [gate_high.reshape(experts, capacity), gate_rest.reshape(experts, capacity)], axis=1
    )
    gate_pair = jnp.pad(gate_pair, ((0, 0), (0, 6), (0, width - capacity)))
    back_sent = jnp.concatenate([back.reshape(experts, capacity, width), gate_pair], axis=1)
    back_got = trade(back_sent, "expert")
    weight_parts = expert_weights(rows_in, low_grads, act, pre)

    grad_normed_two = dot_tn(place_hot, back_got[:, :capacity].reshape(slots, width))
    pair_got = jnp.swapaxes(back_got[:, capacity : capacity + 2, :capacity], 1, 2).reshape(slots, 2)
    grad_gate = jnp.sum(dot_tn(place_hot, pair_got), axis=-1)
    grad_logits = router_probs * (own_hot - gate_full[:, None]) * grad_gate[:, None]
    grad_router = jnp.einsum("td,te->de", normed_two, grad_logits, precision=HIGHEST)
    grad_normed_two = grad_normed_two + jnp.einsum(
        "te,de->td", grad_logits, router_wide, precision=HIGHEST
    )
    grad_norm_two = jnp.sum(grad_normed_two * hat_two, axis=0)
    grad_residual = cot_own + norm_backward(grad_normed_two, gain_two, hat_two, inv_two)
    grad_low = grad_residual.astype(jnp.bfloat16)
    grad_heads = dot_nt(output_full, grad_low).astype(jnp.bfloat16)
    heads_got = trade(grad_heads.reshape(tensor_count, inner, own_rows), "tensor")

    result, heads_got = lax.optimization_barrier((result, heads_got))
    returned = trade(result.reshape(experts, capacity, width), "expert").reshape(slots, width)
    output = residual + gate_low.astype(jnp.float32)[:, None] * dot_tn(place_hot, returned)

    head_shape = (tensor_count, local_heads, HEAD_DIM, own_rows)
    grad_projected, diagonals = attend_back(
        projected, vectors, mixed, heads_got.reshape(head_shape), logs
    )
    grad_projected = grad_projected.reshape(tensor_count, 3 * inner, own_rows)
    joined_full = spread(w_joined_t, "tensor").reshape(tensor_count * 3 * inner, width)
    grad_got = trade(grad_projected, "tensor").reshape(tensor_count * 3 * inner, own_rows)
    grad_normed_one = dot_tn(grad_got, joined_full)
    hat_own = lax.dynamic_slice_in_dim(hat_one, own_start, own_rows, 0)
    inv_own = lax.dynamic_slice_in_dim(inv_one, own_start, own_rows, 0)
    input_grad = grad_residual + norm_backward(grad_normed_one, gain_one, hat_own, inv_own)

    grad_wo = dot_nn(mixed_own, grad_low).astype(jnp.bfloat16)
    grad_wo = trade(grad_wo.reshape(tensor_count, inner, width), "tensor")
    grad_wo = sum_copies(jnp.sum(grad_wo.astype(jnp.float32), axis=0))

    grad_joined = jnp.einsum(
        "bcn,bnd->dc",
        grad_projected,
        normed_one.reshape(tensor_count, own_rows, width),
        preferred_element_type=jnp.float32,
    )
    norm_one = jnp.sum(grad_joined * w_joined.astype(jnp.float32), axis=1) / gain_one
    norm_one = norm_one + sum(swap(norm_one, "tensor", k) for k in range(1, tensor_count))
    grad_table = jnp.einsum(
        "br,hr->bh", bucket_hot.astype(jnp.float32), diagonals[:, 0], precision=HIGHEST
    ).reshape(-1)
    table_size = grad_table.shape[0]
    extra = jnp.stack(
        [norm_one, jnp.pad(grad_table, (0, width - table_size))], axis=1
    )
    extra_high, extra_low = split_low(extra)
    extra = jnp.concatenate([extra_high, extra_low], axis=1).astype(jnp.float32)
    used = 3 * inner
    joined = jnp.concatenate(
        [grad_joined, extra, jnp.zeros((width, -(used + 4) % 128), jnp.float32)], axis=1
    )
    joined = sum_copies(joined)
    grad_norm_one = joined[:, used] + joined[:, used + 2]
    grad_table = (joined[:table_size, used + 1] + joined[:table_size, used + 3]).reshape(
        NUM_BUCKETS, local_heads
    )
    grad_norm_two, grad_router = lax.psum(
        (grad_norm_two, grad_router), ("dp", "expert", "tensor")
    )

    mine, other = weight_parts[:tensor_count], weight_parts[tensor_count:]
    mine = mine.astype(jnp.float32) + swap(other, "dp", 1).astype(jnp.float32)
    mine = mine.astype(jnp.bfloat16)
    total = mine[0].astype(jnp.float32)
    for offset in range(1, tensor_count):
        total = total + swap(mine[offset], "tensor", offset).astype(jnp.float32)
    total = total.astype(jnp.bfloat16)
    rest = swap(total, "dp", 1)
    first = dp_rank == 0
    both = jnp.concatenate(
        [jnp.where(first, total, rest), jnp.where(first, rest, total)], axis=2
    ).astype(jnp.float32)
    return (
        output,
        input_grad,
        joined[:, :inner],
        joined[:, inner : 2 * inner],
        joined[:, 2 * inner : used],
        grad_wo,
        grad_table,
        grad_norm_one,
        grad_norm_two,
        grad_router,
        both[0][None],
        both[1].T[None],
    )


def solution(mesh):
    return jax.shard_map(
        on_device,
        mesh=mesh,
        in_specs=(
            P(("dp", "expert"), None),
            P(("dp", "expert"), None),
            P(),
            P(None, "tensor"),
            P(None, "tensor"),
            P(None, "tensor"),
            P("tensor", None),
            P(None, "tensor"),
            P(),
            P(),
            P(),
            P(("dp", "expert"), None),
            P("expert", None, "tensor"),
            P("expert", "tensor", None),
        ),
        out_specs=(
            P(("dp", "expert", "tensor"), None),
            P(("dp", "expert", "tensor"), None),
            P(None, "tensor"),
            P(None, "tensor"),
            P(None, "tensor"),
            P("tensor", None),
            P(None, "tensor"),
            P(),
            P(),
            P(),
            P("expert", None, "tensor"),
            P("expert", "tensor", None),
        ),
        check_vma=False,
    )
```

```python
import functools
import jax
import jax.numpy as jnp
from jax import lax
from jax.sharding import PartitionSpec as P
from jax.experimental import pallas as pl
from jax.experimental.pallas import tpu as pltpu

HEAD_DIM = 64
NUM_BUCKETS = 32
EPSILON = 1e-06
HIGHEST = lax.Precision.HIGHEST
CHUNK = 512


def cost(work):
    return pl.CostEstimate(flops=work, bytes_accessed=work // 1024, transcendentals=0)

BAND = 128


def dot_nt(a, b):
    return lax.dot_general(a, b, (((1,), (1,)), ((), ())), preferred_element_type=jnp.float32)


def dot_nn(a, b):
    return lax.dot_general(a, b, (((1,), (0,)), ((), ())), preferred_element_type=jnp.float32)


def dot_tn(a, b):
    return lax.dot_general(a, b, (((0,), (0,)), ((), ())), preferred_element_type=jnp.float32)


def fill_band(band, vector):
    span = vector.shape[1]
    rows = jnp.broadcast_to(vector, (8, span))
    rows = pltpu.roll(rows, span - (BAND - 1), 1)
    index = lax.broadcasted_iota(jnp.int32, (8, span), 0)
    for step in (1, 2, 4):
        rows = jnp.where((index & step) != 0, pltpu.roll(rows, step, 1), rows)
    band[0:8, :] = rows
    step = 8
    while step < BAND:
        band[step : 2 * step, :] = pltpu.roll(band[0:step, :], step, 1)
        step *= 2


def fold_band(band):
    span = band.shape[1]
    step = BAND // 2
    while step >= 8:
        band[0:step, :] += pltpu.roll(band[step : 2 * step, :], span - step, 1)
        step //= 2
    rows = band[0:8, :]
    index = lax.broadcasted_iota(jnp.int32, (8, span), 0)
    for step in (1, 2, 4):
        rows = jnp.where((index & step) != 0, pltpu.roll(rows, span - step, 1), rows)
    total = jnp.sum(rows, axis=0, keepdims=True)
    return pltpu.roll(total, BAND - 1, 1)


def attend_kernel(q_ref, k_ref, v_ref, vec_ref, out_ref, log_ref, band):
    seq = k_ref.shape[3]
    own = out_ref.shape[3]

    @pl.when(pl.program_id(1) == 0)
    def _():
        fill_band(band, vec_ref[0])

    keys = k_ref[0, 0].T
    values = v_ref[0, 0]
    for start in range(0, seq, CHUNK):
        queries = q_ref[0, 0, :, start : start + CHUNK] * jnp.bfloat16(HEAD_DIM ** -0.5)
        raw = dot_nn(keys, queries)
        parts = []
        for low in range(0, seq, BAND):
            at = start - low + seq - BAND
            parts.append(raw[low : low + BAND] + band[:, at : at + CHUNK])
        peak = functools.reduce(jnp.maximum, parts)
        peak = jnp.max(peak, axis=0, keepdims=True)
        parts = [jnp.exp(part - peak) for part in parts]
        total = jnp.sum(functools.reduce(jnp.add, parts), axis=0, keepdims=True)
        weights = jnp.concatenate([part.astype(jnp.bfloat16) for part in parts], axis=0)
        mixed = dot_nn(values, weights) / total
        out_ref[start // own, 0, :, start % own : start % own + CHUNK] = mixed.astype(jnp.bfloat16)
        log_ref[0, 0, :, start : start + CHUNK] = peak + jnp.log(total)


def attend(projected, vectors, own):
    heads, seq = vectors.shape[0], vectors.shape[2] // 2
    seqs = projected.shape[1] // seq
    blocks = seq // own
    part = lambda p: pl.BlockSpec((1, 1, HEAD_DIM, seq), lambda h, s, p=p: (p, h, 0, s))
    proj = projected.reshape(3, heads, HEAD_DIM, seqs * seq)
    return pl.pallas_call(
        attend_kernel,
        grid=(heads, seqs),
        in_specs=[part(0), part(1), part(2), pl.BlockSpec((1, 1, 2 * seq), lambda h, s: (h, 0, 0))],
        out_specs=[
            pl.BlockSpec((blocks, 1, HEAD_DIM, own), lambda h, s: (s, h, 0, 0)),
            pl.BlockSpec((1, 1, 1, seq), lambda h, s: (h, s, 0, 0)),
        ],
        out_shape=[
            jax.ShapeDtypeStruct((seqs * blocks, heads, HEAD_DIM, own), jnp.bfloat16),
            jax.ShapeDtypeStruct((heads, seqs, 1, seq), jnp.float32),
        ],
        scratch_shapes=[pltpu.VMEM((BAND, 2 * seq), jnp.float32)],
        compiler_params=pltpu.CompilerParams(vmem_limit_bytes=48 * 2**20),
        cost_estimate=cost(16 * heads * seqs * seq * seq * HEAD_DIM),
    )(proj, proj, proj, vectors)


def attend_back_kernel(q_ref, k_ref, v_ref, o_ref, g_ref, log_ref, vec_ref, out_ref, diag_ref, band, fold, dk, dv):
    seq = k_ref.shape[3]
    own = out_ref.shape[4]
    scale = HEAD_DIM ** -0.5

    @pl.when(pl.program_id(1) == 0)
    def _():
        fill_band(band, vec_ref[0])
        fold[...] = jnp.zeros_like(fold)

    keys_t = k_ref[0, 0]
    keys = keys_t.T
    values = v_ref[0, 0].T
    for start in range(0, seq, CHUNK):
        block, inner = start // own, start % own
        queries = q_ref[0, 0, :, start : start + CHUNK] * jnp.bfloat16(scale)
        grads = g_ref[block, 0, :, inner : inner + CHUNK]
        mixed = o_ref[block, 0, :, inner : inner + CHUNK]
        delta = jnp.sum(grads.astype(jnp.float32) * mixed.astype(jnp.float32), axis=0, keepdims=True)
        logs = log_ref[0, 0, :, start : start + CHUNK]
        raw = dot_nn(keys, queries)
        grad_weights = dot_nn(values, grads)
        low_weights, low_scores = [], []
        for low in range(0, seq, BAND):
            at = start - low + seq - BAND
            weights = jnp.exp(raw[low : low + BAND] + band[:, at : at + CHUNK] - logs)
            scores = weights * (grad_weights[low : low + BAND] - delta)
            fold[:, at : at + CHUNK] += scores
            low_weights.append(weights.astype(jnp.bfloat16))
            low_scores.append(scores.astype(jnp.bfloat16))
        weights = jnp.concatenate(low_weights, axis=0)
        scores = jnp.concatenate(low_scores, axis=0)
        grad_q = dot_nn(keys_t, scores) * scale
        out_ref[block, 0, 0, :, inner : inner + CHUNK] = grad_q.astype(jnp.bfloat16)
        if start == 0:
            dk[...] = dot_nt(queries, scores)
            dv[...] = dot_nt(grads, weights)
        else:
            dk[...] += dot_nt(queries, scores)
            dv[...] += dot_nt(grads, weights)
    for block in range(seq // own):
        out_ref[block, 1, 0] = dk[:, block * own : (block + 1) * own].astype(jnp.bfloat16)
        out_ref[block, 2, 0] = dv[:, block * own : (block + 1) * own].astype(jnp.bfloat16)

    @pl.when(pl.program_id(1) == pl.num_programs(1) - 1)
    def _():
        diag_ref[0] = fold_band(fold)


def attend_back(projected, vectors, mixed, grads, logs):
    heads, seq = vectors.shape[0], vectors.shape[2] // 2
    seqs = projected.shape[1] // seq
    own = mixed.shape[3]
    blocks = seq // own
    part = lambda p: pl.BlockSpec((1, 1, HEAD_DIM, seq), lambda h, s, p=p: (p, h, 0, s))
    side = pl.BlockSpec((blocks, 1, HEAD_DIM, own), lambda h, s: (s, h, 0, 0))
    vec = pl.BlockSpec((1, 1, 2 * seq), lambda h, s: (h, 0, 0))
    proj = projected.reshape(3, heads, HEAD_DIM, seqs * seq)
    return pl.pallas_call(
        attend_back_kernel,
        grid=(heads, seqs),
        in_specs=[part(0), part(1), part(2), side, side,
                  pl.BlockSpec((1, 1, 1, seq), lambda h, s: (h, s, 0, 0)), vec],
        out_specs=[
            pl.BlockSpec((blocks, 3, 1, HEAD_DIM, own), lambda h, s: (s, 0, h, 0, 0)),
            vec,
        ],
        out_shape=[
            jax.ShapeDtypeStruct((seqs * blocks, 3, heads, HEAD_DIM, own), jnp.bfloat16),
            jax.ShapeDtypeStruct((heads, 1, 2 * seq), jnp.float32),
        ],
        scratch_shapes=[
            pltpu.VMEM((BAND, 2 * seq), jnp.float32),
            pltpu.VMEM((BAND, 2 * seq), jnp.float32),
            pltpu.VMEM((HEAD_DIM, seq), jnp.float32),
            pltpu.VMEM((HEAD_DIM, seq), jnp.float32),
        ],
        compiler_params=pltpu.CompilerParams(vmem_limit_bytes=48 * 2**20),
        cost_estimate=cost(32 * heads * seqs * seq * seq * HEAD_DIM),
    )(proj, proj, proj, mixed, grads, logs, vectors)


def place_kernel(capacity, flat_ref, rows_ref, place_ref, *piece_refs):
    flat = flat_ref[...]
    for k, ref in enumerate(piece_refs):
        index = lax.broadcasted_iota(jnp.int32, (capacity, flat.shape[1]), 0) + k * capacity
        hot = (index == flat).astype(jnp.bfloat16)
        place_ref[k * capacity : (k + 1) * capacity, :] = hot
        ref[...] = dot_nn(hot, rows_ref[...]).astype(jnp.bfloat16)


def place_rows(flat, rows, pieces, capacity):
    count, width = rows.shape
    outs = pl.pallas_call(
        functools.partial(place_kernel, capacity),
        out_shape=[jax.ShapeDtypeStruct((pieces * capacity, count), jnp.bfloat16)]
        + [jax.ShapeDtypeStruct((capacity, width), jnp.bfloat16)] * pieces,
        compiler_params=pltpu.CompilerParams(vmem_limit_bytes=48 * 2**20),
        cost_estimate=cost(2 * pieces * capacity * count * width),
    )(flat[None, :], rows)
    return outs[0], list(outs[1:])


def project_kernel(x_ref, gain_ref, weight_ref, out_ref, normed_ref):
    rows = x_ref[...]
    scale = lax.rsqrt(jnp.mean(rows * rows, axis=-1, keepdims=True) + EPSILON)
    normed = (rows * scale * gain_ref[...]).astype(jnp.bfloat16)
    normed_ref[...] = normed
    out_ref[...] = dot_nt(weight_ref[...], normed).astype(jnp.bfloat16)


def project(rows, gain, weights, tile):
    count, width = rows.shape
    columns = weights.shape[0]
    return pl.pallas_call(
        project_kernel,
        grid=(count // tile,),
        in_specs=[
            pl.BlockSpec((tile, width), lambda i: (i, 0)),
            pl.BlockSpec((1, width), lambda i: (0, 0)),
            pl.BlockSpec((columns, width), lambda i: (0, 0)),
        ],
        out_specs=[
            pl.BlockSpec((columns, tile), lambda i: (0, i)),
            pl.BlockSpec((tile, width), lambda i: (i, 0)),
        ],
        out_shape=[
            jax.ShapeDtypeStruct((columns, count), jnp.bfloat16),
            jax.ShapeDtypeStruct((count, width), jnp.bfloat16),
        ],
        compiler_params=pltpu.CompilerParams(vmem_limit_bytes=48 * 2**20),
        cost_estimate=cost(4 * count * width * columns),
    )(rows, gain, weights)


def gelu_parts(values):
    root = 0.7978845608028654
    square = values * values
    bend = jnp.tanh(root * values * (1.0 + 0.044715 * square))
    half = 0.5 + 0.5 * bend
    slope = half + half * (1.0 - bend) * values * (root + (3.0 * 0.044715 * root) * square)
    return values * half, slope


def expert_kernel(places, arrays, pieces, *refs):
    row_refs, grad_refs, refs = refs[:pieces], refs[pieces : 2 * pieces], refs[2 * pieces :]
    first_refs, second_refs, refs = refs[:arrays], refs[arrays : 2 * arrays], refs[2 * arrays :]
    parts = len(places)
    act_ref, pre_ref, xt_ref, lt_ref = refs[:4]
    res_refs, back_refs = refs[4 : 4 + pieces], refs[4 + pieces : 4 + 2 * pieces]
    rows, low, res_sum, back_sum, firsts, seconds, sems = refs[4 + 2 * pieces :]
    step = pl.program_id(0)
    capacity = grad_refs[0].shape[0]
    width = grad_refs[0].shape[1]
    count = pieces * capacity
    tile = min(count, 256)

    def fetch(j):
        (one, at), (two, there) = places[j]
        return (
            pltpu.make_async_copy(first_refs[one].at[at], firsts.at[j % 2], sems.at[0, j % 2]),
            pltpu.make_async_copy(second_refs[two].at[there], seconds.at[j % 2], sems.at[1, j % 2]),
        )

    @pl.when(step == 0)
    def _():
        for copy in fetch(0):
            copy.start()
        for e in range(pieces):
            span = pl.ds(e * capacity, capacity)
            rows[span, :] = row_refs[e][:capacity, :]
            gates = row_refs[e][capacity : capacity + 8, :capacity].astype(jnp.float32).T[:, 0:1]
            low[span, :] = (gates * grad_refs[e][...].astype(jnp.float32)).astype(jnp.bfloat16)
        res_sum[...] = jnp.zeros_like(res_sum)
        back_sum[...] = jnp.zeros_like(back_sum)

    for j in range(parts):

        @pl.when(step == j)
        def _(j=j):
            if j + 1 < parts:
                for copy in fetch(j + 1):
                    copy.start()
            for copy in fetch(j):
                copy.wait()

    @pl.when(step == 0)
    def _():
        xt_ref[...] = rows[...].T
        lt_ref[...] = low[...].T

    first = firsts[step % 2]
    second = seconds[step % 2]
    for start in range(0, count, tile):
        span = pl.ds(start, tile)
        active, slope = gelu_parts(dot_nn(rows[span, :], first))
        active = active.astype(jnp.bfloat16)
        act_ref[0, span, :] = active
        res_sum[span, :] += dot_nn(active, second)
        pre = (dot_nt(low[span, :], second) * slope).astype(jnp.bfloat16)
        pre_ref[0, span, :] = pre
        back_sum[span, :] += dot_nt(pre, first)

    @pl.when(step == parts - 1)
    def _():
        for e in range(pieces):
            span = pl.ds(e * capacity, capacity)
            res_refs[e][...] = res_sum[span, :].astype(jnp.bfloat16)
            back_refs[e][:capacity, :] = back_sum[span, :].astype(jnp.bfloat16)
            sums = jnp.sum(
                res_sum[span, :] * grad_refs[e][...].astype(jnp.float32), axis=1, keepdims=True
            )
            sums = jnp.broadcast_to(sums, (capacity, 128)).T[0:8, :]
            high = sums.astype(jnp.bfloat16).astype(jnp.float32)
            index = lax.broadcasted_iota(jnp.int32, sums.shape, 0)
            pair = jnp.where(index == 0, high, jnp.where(index == 1, sums - high, 0.0))
            back_refs[e][capacity : capacity + 8, :] = jnp.zeros((8, width), jnp.bfloat16)
            back_refs[e][capacity : capacity + 8, :capacity] = pair.astype(jnp.bfloat16)


PLACES = (
    ((0, 0), (0, 0)),
    ((1, 0), (1, 0)),
    ((2, 0), (4, 0)),
    ((3, 0), (5, 0)),
    ((4, 0), (2, 0)),
    ((4, 1), (4, 1)),
    ((5, 0), (3, 0)),
    ((5, 1), (5, 1)),
)
MINE = ((0, 4, 2, 5), (0, 2, 4, 5))
OTHER = ((1, 6, 3, 7), (1, 3, 6, 7))


def expert_apply(arrived, grads, firsts, seconds):
    pieces = len(grads)
    capacity, width = grads[0].shape
    count = pieces * capacity
    hidden = firsts[0].shape[2]
    parts, arrays = len(PLACES), len(firsts)
    sent = pl.BlockSpec(arrived[0].shape, lambda i: (0, 0))
    whole = pl.BlockSpec((capacity, width), lambda i: (0, 0))
    kept = pl.BlockSpec((1, count, hidden), lambda i: (i, 0, 0))
    turned = pl.BlockSpec((width, count), lambda i: (0, 0))
    outs = pl.pallas_call(
        functools.partial(expert_kernel, PLACES, arrays, pieces),
        grid=(parts,),
        in_specs=[sent] * pieces + [whole] * pieces + [pl.BlockSpec(memory_space=pl.ANY)] * (2 * arrays),
        out_specs=[kept, kept, turned, turned] + [whole] * pieces + [sent] * pieces,
        out_shape=[
            jax.ShapeDtypeStruct((parts, count, hidden), jnp.bfloat16),
            jax.ShapeDtypeStruct((parts, count, hidden), jnp.bfloat16),
            jax.ShapeDtypeStruct((width, count), jnp.bfloat16),
            jax.ShapeDtypeStruct((width, count), jnp.bfloat16),
        ]
        + [jax.ShapeDtypeStruct((capacity, width), jnp.bfloat16)] * pieces
        + [jax.ShapeDtypeStruct(arrived[0].shape, jnp.bfloat16)] * pieces,
        scratch_shapes=[
            pltpu.VMEM((count, width), jnp.bfloat16),
            pltpu.VMEM((count, width), jnp.bfloat16),
            pltpu.VMEM((count, width), jnp.float32),
            pltpu.VMEM((count, width), jnp.float32),
            pltpu.VMEM((2, width, hidden), jnp.bfloat16),
            pltpu.VMEM((2, hidden, width), jnp.bfloat16),
            pltpu.SemaphoreType.DMA((2, 2)),
        ],
        compiler_params=pltpu.CompilerParams(vmem_limit_bytes=52 * 2**20),
        cost_estimate=cost(12 * count * width * hidden * parts),
    )(*arrived, *grads, *firsts, *seconds)
    return list(outs[:4]), list(outs[4 : 4 + pieces]), list(outs[4 + pieces :])


def weight_kernel(groups, added, *refs):
    for out, (left, right) in enumerate(((2, 1), (3, 0))):
        total = 0.0
        for g in range(groups):
            total = total + dot_nn(refs[4 * g + left][...], refs[4 * g + right][0])
        if added:
            total = total + refs[4 * groups + out][0].astype(jnp.float32)
        refs[4 * groups + 2 * added + out][0] = total.astype(jnp.bfloat16)


def expert_weights(groups, chosen, added=()):
    steps, hidden = len(chosen[0]), groups[0][0].shape[2]
    width = groups[0][2].shape[0]
    count = sum(group[2].shape[1] for group in groups)
    specs, arrays = [], []

    def pick(i, which):
        return sum(jnp.where(i == j, at, 0) for j, at in enumerate(chosen[which]))

    for act, pre, xt, lt in groups:
        block = (1,) + act.shape[1:]
        whole = pl.BlockSpec(xt.shape, lambda i: (0, 0))
        specs += [
            pl.BlockSpec(block, lambda i: (pick(i, 1), 0, 0)),
            pl.BlockSpec(block, lambda i: (pick(i, 0), 0, 0)),
            whole,
            whole,
        ]
        arrays += [act, pre, xt, lt]
    part = pl.BlockSpec((1, width, hidden), lambda i: (i, 0, 0))
    return pl.pallas_call(
        functools.partial(weight_kernel, len(groups), len(added) // 2),
        grid=(steps,),
        in_specs=specs + [part] * len(added),
        out_specs=[part, part],
        out_shape=[jax.ShapeDtypeStruct((steps, width, hidden), jnp.bfloat16)] * 2,
        compiler_params=pltpu.CompilerParams(vmem_limit_bytes=50 * 2**20),
        cost_estimate=cost(6 * count * width * hidden * steps),
    )(*arrays, *added)


def inverse_rms(rows):
    return lax.rsqrt(jnp.mean(rows * rows, axis=-1, keepdims=True) + EPSILON)


def norm_backward(grad_normed, gain, normed_hat, inv_scale):
    scaled = grad_normed * gain
    return inv_scale * (scaled - normed_hat * jnp.mean(scaled * normed_hat, axis=-1, keepdims=True))


def swap(array, axis, offset):
    count = lax.axis_size(axis)
    return lax.ppermute(array, axis, [(i, i ^ offset) for i in range(count)])


def trade(array, axis):
    return lax.all_to_all(array, axis, 0, 0, tiled=True)


def spread(array, axis):
    return trade(jnp.broadcast_to(array[None], (lax.axis_size(axis),) + array.shape), axis)


def sum_copies(partial):
    experts = lax.axis_size("expert")
    rank = lax.axis_index("dp")
    kept = partial.shape[0]
    partial = jnp.pad(partial, ((0, -kept % (2 * experts)), (0, 0)))
    rows, columns = partial.shape
    half = rows // 2
    mine = lax.dynamic_slice_in_dim(partial, rank * half, half, 0)
    other = lax.dynamic_slice_in_dim(partial, (1 - rank) * half, half, 0).astype(jnp.bfloat16)
    mine = (mine + swap(other, "dp", 1).astype(jnp.float32)).astype(jnp.bfloat16)
    shares = trade(mine.reshape(experts, half // experts, columns), "expert")
    share = jnp.sum(shares.astype(jnp.float32), axis=0).astype(jnp.bfloat16)
    mine = spread(share, "expert").reshape(half, columns)
    other = swap(mine, "dp", 1)
    first = rank == 0
    return jnp.concatenate(
        [jnp.where(first, mine, other), jnp.where(first, other, mine)], axis=0
    )[:kept].astype(jnp.float32)


def on_device(
    layer_input,
    cotangent,
    norm1_gain,
    w_query,
    w_key,
    w_value,
    w_output,
    bias_table,
    bucket,
    norm2_gain,
    router,
    expert_index,
    w_in,
    w_out,
):
    group_rows, width = layer_input.shape
    tensor_count = lax.axis_size("tensor")
    tensor_rank = lax.axis_index("tensor")
    dp_rank = lax.axis_index("dp")
    own_rows = group_rows // tensor_count
    own_start = tensor_rank * own_rows
    local_heads = bias_table.shape[1]
    inner = local_heads * HEAD_DIM
    experts = router.shape[1]
    capacity = 2 * own_rows // experts
    slots = experts * capacity

    half = w_in.shape[2] // 2
    first_mine = lax.dynamic_slice_in_dim(w_in[0], dp_rank * half, half, 1)
    first_other = lax.dynamic_slice_in_dim(w_in[0], (1 - dp_rank) * half, half, 1)
    second_mine = lax.dynamic_slice_in_dim(w_out[0], dp_rank * half, half, 0)
    second_other = lax.dynamic_slice_in_dim(w_out[0], (1 - dp_rank) * half, half, 0)
    w_joined = jnp.concatenate([w_query.T, w_key.T, w_value.T], axis=0)
    output_full = spread(w_output, "tensor")

    routes = lax.dynamic_slice_in_dim(expert_index[:, 0], own_start, own_rows, 0)
    own_hot = routes[:, None] == jnp.arange(experts, dtype=jnp.int32)[None, :]
    row_ids = jnp.arange(own_rows, dtype=jnp.int32)
    earlier = (row_ids[None, :] < row_ids[:, None]).astype(jnp.bfloat16)
    before = jnp.dot(earlier, own_hot.astype(jnp.bfloat16), preferred_element_type=jnp.float32)
    own_hot = own_hot.astype(jnp.float32)
    slot = jnp.sum(before * own_hot, axis=-1).astype(jnp.int32)
    flat = (routes ^ lax.axis_index("expert")) * capacity + slot
    cot_low = lax.dynamic_slice_in_dim(cotangent, own_start, own_rows, 0)
    cot_own = cot_low.astype(jnp.float32)
    place_hot, grad_in = place_rows(flat, cot_low, experts, capacity)
    near = experts // 2
    far = near + experts // 4
    grad_in = [grad_in[0]] + [swap(grad_in[k], "expert", k) for k in range(1, far)] + grad_in[far:]

    gain_one = norm1_gain.astype(jnp.float32)
    projected, normed_one = project(layer_input, gain_one[None, :], w_joined, own_rows)
    high_bit = tensor_count // 2
    first_near = swap(first_mine, "tensor", 1)
    second_near = swap(second_mine, "tensor", high_bit)
    turned = jnp.concatenate([bucket[::-1], jnp.full((1,), -1, jnp.int32)])
    bucket_hot = jnp.arange(NUM_BUCKETS, dtype=jnp.int32)[:, None] == turned[None, :]
    vectors = dot_tn(bias_table, bucket_hot.astype(jnp.bfloat16))[:, None, :]
    mixed, logs = attend(projected, vectors, own_rows)
    mixed, output_full, first_near, second_near, grad_in[1:far] = lax.optimization_barrier(
        (mixed, output_full, first_near, second_near, grad_in[1:far])
    )
    output_full = output_full.reshape(tensor_count * inner, width)
    first_far = swap(jnp.stack([first_mine, first_near]), "tensor", high_bit)
    second_far = swap(jnp.stack([second_mine, second_near]), "tensor", 1)
    grad_in[far:] = [swap(grad_in[k], "expert", k) for k in range(far, experts)]
    mixed_own = trade(mixed.reshape(tensor_count, inner, own_rows), "tensor").reshape(
        tensor_count * inner, own_rows
    )

    input_own = lax.dynamic_slice_in_dim(layer_input, own_start, own_rows, 0)
    residual = input_own + dot_tn(mixed_own, output_full)
    gain_two = norm2_gain.astype(jnp.float32)
    inv_two = inverse_rms(residual)
    hat_two = residual * inv_two
    normed_two = hat_two * gain_two
    router_wide = router.astype(jnp.float32)
    router_probs = jax.nn.softmax(jnp.dot(normed_two, router_wide, precision=HIGHEST), axis=-1)
    gate_full = jnp.sum(router_probs * own_hot, axis=-1)
    gate_low = gate_full.astype(jnp.bfloat16)
    send_rows = dot_nn(place_hot, normed_two.astype(jnp.bfloat16)).astype(jnp.bfloat16)
    send_gates = dot_nn(place_hot, gate_low[:, None]).astype(jnp.bfloat16)
    gate_rows = jnp.pad(send_gates.reshape(experts, 1, capacity), ((0, 0), (0, 7), (0, width - capacity)))
    sent = jnp.concatenate([send_rows.reshape(experts, capacity, width), gate_rows], axis=1)
    sent, grad_in[far:] = lax.optimization_barrier((sent, grad_in[far:]))
    arrived = [sent[0]] + [swap(sent[k], "expert", k) for k in range(1, experts)]

    arrived[1:near], first_far, second_far = lax.optimization_barrier(
        (arrived[1:near], first_far, second_far)
    )
    first_parts = [first_mine[None], first_other[None]]
    second_parts = [second_mine[None], second_other[None]]
    for first, second in ((first_near[None], second_near[None]), (first_far, second_far)):
        first_parts += [first, swap(first, "dp", 1)]
        second_parts += [second, swap(second, "dp", 1)]
    arrived[:near], first_parts, second_parts, joined = lax.optimization_barrier(
        (arrived[:near], first_parts, second_parts, w_joined)
    )
    joined_parts = [w_joined] + [swap(joined, "tensor", k) for k in range(1, tensor_count - 1)]
    groups, results, back_got = [], [], []
    for low, high in ((0, near), (near, far), (far, experts)):
        pieces = arrived[low:high]
        if low == near:
            results, pieces, joined, joined_parts = lax.optimization_barrier(
                (results, pieces, joined, joined_parts)
            )
            joined_parts.append(swap(joined, "tensor", tensor_count - 1))
        if low == far:
            results, pieces, joined_parts = lax.optimization_barrier((results, pieces, joined_parts))
        kept, res, back = expert_apply(pieces, grad_in[low:high], first_parts, second_parts)
        groups.append(kept)
        results += res
        back_got += [
            back[k - low] if k == 0 else swap(back[k - low], "expert", k) for k in range(low, high)
        ]
    others = expert_weights(groups, OTHER)
    first_sum, second_sum = expert_weights(groups, MINE, [swap(part, "dp", 1) for part in others])
    first_sum, second_sum, back_got = lax.optimization_barrier((first_sum, second_sum, back_got))
    first_got = swap(first_sum[2:], "tensor", 1)
    second_got = swap(second_sum[2:], "tensor", high_bit)

    grad_normed_two = dot_tn(place_hot, jnp.concatenate([back[:capacity] for back in back_got]))
    pair_got = jnp.concatenate([back[capacity : capacity + 2, :capacity].T for back in back_got])
    grad_gate = jnp.sum(dot_tn(place_hot, pair_got), axis=-1)
    grad_logits = router_probs * (own_hot - gate_full[:, None]) * grad_gate[:, None]
    grad_router = jnp.einsum("td,te->ed", normed_two, grad_logits, precision=HIGHEST)
    grad_normed_two = grad_normed_two + jnp.einsum(
        "te,de->td", grad_logits, router_wide, precision=HIGHEST
    )
    grad_norm_two = jnp.sum(grad_normed_two * hat_two, axis=0)
    grad_residual = cot_own + norm_backward(grad_normed_two, gain_two, hat_two, inv_two)
    grad_low = grad_residual.astype(jnp.bfloat16)
    grad_heads = dot_nt(output_full, grad_low).astype(jnp.bfloat16)
    heads_got = trade(grad_heads.reshape(tensor_count, inner, own_rows), "tensor")
    grad_wo = dot_nn(mixed_own, grad_low).astype(jnp.bfloat16).reshape(tensor_count, inner, width)
    shared = jnp.concatenate([grad_router, grad_norm_two[None]], axis=0).astype(jnp.bfloat16)
    shared = jnp.pad(shared, ((0, -shared.shape[0] % 8), (0, 0)))
    shared = jnp.broadcast_to(shared[None], (tensor_count,) + shared.shape)
    grad_wo = trade(jnp.concatenate([grad_wo, shared], axis=1), "tensor")
    _, *results = lax.optimization_barrier((grad_low, *results))
    returned = [results[0]] + [swap(results[k], "expert", k) for k in range(1, experts)]

    heads_got, first_got, second_got = lax.optimization_barrier((heads_got, first_got, second_got))
    first_pair = (first_sum[:2].astype(jnp.float32) + first_got.astype(jnp.float32)).astype(jnp.bfloat16)
    second_pair = (second_sum[:2].astype(jnp.float32) + second_got.astype(jnp.float32)).astype(
        jnp.bfloat16
    )
    first_got = swap(first_pair[1], "tensor", high_bit)
    second_got = swap(second_pair[1], "tensor", 1)

    head_shape = (tensor_count, local_heads, HEAD_DIM, own_rows)
    grad_projected, diagonals = attend_back(
        projected, vectors, mixed, heads_got.reshape(head_shape), logs
    )
    grad_projected = grad_projected.reshape(tensor_count, 3 * inner, own_rows)
    grad_projected, first_got, second_got, returned, grad_wo = lax.optimization_barrier(
        (grad_projected, first_got, second_got, returned, grad_wo)
    )

    pairs = ((first_pair, first_got), (second_pair, second_got))
    total = jnp.stack([pair[0].astype(jnp.float32) + got.astype(jnp.float32) for pair, got in pairs])
    total = total.astype(jnp.bfloat16)
    rest = swap(total, "dp", 1)
    first = dp_rank == 0
    both = jnp.concatenate(
        [jnp.where(first, total, rest), jnp.where(first, rest, total)], axis=2
    ).astype(jnp.float32)
    output = residual + gate_low.astype(jnp.float32)[:, None] * dot_tn(
        place_hot, jnp.concatenate(returned)
    )

    grad_normed_one = dot_tn(
        lax.dynamic_index_in_dim(grad_projected, tensor_rank, 0, keepdims=False), w_joined
    )
    for k in range(1, tensor_count):
        sent = lax.dynamic_index_in_dim(grad_projected, tensor_rank ^ k, 0, keepdims=False)
        grad_normed_one = grad_normed_one + dot_tn(swap(sent, "tensor", k), joined_parts[k])
    inv_own = inverse_rms(input_own)
    input_grad = grad_residual + norm_backward(grad_normed_one, gain_one, input_own * inv_own, inv_own)

    grad_joined = jnp.einsum(
        "bcn,bnd->cd",
        grad_projected,
        normed_one.reshape(tensor_count, own_rows, width),
        preferred_element_type=jnp.float32,
    )
    norm_one = jnp.sum(grad_joined * w_joined.astype(jnp.float32), axis=0) / gain_one
    grad_table = jnp.einsum(
        "br,hr->hb", bucket_hot.astype(jnp.float32), diagonals[:, 0], precision=HIGHEST
    ).reshape(-1)
    table_size = grad_table.shape[0]
    used = 3 * inner
    joined = sum_copies(
        jnp.concatenate(
            [
                grad_joined,
                jnp.sum(grad_wo.astype(jnp.float32), axis=0),
                norm_one[None],
                jnp.pad(grad_table, (0, width - table_size))[None],
            ],
            axis=0,
        )
    )
    shared = joined[used + inner :]
    norm_one = shared[-2]
    norm_one = norm_one + sum(swap(norm_one, "tensor", k) for k in range(1, tensor_count))
    return (
        output,
        input_grad,
        joined[:inner].T,
        joined[inner : 2 * inner].T,
        joined[2 * inner : used].T,
        joined[used : used + inner],
        shared[-1, :table_size].reshape(local_heads, NUM_BUCKETS).T,
        norm_one,
        shared[experts],
        shared[:experts].T,
        both[0][None],
        both[1].T[None],
    )


def solution(mesh):
    return jax.shard_map(
        on_device,
        mesh=mesh,
        in_specs=(
            P(("dp", "expert"), None),
            P(("dp", "expert"), None),
            P(),
            P(None, "tensor"),
            P(None, "tensor"),
            P(None, "tensor"),
            P("tensor", None),
            P(None, "tensor"),
            P(),
            P(),
            P(),
            P(("dp", "expert"), None),
            P("expert", None, "tensor"),
            P("expert", "tensor", None),
        ),
        out_specs=(
            P(("dp", "expert", "tensor"), None),
            P(("dp", "expert", "tensor"), None),
            P(None, "tensor"),
            P(None, "tensor"),
            P(None, "tensor"),
            P("tensor", None),
            P(None, "tensor"),
            P(),
            P(),
            P(),
            P("expert", None, "tensor"),
            P("expert", "tensor", None),
        ),
        check_vma=False,
    )
```

```python
import functools
import jax
import jax.numpy as jnp
from jax import lax
from jax.sharding import PartitionSpec as P
from jax.experimental import pallas as pl
from jax.experimental.pallas import tpu as pltpu

HEAD_DIM = 64
NUM_BUCKETS = 32
EPSILON = 1e-06
HIGHEST = lax.Precision.HIGHEST
CHUNK = 512


def cost(work):
    return pl.CostEstimate(flops=work, bytes_accessed=work // 1024, transcendentals=0)

BAND = 128


def dot_nt(a, b):
    return lax.dot_general(a, b, (((1,), (1,)), ((), ())), preferred_element_type=jnp.float32)


def dot_nn(a, b):
    return lax.dot_general(a, b, (((1,), (0,)), ((), ())), preferred_element_type=jnp.float32)


def dot_tn(a, b):
    return lax.dot_general(a, b, (((0,), (0,)), ((), ())), preferred_element_type=jnp.float32)


def fill_band(band, vector):
    span = vector.shape[1]
    rows = jnp.broadcast_to(vector, (8, span))
    rows = pltpu.roll(rows, span - (BAND - 1), 1)
    index = lax.broadcasted_iota(jnp.int32, (8, span), 0)
    for step in (1, 2, 4):
        rows = jnp.where((index & step) != 0, pltpu.roll(rows, step, 1), rows)
    band[0:8, :] = rows
    step = 8
    while step < BAND:
        band[step : 2 * step, :] = pltpu.roll(band[0:step, :], step, 1)
        step *= 2


def fold_band(band):
    span = band.shape[1]
    step = BAND // 2
    while step >= 8:
        band[0:step, :] += pltpu.roll(band[step : 2 * step, :], span - step, 1)
        step //= 2
    rows = band[0:8, :]
    index = lax.broadcasted_iota(jnp.int32, (8, span), 0)
    for step in (1, 2, 4):
        rows = jnp.where((index & step) != 0, pltpu.roll(rows, span - step, 1), rows)
    total = jnp.sum(rows, axis=0, keepdims=True)
    return pltpu.roll(total, BAND - 1, 1)


def attend_kernel(q_ref, k_ref, v_ref, vec_ref, out_ref, log_ref, band):
    seq = k_ref.shape[3]
    own = out_ref.shape[3]

    @pl.when(pl.program_id(1) == 0)
    def _():
        fill_band(band, vec_ref[0])

    keys = k_ref[0, 0].T
    values = v_ref[0, 0]
    for start in range(0, seq, CHUNK):
        queries = q_ref[0, 0, :, start : start + CHUNK] * jnp.bfloat16(HEAD_DIM ** -0.5)
        raw = dot_nn(keys, queries)
        parts = []
        for low in range(0, seq, BAND):
            at = start - low + seq - BAND
            parts.append(raw[low : low + BAND] + band[:, at : at + CHUNK])
        peak = functools.reduce(jnp.maximum, parts)
        peak = jnp.max(peak, axis=0, keepdims=True)
        parts = [jnp.exp(part - peak) for part in parts]
        total = jnp.sum(functools.reduce(jnp.add, parts), axis=0, keepdims=True)
        weights = jnp.concatenate([part.astype(jnp.bfloat16) for part in parts], axis=0)
        mixed = dot_nn(values, weights) / total
        out_ref[start // own, 0, :, start % own : start % own + CHUNK] = mixed.astype(jnp.bfloat16)
        log_ref[0, 0, :, start : start + CHUNK] = peak + jnp.log(total)


def attend(projected, vectors, own):
    heads, seq = vectors.shape[0], vectors.shape[2] // 2
    seqs = projected.shape[1] // seq
    blocks = seq // own
    part = lambda p: pl.BlockSpec((1, 1, HEAD_DIM, seq), lambda h, s, p=p: (p, h, 0, s))
    proj = projected.reshape(3, heads, HEAD_DIM, seqs * seq)
    return pl.pallas_call(
        attend_kernel,
        grid=(heads, seqs),
        in_specs=[part(0), part(1), part(2), pl.BlockSpec((1, 1, 2 * seq), lambda h, s: (h, 0, 0))],
        out_specs=[
            pl.BlockSpec((blocks, 1, HEAD_DIM, own), lambda h, s: (s, h, 0, 0)),
            pl.BlockSpec((1, 1, 1, seq), lambda h, s: (h, s, 0, 0)),
        ],
        out_shape=[
            jax.ShapeDtypeStruct((seqs * blocks, heads, HEAD_DIM, own), jnp.bfloat16),
            jax.ShapeDtypeStruct((heads, seqs, 1, seq), jnp.float32),
        ],
        scratch_shapes=[pltpu.VMEM((BAND, 2 * seq), jnp.float32)],
        compiler_params=pltpu.CompilerParams(vmem_limit_bytes=48 * 2**20),
        cost_estimate=cost(16 * heads * seqs * seq * seq * HEAD_DIM),
    )(proj, proj, proj, vectors)


def attend_back_kernel(q_ref, k_ref, v_ref, o_ref, g_ref, log_ref, vec_ref, out_ref, diag_ref, band, fold, dk, dv):
    seq = k_ref.shape[3]
    own = out_ref.shape[4]
    scale = HEAD_DIM ** -0.5

    @pl.when(pl.program_id(1) == 0)
    def _():
        fill_band(band, vec_ref[0])
        fold[...] = jnp.zeros_like(fold)

    keys_t = k_ref[0, 0]
    keys = keys_t.T
    values = v_ref[0, 0].T
    for start in range(0, seq, CHUNK):
        block, inner = start // own, start % own
        queries = q_ref[0, 0, :, start : start + CHUNK] * jnp.bfloat16(scale)
        grads = g_ref[block, 0, :, inner : inner + CHUNK]
        mixed = o_ref[block, 0, :, inner : inner + CHUNK]
        delta = jnp.sum(grads.astype(jnp.float32) * mixed.astype(jnp.float32), axis=0, keepdims=True)
        logs = log_ref[0, 0, :, start : start + CHUNK]
        raw = dot_nn(keys, queries)
        grad_weights = dot_nn(values, grads)
        low_weights, low_scores = [], []
        for low in range(0, seq, BAND):
            at = start - low + seq - BAND
            weights = jnp.exp(raw[low : low + BAND] + band[:, at : at + CHUNK] - logs)
            scores = weights * (grad_weights[low : low + BAND] - delta)
            fold[:, at : at + CHUNK] += scores
            low_weights.append(weights.astype(jnp.bfloat16))
            low_scores.append(scores.astype(jnp.bfloat16))
        weights = jnp.concatenate(low_weights, axis=0)
        scores = jnp.concatenate(low_scores, axis=0)
        grad_q = dot_nn(keys_t, scores) * scale
        out_ref[block, 0, 0, :, inner : inner + CHUNK] = grad_q.astype(jnp.bfloat16)
        if start == 0:
            dk[...] = dot_nt(queries, scores)
            dv[...] = dot_nt(grads, weights)
        else:
            dk[...] += dot_nt(queries, scores)
            dv[...] += dot_nt(grads, weights)
    for block in range(seq // own):
        out_ref[block, 1, 0] = dk[:, block * own : (block + 1) * own].astype(jnp.bfloat16)
        out_ref[block, 2, 0] = dv[:, block * own : (block + 1) * own].astype(jnp.bfloat16)

    @pl.when(pl.program_id(1) == pl.num_programs(1) - 1)
    def _():
        diag_ref[0] = fold_band(fold)


def attend_back(projected, vectors, mixed, grads, logs):
    heads, seq = vectors.shape[0], vectors.shape[2] // 2
    seqs = projected.shape[1] // seq
    own = mixed.shape[3]
    blocks = seq // own
    part = lambda p: pl.BlockSpec((1, 1, HEAD_DIM, seq), lambda h, s, p=p: (p, h, 0, s))
    side = pl.BlockSpec((blocks, 1, HEAD_DIM, own), lambda h, s: (s, h, 0, 0))
    vec = pl.BlockSpec((1, 1, 2 * seq), lambda h, s: (h, 0, 0))
    proj = projected.reshape(3, heads, HEAD_DIM, seqs * seq)
    return pl.pallas_call(
        attend_back_kernel,
        grid=(heads, seqs),
        in_specs=[part(0), part(1), part(2), side, side,
                  pl.BlockSpec((1, 1, 1, seq), lambda h, s: (h, s, 0, 0)), vec],
        out_specs=[
            pl.BlockSpec((blocks, 3, 1, HEAD_DIM, own), lambda h, s: (s, 0, h, 0, 0)),
            vec,
        ],
        out_shape=[
            jax.ShapeDtypeStruct((seqs * blocks, 3, heads, HEAD_DIM, own), jnp.bfloat16),
            jax.ShapeDtypeStruct((heads, 1, 2 * seq), jnp.float32),
        ],
        scratch_shapes=[
            pltpu.VMEM((BAND, 2 * seq), jnp.float32),
            pltpu.VMEM((BAND, 2 * seq), jnp.float32),
            pltpu.VMEM((HEAD_DIM, seq), jnp.float32),
            pltpu.VMEM((HEAD_DIM, seq), jnp.float32),
        ],
        compiler_params=pltpu.CompilerParams(vmem_limit_bytes=48 * 2**20),
        cost_estimate=cost(32 * heads * seqs * seq * seq * HEAD_DIM),
    )(proj, proj, proj, mixed, grads, logs, vectors)


def dot_exact(a, b, axes):
    return lax.dot_general(
        a, b, ((axes[:1], axes[1:]), ((), ())), precision=HIGHEST, preferred_element_type=jnp.float32
    )


def place_kernel(capacity, row_ref, column_ref, rows_ref, place_ref, turned_ref, *piece_refs):
    flat = row_ref[...]
    column = column_ref[...]
    for k, ref in enumerate(piece_refs):
        span = slice(k * capacity, (k + 1) * capacity)
        index = lax.broadcasted_iota(jnp.int32, (capacity, flat.shape[1]), 0) + k * capacity
        hot = (index == flat).astype(jnp.bfloat16)
        place_ref[span, :] = hot
        ref[...] = dot_nn(hot, rows_ref[...]).astype(jnp.bfloat16)
    index = lax.broadcasted_iota(jnp.int32, turned_ref.shape, 1)
    turned_ref[...] = (index == column).astype(jnp.bfloat16)


def place_rows(flat, rows, pieces, capacity):
    count, width = rows.shape
    outs = pl.pallas_call(
        functools.partial(place_kernel, capacity),
        out_shape=[
            jax.ShapeDtypeStruct((pieces * capacity, count), jnp.bfloat16),
            jax.ShapeDtypeStruct((count, pieces * capacity), jnp.bfloat16),
        ]
        + [jax.ShapeDtypeStruct((capacity, width), jnp.bfloat16)] * pieces,
        compiler_params=pltpu.CompilerParams(vmem_limit_bytes=48 * 2**20),
        cost_estimate=cost(2 * pieces * capacity * count * width),
    )(flat[None, :], flat[:, None], rows)
    return outs[0], outs[1], list(outs[2:])


def second_norm(rows, gain):
    scale = lax.rsqrt(jnp.mean(rows * rows, axis=-1, keepdims=True) + EPSILON)
    hat = rows * scale
    return scale, hat, hat * gain


def send_kernel(capacity, mixed_ref, weight_ref, rows_ref, gain_ref, router_ref, hot_ref, place_ref, *refs):
    residual_ref, probs_ref, gate_ref = refs[:3]
    residual = rows_ref[...] + dot_tn(mixed_ref[...], weight_ref[...])
    residual_ref[...] = residual
    _, _, normed = second_norm(residual, gain_ref[...])
    logits = dot_exact(router_ref[...], normed, (1, 1))
    logits = jnp.exp(logits - jnp.max(logits, axis=0, keepdims=True))
    probs = logits / jnp.sum(logits, axis=0, keepdims=True)
    probs_ref[...] = probs
    gate = jnp.sum(probs * hot_ref[...], axis=0, keepdims=True)
    gate_ref[...] = gate
    low = normed.astype(jnp.bfloat16)
    gates = jnp.broadcast_to(gate.astype(jnp.bfloat16), (8, gate.shape[1]))
    for k, ref in enumerate(refs[3:]):
        place = place_ref[k * capacity : (k + 1) * capacity, :]
        ref[:capacity, :] = dot_nn(place, low).astype(jnp.bfloat16)
        ref[capacity : capacity + 8, :] = jnp.zeros((8, ref.shape[1]), jnp.bfloat16)
        ref[capacity : capacity + 8, :capacity] = dot_nt(gates, place).astype(jnp.bfloat16)


def send_rows(mixed, weight, rows, gain, router, hot, place):
    experts, count = hot.shape
    width = rows.shape[1]
    capacity = place.shape[0] // experts
    outs = pl.pallas_call(
        functools.partial(send_kernel, capacity),
        out_shape=[
            jax.ShapeDtypeStruct((count, width), jnp.float32),
            jax.ShapeDtypeStruct((experts, count), jnp.float32),
            jax.ShapeDtypeStruct((1, count), jnp.float32),
        ]
        + [jax.ShapeDtypeStruct((capacity + 8, width), jnp.bfloat16)] * experts,
        compiler_params=pltpu.CompilerParams(vmem_limit_bytes=48 * 2**20),
        cost_estimate=cost(6 * width * count * width),
    )(mixed, weight, rows, gain, router, hot, place)
    return outs[0], outs[1], outs[2], list(outs[3:])


def receive_kernel(capacity, residual_ref, cot_ref, gain_ref, router_ref, hot_ref, probs_ref, gate_ref, place_ref, turned_ref, weight_ref, *refs):
    backs, (grad_ref, low_ref, heads_ref, router_grad_ref, gain_grad_ref) = refs[:-5], refs[-5:]
    scale, hat, normed = second_norm(residual_ref[...], gain_ref[...])
    grad, pair = 0.0, 0.0
    for k, ref in enumerate(backs):
        span = slice(k * capacity, (k + 1) * capacity)
        grad = grad + dot_nn(turned_ref[:, span], ref[:capacity, :])
        pair = pair + dot_nn(ref[capacity : capacity + 8, :capacity], place_ref[span, :])
    grad_gate = jnp.sum(pair, axis=0, keepdims=True)
    grad_logits = probs_ref[...] * (hot_ref[...] - gate_ref[...]) * grad_gate
    router_grad_ref[...] = dot_exact(grad_logits, normed, (1, 0))
    grad = grad + dot_exact(grad_logits, router_ref[...], (0, 0))
    gain_grad_ref[...] = jnp.sum(grad * hat, axis=0, keepdims=True)
    scaled = grad * gain_ref[...]
    grad = scale * (scaled - hat * jnp.mean(scaled * hat, axis=-1, keepdims=True))
    grad = grad + cot_ref[...].astype(jnp.float32)
    grad_ref[...] = grad
    low = grad.astype(jnp.bfloat16)
    low_ref[...] = low
    heads_ref[...] = dot_nt(weight_ref[...], low).astype(jnp.bfloat16)


def receive_rows(residual, cot, gain, router, hot, probs, gate, place, turned, weight, backs):
    experts, count = hot.shape
    width = residual.shape[1]
    return pl.pallas_call(
        functools.partial(receive_kernel, place.shape[0] // experts),
        out_shape=[
            jax.ShapeDtypeStruct((count, width), jnp.float32),
            jax.ShapeDtypeStruct((count, width), jnp.bfloat16),
            jax.ShapeDtypeStruct((weight.shape[0], count), jnp.bfloat16),
            jax.ShapeDtypeStruct((experts, width), jnp.float32),
            jax.ShapeDtypeStruct((1, width), jnp.float32),
        ],
        compiler_params=pltpu.CompilerParams(vmem_limit_bytes=48 * 2**20),
        cost_estimate=cost(6 * width * count * width),
    )(residual, cot, gain, router, hot, probs, gate, place, turned, weight, *backs)


def project_kernel(x_ref, gain_ref, weight_ref, out_ref, normed_ref):
    rows = x_ref[...]
    scale = lax.rsqrt(jnp.mean(rows * rows, axis=-1, keepdims=True) + EPSILON)
    normed = (rows * scale * gain_ref[...]).astype(jnp.bfloat16)
    normed_ref[...] = normed
    out_ref[...] = dot_nt(weight_ref[...], normed).astype(jnp.bfloat16)


def project(rows, gain, weights, tile):
    count, width = rows.shape
    columns = weights.shape[0]
    return pl.pallas_call(
        project_kernel,
        grid=(count // tile,),
        in_specs=[
            pl.BlockSpec((tile, width), lambda i: (i, 0)),
            pl.BlockSpec((1, width), lambda i: (0, 0)),
            pl.BlockSpec((columns, width), lambda i: (0, 0)),
        ],
        out_specs=[
            pl.BlockSpec((columns, tile), lambda i: (0, i)),
            pl.BlockSpec((tile, width), lambda i: (i, 0)),
        ],
        out_shape=[
            jax.ShapeDtypeStruct((columns, count), jnp.bfloat16),
            jax.ShapeDtypeStruct((count, width), jnp.bfloat16),
        ],
        compiler_params=pltpu.CompilerParams(vmem_limit_bytes=48 * 2**20),
        cost_estimate=cost(4 * count * width * columns),
    )(rows, gain, weights)


def gelu_parts(values):
    root = 0.7978845608028654
    square = values * values
    bend = jnp.tanh(root * values * (1.0 + 0.044715 * square))
    half = 0.5 + 0.5 * bend
    slope = half + half * (1.0 - bend) * values * (root + (3.0 * 0.044715 * root) * square)
    return values * half, slope


def expert_kernel(parts, pieces, *refs):
    row_refs, grad_refs, refs = refs[:pieces], refs[pieces : 2 * pieces], refs[2 * pieces :]
    first_refs, second_refs, refs = refs[:parts], refs[parts : 2 * parts], refs[2 * parts :]
    act_ref, pre_ref, xt_ref, lt_ref = refs[:4]
    res_refs, back_refs = refs[4 : 4 + pieces], refs[4 + pieces : 4 + 2 * pieces]
    rows, low, res_sum, back_sum, firsts, seconds, sems = refs[4 + 2 * pieces :]
    step = pl.program_id(0)
    capacity = grad_refs[0].shape[0]
    width = grad_refs[0].shape[1]
    count = pieces * capacity
    tile = min(count, 256)

    def fetch(j):
        copies = []
        for i in range(2):
            to = (j % 2, i)
            copies.append(pltpu.make_async_copy(first_refs[2 * j + i], firsts.at[to], sems.at[(0,) + to]))
            copies.append(pltpu.make_async_copy(second_refs[2 * j + i], seconds.at[to], sems.at[(1,) + to]))
        return copies

    @pl.when(step == 0)
    def _():
        for copy in fetch(0):
            copy.start()
        for e in range(pieces):
            span = pl.ds(e * capacity, capacity)
            rows[span, :] = row_refs[e][:capacity, :]
            gates = row_refs[e][capacity : capacity + 8, :capacity].astype(jnp.float32).T[:, 0:1]
            low[span, :] = (gates * grad_refs[e][...].astype(jnp.float32)).astype(jnp.bfloat16)
        res_sum[...] = jnp.zeros_like(res_sum)
        back_sum[...] = jnp.zeros_like(back_sum)

    for j in range(parts // 2):

        @pl.when(step == j)
        def _(j=j):
            if j + 1 < parts // 2:
                for copy in fetch(j + 1):
                    copy.start()
            for copy in fetch(j):
                copy.wait()

    @pl.when(step == 0)
    def _():
        xt_ref[...] = rows[...].T
        lt_ref[...] = low[...].T

    slot = step % 2
    spans = [pl.ds(start, tile) for start in range(0, count, tile)]
    chains = [(i, span) for span in spans for i in range(2)]
    values = [dot_nn(rows[span, :], firsts[slot, i]) for i, span in chains]
    grads = [dot_nt(low[span, :], seconds[slot, i]) for i, span in chains]
    for (i, span), value, grad in zip(chains, values, grads):
        active, slope = gelu_parts(value)
        active = active.astype(jnp.bfloat16)
        act_ref[i, span, :] = active
        res_sum[span, :] += dot_nn(active, seconds[slot, i])
        pre = (grad * slope).astype(jnp.bfloat16)
        pre_ref[i, span, :] = pre
        back_sum[span, :] += dot_nt(pre, firsts[slot, i])

    @pl.when(step == parts // 2 - 1)
    def _():
        for e in range(pieces):
            span = pl.ds(e * capacity, capacity)
            res_refs[e][...] = res_sum[span, :].astype(jnp.bfloat16)
            back_refs[e][:capacity, :] = back_sum[span, :].astype(jnp.bfloat16)
            sums = jnp.sum(
                res_sum[span, :] * grad_refs[e][...].astype(jnp.float32), axis=1, keepdims=True
            )
            sums = jnp.broadcast_to(sums, (capacity, 128)).T[0:8, :]
            high = sums.astype(jnp.bfloat16).astype(jnp.float32)
            index = lax.broadcasted_iota(jnp.int32, sums.shape, 0)
            pair = jnp.where(index == 0, high, jnp.where(index == 1, sums - high, 0.0))
            back_refs[e][capacity : capacity + 8, :] = jnp.zeros((8, width), jnp.bfloat16)
            back_refs[e][capacity : capacity + 8, :capacity] = pair.astype(jnp.bfloat16)


MINE = ((0, 4, 2, 6), (0, 2, 4, 6))
OTHER = ((1, 5, 3, 7), (1, 3, 5, 7))


def expert_apply(arrived, grads, firsts, seconds):
    pieces = len(grads)
    capacity, width = grads[0].shape
    count = pieces * capacity
    parts, hidden = len(firsts), firsts[0].shape[1]
    sent = pl.BlockSpec(arrived[0].shape, lambda i: (0, 0))
    whole = pl.BlockSpec((capacity, width), lambda i: (0, 0))
    kept = pl.BlockSpec((2, count, hidden), lambda i: (i, 0, 0))
    turned = pl.BlockSpec((width, count), lambda i: (0, 0))
    outs = pl.pallas_call(
        functools.partial(expert_kernel, parts, pieces),
        grid=(parts // 2,),
        in_specs=[sent] * pieces + [whole] * pieces + [pl.BlockSpec(memory_space=pl.ANY)] * (2 * parts),
        out_specs=[kept, kept, turned, turned] + [whole] * pieces + [sent] * pieces,
        out_shape=[
            jax.ShapeDtypeStruct((parts, count, hidden), jnp.bfloat16),
            jax.ShapeDtypeStruct((parts, count, hidden), jnp.bfloat16),
            jax.ShapeDtypeStruct((width, count), jnp.bfloat16),
            jax.ShapeDtypeStruct((width, count), jnp.bfloat16),
        ]
        + [jax.ShapeDtypeStruct((capacity, width), jnp.bfloat16)] * pieces
        + [jax.ShapeDtypeStruct(arrived[0].shape, jnp.bfloat16)] * pieces,
        scratch_shapes=[
            pltpu.VMEM((count, width), jnp.bfloat16),
            pltpu.VMEM((count, width), jnp.bfloat16),
            pltpu.VMEM((count, width), jnp.float32),
            pltpu.VMEM((count, width), jnp.float32),
            pltpu.VMEM((2, 2, width, hidden), jnp.bfloat16),
            pltpu.VMEM((2, 2, hidden, width), jnp.bfloat16),
            pltpu.SemaphoreType.DMA((2, 2, 2)),
        ],
        compiler_params=pltpu.CompilerParams(vmem_limit_bytes=52 * 2**20),
        cost_estimate=cost(12 * count * width * hidden * parts),
    )(*arrived, *grads, *firsts, *seconds)
    return list(outs[:4]), list(outs[4 : 4 + pieces]), list(outs[4 + pieces :])


def weight_kernel(groups, *refs):
    step = pl.program_id(0)
    outs = refs[4 * groups :]
    steps = pl.num_programs(0) // 2
    for out, (left, right) in enumerate(((2, 1), (3, 0))):
        total = 0.0
        for g in range(groups):
            total = total + dot_nn(refs[4 * g + left][...], refs[4 * g + right][0])
        total = total.astype(jnp.bfloat16)

        @pl.when(step < steps)
        def _():
            outs[out][0] = total

        @pl.when(step >= steps)
        def _():
            outs[2 + out][0] = total


def expert_weights(groups):
    chosen = [OTHER[i] + MINE[i] for i in range(2)]
    steps, hidden = len(chosen[0]), groups[0][0].shape[2]
    width = groups[0][2].shape[0]
    specs, arrays = [], []

    def pick(i, which):
        return sum(jnp.where(i == j, at, 0) for j, at in enumerate(chosen[which]))

    for act, pre, xt, lt in groups:
        block = (1,) + act.shape[1:]
        whole = pl.BlockSpec(xt.shape, lambda i: (0, 0))
        specs += [
            pl.BlockSpec(block, lambda i: (pick(i, 1), 0, 0)),
            pl.BlockSpec(block, lambda i: (pick(i, 0), 0, 0)),
            whole,
            whole,
        ]
        arrays += [act, pre, xt, lt]
    half = steps // 2
    early = pl.BlockSpec((1, width, hidden), lambda i: (jnp.minimum(i, half - 1), 0, 0))
    late = pl.BlockSpec((1, width, hidden), lambda i: (jnp.maximum(i - half, 0), 0, 0))
    count = sum(group[2].shape[1] for group in groups)
    return pl.pallas_call(
        functools.partial(weight_kernel, len(groups)),
        grid=(steps,),
        in_specs=specs,
        out_specs=[early, early, late, late],
        out_shape=[jax.ShapeDtypeStruct((half, width, hidden), jnp.bfloat16)] * 4,
        compiler_params=pltpu.CompilerParams(vmem_limit_bytes=50 * 2**20),
        cost_estimate=cost(6 * count * width * hidden * steps),
    )(*arrays)


def inverse_rms(rows):
    return lax.rsqrt(jnp.mean(rows * rows, axis=-1, keepdims=True) + EPSILON)


def norm_backward(grad_normed, gain, normed_hat, inv_scale):
    scaled = grad_normed * gain
    return inv_scale * (scaled - normed_hat * jnp.mean(scaled * normed_hat, axis=-1, keepdims=True))


def swap(array, axis, offset):
    count = lax.axis_size(axis)
    return lax.ppermute(array, axis, [(i, i ^ offset) for i in range(count)])


def trade(array, axis):
    return lax.all_to_all(array, axis, 0, 0, tiled=True)


def low_sum(*arrays):
    return sum(array.astype(jnp.float32) for array in arrays).astype(jnp.bfloat16)


def spread(array, axis):
    return trade(jnp.broadcast_to(array[None], (lax.axis_size(axis),) + array.shape), axis)


def on_device(
    layer_input,
    cotangent,
    norm1_gain,
    w_query,
    w_key,
    w_value,
    w_output,
    bias_table,
    bucket,
    norm2_gain,
    router,
    expert_index,
    w_in,
    w_out,
):
    group_rows, width = layer_input.shape
    tensor_count = lax.axis_size("tensor")
    tensor_rank = lax.axis_index("tensor")
    dp_rank = lax.axis_index("dp")
    own_rows = group_rows // tensor_count
    own_start = tensor_rank * own_rows
    local_heads = bias_table.shape[1]
    inner = local_heads * HEAD_DIM
    experts = router.shape[1]
    capacity = 2 * own_rows // experts
    slots = experts * capacity

    half = w_in.shape[2] // 2
    first_mine = lax.dynamic_slice_in_dim(w_in[0], dp_rank * half, half, 1)
    first_other = lax.dynamic_slice_in_dim(w_in[0], (1 - dp_rank) * half, half, 1)
    second_mine = lax.dynamic_slice_in_dim(w_out[0], dp_rank * half, half, 0)
    second_other = lax.dynamic_slice_in_dim(w_out[0], (1 - dp_rank) * half, half, 0)
    w_joined = jnp.concatenate([w_query.T, w_key.T, w_value.T], axis=0)
    output_full = spread(w_output, "tensor")

    routes = lax.dynamic_slice_in_dim(expert_index[:, 0], own_start, own_rows, 0)
    own_hot = routes[:, None] == jnp.arange(experts, dtype=jnp.int32)[None, :]
    row_ids = jnp.arange(own_rows, dtype=jnp.int32)
    earlier = (row_ids[None, :] < row_ids[:, None]).astype(jnp.bfloat16)
    before = jnp.dot(earlier, own_hot.astype(jnp.bfloat16), preferred_element_type=jnp.float32)
    own_hot = own_hot.astype(jnp.float32)
    slot = jnp.sum(before * own_hot, axis=-1).astype(jnp.int32)
    flat = (routes ^ lax.axis_index("expert")) * capacity + slot
    cot_low = lax.dynamic_slice_in_dim(cotangent, own_start, own_rows, 0)
    place_hot, place_turned, grad_in = place_rows(flat, cot_low, experts, capacity)
    near = experts // 2
    far = near + experts // 4
    grad_in = [grad_in[0]] + [swap(grad_in[k], "expert", k) for k in range(1, far)] + grad_in[far:]

    gain_one = norm1_gain.astype(jnp.float32)
    projected, normed_one = project(layer_input, gain_one[None, :], w_joined, own_rows)
    high_bit = tensor_count // 2
    first_near = swap(first_mine, "tensor", 1)
    second_near = swap(second_mine, "tensor", high_bit)
    first_far = [swap(first_mine, "tensor", high_bit)]
    second_far = [swap(second_mine, "tensor", 1)]
    turned = jnp.concatenate([bucket[::-1], jnp.full((1,), -1, jnp.int32)])
    bucket_hot = jnp.arange(NUM_BUCKETS, dtype=jnp.int32)[:, None] == turned[None, :]
    vectors = dot_tn(bias_table, bucket_hot.astype(jnp.bfloat16))[:, None, :]
    mixed, logs = attend(projected, vectors, own_rows)
    mixed, output_full, first_near, second_near, first_far, second_far, grad_in[1:far] = (
        lax.optimization_barrier(
            (mixed, output_full, first_near, second_near, first_far, second_far, grad_in[1:far])
        )
    )
    output_full = output_full.reshape(tensor_count * inner, width)
    first_far.append(swap(first_near, "tensor", high_bit))
    second_far.append(swap(second_near, "tensor", 1))
    grad_in[far:] = [swap(grad_in[k], "expert", k) for k in range(far, experts)]
    mixed_own = trade(mixed.reshape(tensor_count, inner, own_rows), "tensor").reshape(
        tensor_count * inner, own_rows
    )

    input_own = lax.dynamic_slice_in_dim(layer_input, own_start, own_rows, 0)
    gain_two = norm2_gain.astype(jnp.float32)[None, :]
    router_turned = router.astype(jnp.float32).T
    hot_turned = own_hot.T
    residual, router_probs, gate, sent = send_rows(
        mixed_own, output_full, input_own, gain_two, router_turned, hot_turned, place_hot
    )
    sent, grad_in[far:] = lax.optimization_barrier((sent, grad_in[far:]))
    arrived = [sent[0]] + [swap(sent[k], "expert", k) for k in range(1, experts)]

    first_parts, second_parts = [first_mine, first_other], [second_mine, second_other]
    for first, second in ((first_near, second_far[0]), (first_far[0], second_near)):
        first_parts += [first, swap(first, "dp", 1)]
        second_parts += [second, swap(second, "dp", 1)]
    arrived[1:near], first, second = lax.optimization_barrier(
        (arrived[1:near], first_far[1], second_far[1])
    )
    first_parts += [first, swap(first, "dp", 1)]
    second_parts += [second, swap(second, "dp", 1)]
    arrived[:near], first_parts, second_parts, joined = lax.optimization_barrier(
        (arrived[:near], first_parts, second_parts, w_joined)
    )
    joined_parts = [w_joined] + [swap(joined, "tensor", k) for k in range(1, tensor_count - 1)]
    groups, results, back_got = [], [], []
    for low, high in ((0, near), (near, far), (far, experts)):
        pieces = arrived[low:high]
        if low == near:
            results, pieces, joined, joined_parts = lax.optimization_barrier(
                (results, pieces, joined, joined_parts)
            )
            joined_parts.append(swap(joined, "tensor", tensor_count - 1))
        if low == far:
            results, pieces = lax.optimization_barrier((results, pieces))
        kept, res, back = expert_apply(pieces, grad_in[low:high], first_parts, second_parts)
        groups.append(kept)
        results += res
        back_got += [
            back[k - low] if k == 0 else swap(back[k - low], "expert", k) for k in range(low, high)
        ]
    groups, joined_parts = lax.optimization_barrier((groups, joined_parts))
    first_other, second_other, first_sum, second_sum = expert_weights(groups)
    first_other, second_other, first_sum, second_sum, back_got = lax.optimization_barrier(
        (first_other, second_other, first_sum, second_sum, back_got)
    )
    first_other, second_other = swap(first_other, "dp", 1), swap(second_other, "dp", 1)

    grad_residual, grad_low, grad_heads, grad_router, grad_norm_two = receive_rows(
        residual,
        cot_low,
        gain_two,
        router_turned,
        hot_turned,
        router_probs,
        gate,
        place_hot,
        place_turned,
        output_full,
        back_got,
    )
    heads_got = trade(grad_heads.reshape(tensor_count, inner, own_rows), "tensor")
    grad_wo = dot_nn(mixed_own, grad_low).astype(jnp.bfloat16).reshape(tensor_count, inner, width)
    shared = jnp.concatenate([grad_router, grad_norm_two], axis=0).astype(jnp.bfloat16)
    shared = jnp.pad(shared, ((0, -shared.shape[0] % 8), (0, 0)))
    shared = jnp.broadcast_to(shared[None], (tensor_count,) + shared.shape)
    grad_wo = trade(jnp.concatenate([grad_wo, shared], axis=1), "tensor")
    _, *results = lax.optimization_barrier((grad_low, *results))
    returned = [results[0]] + [swap(results[k], "expert", k) for k in range(1, experts)]

    heads_got, first_other, second_other = lax.optimization_barrier(
        (heads_got, first_other, second_other)
    )
    first_got = swap(low_sum(first_sum[2:], first_other[2:]), "tensor", 1)
    second_got = swap(low_sum(second_sum[2:], second_other[2:]), "tensor", high_bit)
    head_shape = (tensor_count, local_heads, HEAD_DIM, own_rows)
    grad_projected, diagonals = attend_back(
        projected, vectors, mixed, heads_got.reshape(head_shape), logs
    )
    grad_projected = grad_projected.reshape(tensor_count, 3 * inner, own_rows)
    grad_projected, first_got, second_got, returned, grad_wo = lax.optimization_barrier(
        (grad_projected, first_got, second_got, returned, grad_wo)
    )

    grad_got = [lax.dynamic_index_in_dim(grad_projected, tensor_rank, 0, keepdims=False)]
    for k in range(1, tensor_count):
        sent = lax.dynamic_index_in_dim(grad_projected, tensor_rank ^ k, 0, keepdims=False)
        grad_got.append(swap(sent, "tensor", k))

    grad_wo = jnp.sum(grad_wo.astype(jnp.float32), axis=0)
    grad_joined = jnp.einsum(
        "bcn,bnd->cd",
        grad_projected,
        normed_one.reshape(tensor_count, own_rows, width),
        preferred_element_type=jnp.float32,
    )
    norm_one = jnp.sum(grad_joined * w_joined.astype(jnp.float32), axis=0) / gain_one
    grad_table = jnp.einsum(
        "br,hr->hb", bucket_hot.astype(jnp.float32), diagonals[:, 0], precision=HIGHEST
    ).reshape(-1)
    table_size = grad_table.shape[0]
    used = 3 * inner
    main = jnp.concatenate(
        [grad_joined, grad_wo, jnp.pad(grad_table, (0, width - table_size))[None]], axis=0
    )
    main = jnp.pad(main, ((0, -main.shape[0] % 16), (0, 0)))
    rows = main.shape[0] // 2
    main_mine = lax.dynamic_slice_in_dim(main, dp_rank * rows, rows, 0)
    main_other = lax.dynamic_slice_in_dim(main, (1 - dp_rank) * rows, rows, 0)
    extra = jnp.pad(norm_one[None], ((0, (-rows - 1) % max(8, experts)), (0, 0)))
    main_mine = jnp.concatenate([main_mine, extra], axis=0)
    main_other = jnp.concatenate([main_other, extra], axis=0).astype(jnp.bfloat16)
    main_other, returned, first_got, second_got = lax.optimization_barrier(
        (swap(main_other, "dp", 1), returned, first_got, second_got)
    )
    main_mine = (main_mine + main_other.astype(jnp.float32)).astype(jnp.bfloat16)
    shares = trade(main_mine.reshape(experts, -1, width), "expert")

    first_pair = low_sum(first_sum[:2], first_other[:2], first_got)
    second_pair = low_sum(second_sum[:2], second_other[:2], second_got)
    first_got = swap(first_pair[1], "tensor", high_bit)
    second_got = swap(second_pair[1], "tensor", 1)
    output = residual + gate[0].astype(jnp.bfloat16).astype(jnp.float32)[:, None] * dot_nn(
        place_turned, jnp.concatenate(returned)
    )
    shares, grad_got, input_own = lax.optimization_barrier((shares, grad_got, input_own))
    main_mine = spread(low_sum(*shares), "expert").reshape(main_mine.shape)
    main_mine, first_got, second_got = lax.optimization_barrier((main_mine, first_got, second_got))
    pairs = ((first_pair, first_got), (second_pair, second_got))
    total = jnp.stack([low_sum(pair[0], got) for pair, got in pairs])
    rest = swap(total, "dp", 1)
    norm_one = main_mine[rows].astype(jnp.float32)
    norm_one = norm_one + sum(swap(norm_one, "tensor", k) for k in range(1, tensor_count))
    main_mine = main_mine[:rows]
    main_other = swap(main_mine, "dp", 1)
    first = dp_rank == 0
    both = jnp.concatenate(
        [jnp.where(first, total, rest), jnp.where(first, rest, total)], axis=2
    ).astype(jnp.float32)
    joined = jnp.concatenate(
        [jnp.where(first, main_mine, main_other), jnp.where(first, main_other, main_mine)], axis=0
    ).astype(jnp.float32)
    shared = joined[used + inner :]

    grad_normed_one = sum(dot_tn(got, part) for got, part in zip(grad_got, joined_parts))
    inv_own = inverse_rms(input_own)
    input_grad = grad_residual + norm_backward(grad_normed_one, gain_one, input_own * inv_own, inv_own)
    return (
        output,
        input_grad,
        joined[:inner].T,
        joined[inner : 2 * inner].T,
        joined[2 * inner : used].T,
        joined[used : used + inner],
        shared[grad_wo.shape[0] - inner, :table_size].reshape(local_heads, NUM_BUCKETS).T,
        norm_one,
        shared[experts],
        shared[:experts].T,
        both[0][None],
        both[1].T[None],
    )


def solution(mesh):
    return jax.shard_map(
        on_device,
        mesh=mesh,
        in_specs=(
            P(("dp", "expert"), None),
            P(("dp", "expert"), None),
            P(),
            P(None, "tensor"),
            P(None, "tensor"),
            P(None, "tensor"),
            P("tensor", None),
            P(None, "tensor"),
            P(),
            P(),
            P(),
            P(("dp", "expert"), None),
            P("expert", None, "tensor"),
            P("expert", "tensor", None),
        ),
        out_specs=(
            P(("dp", "expert", "tensor"), None),
            P(("dp", "expert", "tensor"), None),
            P(None, "tensor"),
            P(None, "tensor"),
            P(None, "tensor"),
            P("tensor", None),
            P(None, "tensor"),
            P(),
            P(),
            P(),
            P("expert", None, "tensor"),
            P("expert", "tensor", None),
        ),
        check_vma=False,
    )
```

```python
import functools
import jax
import jax.numpy as jnp
from jax import lax
from jax.sharding import PartitionSpec as P
from jax.experimental import pallas as pl
from jax.experimental.pallas import tpu as pltpu

HEAD_DIM = 64
NUM_BUCKETS = 32
EPSILON = 1e-06
HIGHEST = lax.Precision.HIGHEST
CHUNK = 512


def cost(work):
    return pl.CostEstimate(flops=work, bytes_accessed=work // 1024, transcendentals=0)

BAND = 128


def dot_nt(a, b):
    return lax.dot_general(a, b, (((1,), (1,)), ((), ())), preferred_element_type=jnp.float32)


def dot_nn(a, b):
    return lax.dot_general(a, b, (((1,), (0,)), ((), ())), preferred_element_type=jnp.float32)


def dot_tn(a, b):
    return lax.dot_general(a, b, (((0,), (0,)), ((), ())), preferred_element_type=jnp.float32)


def fill_band(band, vector):
    span = vector.shape[1]
    rows = jnp.broadcast_to(vector, (8, span))
    rows = pltpu.roll(rows, span - (BAND - 1), 1)
    index = lax.broadcasted_iota(jnp.int32, (8, span), 0)
    for step in (1, 2, 4):
        rows = jnp.where((index & step) != 0, pltpu.roll(rows, step, 1), rows)
    band[0:8, :] = rows
    step = 8
    while step < BAND:
        band[step : 2 * step, :] = pltpu.roll(band[0:step, :], step, 1)
        step *= 2


def fold_band(band):
    span = band.shape[1]
    step = BAND // 2
    while step >= 8:
        band[0:step, :] += pltpu.roll(band[step : 2 * step, :], span - step, 1)
        step //= 2
    rows = band[0:8, :]
    index = lax.broadcasted_iota(jnp.int32, (8, span), 0)
    for step in (1, 2, 4):
        rows = jnp.where((index & step) != 0, pltpu.roll(rows, span - step, 1), rows)
    total = jnp.sum(rows, axis=0, keepdims=True)
    return pltpu.roll(total, BAND - 1, 1)


def attend_kernel(q_ref, k_ref, v_ref, vec_ref, out_ref, log_ref, band):
    seq = k_ref.shape[3]
    own = out_ref.shape[3]

    @pl.when(pl.program_id(1) == 0)
    def _():
        fill_band(band, vec_ref[0])

    keys = k_ref[0, 0].T
    values = v_ref[0, 0]
    for start in range(0, seq, CHUNK):
        queries = q_ref[0, 0, :, start : start + CHUNK] * jnp.bfloat16(HEAD_DIM ** -0.5)
        raw = dot_nn(keys, queries)
        parts = []
        for low in range(0, seq, BAND):
            at = start - low + seq - BAND
            parts.append(raw[low : low + BAND] + band[:, at : at + CHUNK])
        peak = functools.reduce(jnp.maximum, parts)
        peak = jnp.max(peak, axis=0, keepdims=True)
        parts = [jnp.exp(part - peak) for part in parts]
        total = jnp.sum(functools.reduce(jnp.add, parts), axis=0, keepdims=True)
        weights = jnp.concatenate([part.astype(jnp.bfloat16) for part in parts], axis=0)
        mixed = dot_nn(values, weights) / total
        out_ref[start // own, 0, :, start % own : start % own + CHUNK] = mixed.astype(jnp.bfloat16)
        log_ref[0, 0, :, start : start + CHUNK] = peak + jnp.log(total)


def attend(projected, vectors, own):
    heads, seq = vectors.shape[0], vectors.shape[2] // 2
    seqs = projected.shape[1] // seq
    blocks = seq // own
    part = lambda p: pl.BlockSpec((1, 1, HEAD_DIM, seq), lambda h, s, p=p: (p, h, 0, s))
    proj = projected.reshape(3, heads, HEAD_DIM, seqs * seq)
    return pl.pallas_call(
        attend_kernel,
        grid=(heads, seqs),
        in_specs=[part(0), part(1), part(2), pl.BlockSpec((1, 1, 2 * seq), lambda h, s: (h, 0, 0))],
        out_specs=[
            pl.BlockSpec((blocks, 1, HEAD_DIM, own), lambda h, s: (s, h, 0, 0)),
            pl.BlockSpec((1, 1, 1, seq), lambda h, s: (h, s, 0, 0)),
        ],
        out_shape=[
            jax.ShapeDtypeStruct((seqs * blocks, heads, HEAD_DIM, own), jnp.bfloat16),
            jax.ShapeDtypeStruct((heads, seqs, 1, seq), jnp.float32),
        ],
        scratch_shapes=[pltpu.VMEM((BAND, 2 * seq), jnp.float32)],
        compiler_params=pltpu.CompilerParams(vmem_limit_bytes=48 * 2**20),
        cost_estimate=cost(16 * heads * seqs * seq * seq * HEAD_DIM),
    )(proj, proj, proj, vectors)


def attend_back_kernel(q_ref, k_ref, v_ref, o_ref, g_ref, log_ref, vec_ref, out_ref, diag_ref, band, fold, dk, dv):
    seq = k_ref.shape[3]
    own = out_ref.shape[4]
    scale = HEAD_DIM ** -0.5

    @pl.when(pl.program_id(1) == 0)
    def _():
        fill_band(band, vec_ref[0])
        fold[...] = jnp.zeros_like(fold)

    keys_t = k_ref[0, 0]
    keys = keys_t.T
    values = v_ref[0, 0].T
    for start in range(0, seq, CHUNK):
        block, inner = start // own, start % own
        queries = q_ref[0, 0, :, start : start + CHUNK] * jnp.bfloat16(scale)
        grads = g_ref[block, 0, :, inner : inner + CHUNK]
        mixed = o_ref[block, 0, :, inner : inner + CHUNK]
        delta = jnp.sum(grads.astype(jnp.float32) * mixed.astype(jnp.float32), axis=0, keepdims=True)
        logs = log_ref[0, 0, :, start : start + CHUNK]
        raw = dot_nn(keys, queries)
        grad_weights = dot_nn(values, grads)
        low_weights, low_scores = [], []
        for low in range(0, seq, BAND):
            at = start - low + seq - BAND
            weights = jnp.exp(raw[low : low + BAND] + band[:, at : at + CHUNK] - logs)
            scores = weights * (grad_weights[low : low + BAND] - delta)
            fold[:, at : at + CHUNK] += scores
            low_weights.append(weights.astype(jnp.bfloat16))
            low_scores.append(scores.astype(jnp.bfloat16))
        weights = jnp.concatenate(low_weights, axis=0)
        scores = jnp.concatenate(low_scores, axis=0)
        grad_q = dot_nn(keys_t, scores) * scale
        out_ref[block, 0, 0, :, inner : inner + CHUNK] = grad_q.astype(jnp.bfloat16)
        if start == 0:
            dk[...] = dot_nt(queries, scores)
            dv[...] = dot_nt(grads, weights)
        else:
            dk[...] += dot_nt(queries, scores)
            dv[...] += dot_nt(grads, weights)
    for block in range(seq // own):
        out_ref[block, 1, 0] = dk[:, block * own : (block + 1) * own].astype(jnp.bfloat16)
        out_ref[block, 2, 0] = dv[:, block * own : (block + 1) * own].astype(jnp.bfloat16)

    @pl.when(pl.program_id(1) == pl.num_programs(1) - 1)
    def _():
        diag_ref[0] = fold_band(fold)


def attend_back(projected, vectors, mixed, grads, logs):
    heads, seq = vectors.shape[0], vectors.shape[2] // 2
    seqs = projected.shape[1] // seq
    own = mixed.shape[3]
    blocks = seq // own
    part = lambda p: pl.BlockSpec((1, 1, HEAD_DIM, seq), lambda h, s, p=p: (p, h, 0, s))
    side = pl.BlockSpec((blocks, 1, HEAD_DIM, own), lambda h, s: (s, h, 0, 0))
    vec = pl.BlockSpec((1, 1, 2 * seq), lambda h, s: (h, 0, 0))
    proj = projected.reshape(3, heads, HEAD_DIM, seqs * seq)
    return pl.pallas_call(
        attend_back_kernel,
        grid=(heads, seqs),
        in_specs=[part(0), part(1), part(2), side, side,
                  pl.BlockSpec((1, 1, 1, seq), lambda h, s: (h, s, 0, 0)), vec],
        out_specs=[
            pl.BlockSpec((blocks, 3, 1, HEAD_DIM, own), lambda h, s: (s, 0, h, 0, 0)),
            vec,
        ],
        out_shape=[
            jax.ShapeDtypeStruct((seqs * blocks, 3, heads, HEAD_DIM, own), jnp.bfloat16),
            jax.ShapeDtypeStruct((heads, 1, 2 * seq), jnp.float32),
        ],
        scratch_shapes=[
            pltpu.VMEM((BAND, 2 * seq), jnp.float32),
            pltpu.VMEM((BAND, 2 * seq), jnp.float32),
            pltpu.VMEM((HEAD_DIM, seq), jnp.float32),
            pltpu.VMEM((HEAD_DIM, seq), jnp.float32),
        ],
        compiler_params=pltpu.CompilerParams(vmem_limit_bytes=48 * 2**20),
        cost_estimate=cost(32 * heads * seqs * seq * seq * HEAD_DIM),
    )(proj, proj, proj, mixed, grads, logs, vectors)


def dot_exact(a, b, axes):
    return lax.dot_general(
        a, b, ((axes[:1], axes[1:]), ((), ())), precision=HIGHEST, preferred_element_type=jnp.float32
    )


def place_kernel(capacity, row_ref, column_ref, rows_ref, place_ref, turned_ref, *piece_refs):
    flat = row_ref[...]
    column = column_ref[...]
    for k, ref in enumerate(piece_refs):
        span = slice(k * capacity, (k + 1) * capacity)
        index = lax.broadcasted_iota(jnp.int32, (capacity, flat.shape[1]), 0) + k * capacity
        hot = (index == flat).astype(jnp.bfloat16)
        place_ref[span, :] = hot
        ref[...] = dot_nn(hot, rows_ref[...]).astype(jnp.bfloat16)
    index = lax.broadcasted_iota(jnp.int32, turned_ref.shape, 1)
    turned_ref[...] = (index == column).astype(jnp.bfloat16)


def place_rows(flat, rows, pieces, capacity):
    count, width = rows.shape
    outs = pl.pallas_call(
        functools.partial(place_kernel, capacity),
        out_shape=[
            jax.ShapeDtypeStruct((pieces * capacity, count), jnp.bfloat16),
            jax.ShapeDtypeStruct((count, pieces * capacity), jnp.bfloat16),
        ]
        + [jax.ShapeDtypeStruct((capacity, width), jnp.bfloat16)] * pieces,
        compiler_params=pltpu.CompilerParams(vmem_limit_bytes=48 * 2**20),
        cost_estimate=cost(2 * pieces * capacity * count * width),
    )(flat[None, :], flat[:, None], rows)
    return outs[0], outs[1], list(outs[2:])


def second_norm(rows, gain):
    scale = lax.rsqrt(jnp.mean(rows * rows, axis=-1, keepdims=True) + EPSILON)
    hat = rows * scale
    return scale, hat, hat * gain


def send_kernel(capacity, mixed_ref, weight_ref, rows_ref, gain_ref, router_ref, hot_ref, place_ref, *refs):
    residual_ref, probs_ref, gate_ref = refs[:3]
    residual = rows_ref[...] + dot_tn(mixed_ref[...], weight_ref[...])
    residual_ref[...] = residual
    _, _, normed = second_norm(residual, gain_ref[...])
    logits = dot_exact(router_ref[...], normed, (1, 1))
    logits = jnp.exp(logits - jnp.max(logits, axis=0, keepdims=True))
    probs = logits / jnp.sum(logits, axis=0, keepdims=True)
    probs_ref[...] = probs
    gate = jnp.sum(probs * hot_ref[...], axis=0, keepdims=True)
    gate_ref[...] = gate
    low = normed.astype(jnp.bfloat16)
    gates = jnp.broadcast_to(gate.astype(jnp.bfloat16), (8, gate.shape[1]))
    for k, ref in enumerate(refs[3:]):
        place = place_ref[k * capacity : (k + 1) * capacity, :]
        ref[:capacity, :] = dot_nn(place, low).astype(jnp.bfloat16)
        ref[capacity : capacity + 8, :] = jnp.zeros((8, ref.shape[1]), jnp.bfloat16)
        ref[capacity : capacity + 8, :capacity] = dot_nt(gates, place).astype(jnp.bfloat16)


def send_rows(mixed, weight, rows, gain, router, hot, place):
    experts, count = hot.shape
    width = rows.shape[1]
    capacity = place.shape[0] // experts
    outs = pl.pallas_call(
        functools.partial(send_kernel, capacity),
        out_shape=[
            jax.ShapeDtypeStruct((count, width), jnp.float32),
            jax.ShapeDtypeStruct((experts, count), jnp.float32),
            jax.ShapeDtypeStruct((1, count), jnp.float32),
        ]
        + [jax.ShapeDtypeStruct((capacity + 8, width), jnp.bfloat16)] * experts,
        compiler_params=pltpu.CompilerParams(vmem_limit_bytes=48 * 2**20),
        cost_estimate=cost(6 * width * count * width),
    )(mixed, weight, rows, gain, router, hot, place)
    return outs[0], outs[1], outs[2], list(outs[3:])


def receive_kernel(capacity, residual_ref, cot_ref, gain_ref, router_ref, hot_ref, probs_ref, gate_ref, place_ref, turned_ref, weight_ref, *refs):
    backs, (grad_ref, low_ref, heads_ref, router_grad_ref, gain_grad_ref) = refs[:-5], refs[-5:]
    scale, hat, normed = second_norm(residual_ref[...], gain_ref[...])
    grad, pair = 0.0, 0.0
    for k, ref in enumerate(backs):
        span = slice(k * capacity, (k + 1) * capacity)
        grad = grad + dot_nn(turned_ref[:, span], ref[:capacity, :])
        pair = pair + dot_nn(ref[capacity : capacity + 8, :capacity], place_ref[span, :])
    grad_gate = jnp.sum(pair, axis=0, keepdims=True)
    grad_logits = probs_ref[...] * (hot_ref[...] - gate_ref[...]) * grad_gate
    router_grad_ref[...] = dot_exact(grad_logits, normed, (1, 0))
    grad = grad + dot_exact(grad_logits, router_ref[...], (0, 0))
    gain_grad_ref[...] = jnp.sum(grad * hat, axis=0, keepdims=True)
    scaled = grad * gain_ref[...]
    grad = scale * (scaled - hat * jnp.mean(scaled * hat, axis=-1, keepdims=True))
    grad = grad + cot_ref[...].astype(jnp.float32)
    grad_ref[...] = grad
    low = grad.astype(jnp.bfloat16)
    low_ref[...] = low
    heads_ref[...] = dot_nt(weight_ref[...], low).astype(jnp.bfloat16)


def receive_rows(residual, cot, gain, router, hot, probs, gate, place, turned, weight, backs):
    experts, count = hot.shape
    width = residual.shape[1]
    return pl.pallas_call(
        functools.partial(receive_kernel, place.shape[0] // experts),
        out_shape=[
            jax.ShapeDtypeStruct((count, width), jnp.float32),
            jax.ShapeDtypeStruct((count, width), jnp.bfloat16),
            jax.ShapeDtypeStruct((weight.shape[0], count), jnp.bfloat16),
            jax.ShapeDtypeStruct((experts, width), jnp.float32),
            jax.ShapeDtypeStruct((1, width), jnp.float32),
        ],
        compiler_params=pltpu.CompilerParams(vmem_limit_bytes=48 * 2**20),
        cost_estimate=cost(6 * width * count * width),
    )(residual, cot, gain, router, hot, probs, gate, place, turned, weight, *backs)


def project_kernel(x_ref, gain_ref, weight_ref, out_ref, normed_ref):
    rows = x_ref[...]
    scale = lax.rsqrt(jnp.mean(rows * rows, axis=-1, keepdims=True) + EPSILON)
    normed = (rows * scale * gain_ref[...]).astype(jnp.bfloat16)
    normed_ref[...] = normed
    out_ref[...] = dot_nt(weight_ref[...], normed).astype(jnp.bfloat16)


def project(rows, gain, weights, tile):
    count, width = rows.shape
    columns = weights.shape[0]
    return pl.pallas_call(
        project_kernel,
        grid=(count // tile,),
        in_specs=[
            pl.BlockSpec((tile, width), lambda i: (i, 0)),
            pl.BlockSpec((1, width), lambda i: (0, 0)),
            pl.BlockSpec((columns, width), lambda i: (0, 0)),
        ],
        out_specs=[
            pl.BlockSpec((columns, tile), lambda i: (0, i)),
            pl.BlockSpec((tile, width), lambda i: (i, 0)),
        ],
        out_shape=[
            jax.ShapeDtypeStruct((columns, count), jnp.bfloat16),
            jax.ShapeDtypeStruct((count, width), jnp.bfloat16),
        ],
        compiler_params=pltpu.CompilerParams(vmem_limit_bytes=48 * 2**20),
        cost_estimate=cost(4 * count * width * columns),
    )(rows, gain, weights)


def gelu_parts(values):
    root = 0.7978845608028654
    square = values * values
    bend = jnp.tanh(root * values * (1.0 + 0.044715 * square))
    half = 0.5 + 0.5 * bend
    slope = half + half * (1.0 - bend) * values * (root + (3.0 * 0.044715 * root) * square)
    return values * half, slope


def expert_kernel(parts, pieces, *refs):
    row_refs, grad_refs, refs = refs[:pieces], refs[pieces : 2 * pieces], refs[2 * pieces :]
    first_refs, second_refs, refs = refs[:parts], refs[parts : 2 * parts], refs[2 * parts :]
    act_ref, pre_ref, xt_ref, lt_ref = refs[:4]
    res_refs, back_refs = refs[4 : 4 + pieces], refs[4 + pieces : 4 + 2 * pieces]
    rows, low, res_sum, back_sum, firsts, seconds, sems = refs[4 + 2 * pieces :]
    step = pl.program_id(0)
    capacity = grad_refs[0].shape[0]
    width = grad_refs[0].shape[1]
    count = pieces * capacity
    tile = min(count, 256)

    def fetch(j):
        copies = []
        for i in range(2):
            to = (j % 2, i)
            copies.append(pltpu.make_async_copy(first_refs[2 * j + i], firsts.at[to], sems.at[(0,) + to]))
            copies.append(pltpu.make_async_copy(second_refs[2 * j + i], seconds.at[to], sems.at[(1,) + to]))
        return copies

    @pl.when(step == 0)
    def _():
        for copy in fetch(0):
            copy.start()
        for e in range(pieces):
            span = pl.ds(e * capacity, capacity)
            rows[span, :] = row_refs[e][:capacity, :]
            gates = row_refs[e][capacity : capacity + 8, :capacity].astype(jnp.float32).T[:, 0:1]
            low[span, :] = (gates * grad_refs[e][...].astype(jnp.float32)).astype(jnp.bfloat16)
        res_sum[...] = jnp.zeros_like(res_sum)
        back_sum[...] = jnp.zeros_like(back_sum)

    for j in range(parts // 2):

        @pl.when(step == j)
        def _(j=j):
            if j + 1 < parts // 2:
                for copy in fetch(j + 1):
                    copy.start()
            for copy in fetch(j):
                copy.wait()

    @pl.when(step == 0)
    def _():
        xt_ref[...] = rows[...].T
        lt_ref[...] = low[...].T

    slot = step % 2
    spans = [pl.ds(start, tile) for start in range(0, count, tile)]
    chains = [(i, span) for span in spans for i in range(2)]
    values = [dot_nn(rows[span, :], firsts[slot, i]) for i, span in chains]
    grads = [dot_nt(low[span, :], seconds[slot, i]) for i, span in chains]
    for (i, span), value, grad in zip(chains, values, grads):
        active, slope = gelu_parts(value)
        active = active.astype(jnp.bfloat16)
        act_ref[i, span, :] = active
        res_sum[span, :] += dot_nn(active, seconds[slot, i])
        pre = (grad * slope).astype(jnp.bfloat16)
        pre_ref[i, span, :] = pre
        back_sum[span, :] += dot_nt(pre, firsts[slot, i])

    @pl.when(step == parts // 2 - 1)
    def _():
        for e in range(pieces):
            span = pl.ds(e * capacity, capacity)
            res_refs[e][...] = res_sum[span, :].astype(jnp.bfloat16)
            back_refs[e][:capacity, :] = back_sum[span, :].astype(jnp.bfloat16)
            sums = jnp.sum(
                res_sum[span, :] * grad_refs[e][...].astype(jnp.float32), axis=1, keepdims=True
            )
            sums = jnp.broadcast_to(sums, (capacity, 128)).T[0:8, :]
            high = sums.astype(jnp.bfloat16).astype(jnp.float32)
            index = lax.broadcasted_iota(jnp.int32, sums.shape, 0)
            pair = jnp.where(index == 0, high, jnp.where(index == 1, sums - high, 0.0))
            back_refs[e][capacity : capacity + 8, :] = jnp.zeros((8, width), jnp.bfloat16)
            back_refs[e][capacity : capacity + 8, :capacity] = pair.astype(jnp.bfloat16)


MINE = ((0, 4, 2, 6), (0, 2, 4, 6))
OTHER = ((1, 5, 3, 7), (1, 3, 5, 7))


def expert_apply(arrived, grads, firsts, seconds):
    pieces = len(grads)
    capacity, width = grads[0].shape
    count = pieces * capacity
    parts, hidden = len(firsts), firsts[0].shape[1]
    sent = pl.BlockSpec(arrived[0].shape, lambda i: (0, 0))
    whole = pl.BlockSpec((capacity, width), lambda i: (0, 0))
    kept = pl.BlockSpec((2, count, hidden), lambda i: (i, 0, 0))
    turned = pl.BlockSpec((width, count), lambda i: (0, 0))
    outs = pl.pallas_call(
        functools.partial(expert_kernel, parts, pieces),
        grid=(parts // 2,),
        in_specs=[sent] * pieces + [whole] * pieces + [pl.BlockSpec(memory_space=pl.ANY)] * (2 * parts),
        out_specs=[kept, kept, turned, turned] + [whole] * pieces + [sent] * pieces,
        out_shape=[
            jax.ShapeDtypeStruct((parts, count, hidden), jnp.bfloat16),
            jax.ShapeDtypeStruct((parts, count, hidden), jnp.bfloat16),
            jax.ShapeDtypeStruct((width, count), jnp.bfloat16),
            jax.ShapeDtypeStruct((width, count), jnp.bfloat16),
        ]
        + [jax.ShapeDtypeStruct((capacity, width), jnp.bfloat16)] * pieces
        + [jax.ShapeDtypeStruct(arrived[0].shape, jnp.bfloat16)] * pieces,
        scratch_shapes=[
            pltpu.VMEM((count, width), jnp.bfloat16),
            pltpu.VMEM((count, width), jnp.bfloat16),
            pltpu.VMEM((count, width), jnp.float32),
            pltpu.VMEM((count, width), jnp.float32),
            pltpu.VMEM((2, 2, width, hidden), jnp.bfloat16),
            pltpu.VMEM((2, 2, hidden, width), jnp.bfloat16),
            pltpu.SemaphoreType.DMA((2, 2, 2)),
        ],
        compiler_params=pltpu.CompilerParams(vmem_limit_bytes=52 * 2**20),
        cost_estimate=cost(12 * count * width * hidden * parts),
    )(*arrived, *grads, *firsts, *seconds)
    return list(outs[:4]), list(outs[4 : 4 + pieces]), list(outs[4 + pieces :])


def weight_kernel(groups, *refs):
    step = pl.program_id(0)
    outs = refs[4 * groups :]
    steps = pl.num_programs(0) // 2
    for out, (left, right) in enumerate(((2, 1), (3, 0))):
        total = 0.0
        for g in range(groups):
            total = total + dot_nn(refs[4 * g + left][...], refs[4 * g + right][0])
        total = total.astype(jnp.bfloat16)

        @pl.when(step < steps)
        def _():
            outs[out][0] = total

        @pl.when(step >= steps)
        def _():
            outs[2 + out][0] = total


def expert_weights(groups):
    chosen = [OTHER[i] + MINE[i] for i in range(2)]
    steps, hidden = len(chosen[0]), groups[0][0].shape[2]
    width = groups[0][2].shape[0]
    specs, arrays = [], []

    def pick(i, which):
        return sum(jnp.where(i == j, at, 0) for j, at in enumerate(chosen[which]))

    for act, pre, xt, lt in groups:
        block = (1,) + act.shape[1:]
        whole = pl.BlockSpec(xt.shape, lambda i: (0, 0))
        specs += [
            pl.BlockSpec(block, lambda i: (pick(i, 1), 0, 0)),
            pl.BlockSpec(block, lambda i: (pick(i, 0), 0, 0)),
            whole,
            whole,
        ]
        arrays += [act, pre, xt, lt]
    half = steps // 2
    early = pl.BlockSpec((1, width, hidden), lambda i: (jnp.minimum(i, half - 1), 0, 0))
    late = pl.BlockSpec((1, width, hidden), lambda i: (jnp.maximum(i - half, 0), 0, 0))
    count = sum(group[2].shape[1] for group in groups)
    return pl.pallas_call(
        functools.partial(weight_kernel, len(groups)),
        grid=(steps,),
        in_specs=specs,
        out_specs=[early, early, late, late],
        out_shape=[jax.ShapeDtypeStruct((half, width, hidden), jnp.bfloat16)] * 4,
        compiler_params=pltpu.CompilerParams(vmem_limit_bytes=50 * 2**20),
        cost_estimate=cost(6 * count * width * hidden * steps),
    )(*arrays)


def joined_kernel(rank_ref, grads_ref, normed_ref, weight_ref, gain_ref, wo_ref, table_ref, mine_ref, other_ref, main):
    blocks, columns, own = grads_ref.shape
    half = main.shape[0] // 2
    extra = mine_ref.shape[0] - half
    joined = 0.0
    for b in range(blocks):
        joined = joined + dot_nn(grads_ref[b], normed_ref[b * own : (b + 1) * own, :])
    main[:columns, :] = joined
    norm = jnp.sum(joined * weight_ref[...].astype(jnp.float32), axis=0, keepdims=True) / gain_ref[...]
    output = 0.0
    for b in range(blocks):
        output = output + wo_ref[b].astype(jnp.float32)
    end = columns + wo_ref.shape[1]
    main[columns:end, :] = output
    index = lax.broadcasted_iota(jnp.int32, (main.shape[0] - end, main.shape[1]), 0)
    main[end:, :] = jnp.where(index == 0, table_ref[...], 0.0)
    rank = rank_ref[0]
    index = lax.broadcasted_iota(jnp.int32, (extra, main.shape[1]), 0)
    norm = jnp.where(index == 0, norm, 0.0)
    mine_ref[:half, :] = main[pl.ds(pl.multiple_of(rank * half, 8), half), :]
    mine_ref[half:, :] = norm
    other = main[pl.ds(pl.multiple_of((1 - rank) * half, 8), half), :]
    other_ref[:half, :] = other.astype(jnp.bfloat16)
    other_ref[half:, :] = norm.astype(jnp.bfloat16)


def joined_halves(rank, grads, normed, weight, gain, wo, table, experts):
    width = normed.shape[1]
    rows = grads.shape[1] + wo.shape[1] + 1
    half = (rows + 31) // 32 * 16
    unit = max(16, experts)
    total = (half + unit) // unit * unit
    vmem = pl.BlockSpec(memory_space=pltpu.VMEM)
    return half, pl.pallas_call(
        joined_kernel,
        in_specs=[pl.BlockSpec(memory_space=pltpu.SMEM)] + [vmem] * 6,
        out_shape=[
            jax.ShapeDtypeStruct((total, width), jnp.float32),
            jax.ShapeDtypeStruct((total, width), jnp.bfloat16),
        ],
        scratch_shapes=[pltpu.VMEM((2 * half, width), jnp.float32)],
        compiler_params=pltpu.CompilerParams(vmem_limit_bytes=48 * 2**20),
        cost_estimate=cost(4 * rows * width * normed.shape[0]),
    )(rank, grads, normed, weight, gain, wo, table)


def halves_kernel(rank_ref, mine_ref, other_ref, query_ref, key_ref, value_ref, output_ref, rest_ref, main):
    half = main.shape[0] // 2
    rank = rank_ref[0]
    main[pl.ds(pl.multiple_of(rank * half, 8), half), :] = mine_ref[:half, :].astype(jnp.float32)
    main[pl.ds(pl.multiple_of((1 - rank) * half, 8), half), :] = other_ref[:half, :].astype(jnp.float32)
    start = 0
    for ref in (query_ref, key_ref, value_ref, output_ref, rest_ref):
        ref[...] = main[start : start + ref.shape[0], :]
        start += ref.shape[0]


def joined_whole(rank, mine, other, half, inner):
    width = mine.shape[1]
    vmem = pl.BlockSpec(memory_space=pltpu.VMEM)
    part = jax.ShapeDtypeStruct((inner, width), jnp.float32)
    return pl.pallas_call(
        halves_kernel,
        in_specs=[pl.BlockSpec(memory_space=pltpu.SMEM), vmem, vmem],
        out_shape=[part] * 4 + [jax.ShapeDtypeStruct((2 * half - 4 * inner, width), jnp.float32)],
        scratch_shapes=[pltpu.VMEM((2 * half, width), jnp.float32)],
        compiler_params=pltpu.CompilerParams(vmem_limit_bytes=48 * 2**20),
        cost_estimate=cost(1000 * half * width),
    )(rank, mine, other)


def both_kernel(rank_ref, mine_ref, other_ref, first_ref, second_ref):
    half = mine_ref.shape[2]
    rank = rank_ref[0]
    for place in range(2):

        @pl.when(rank == place)
        def _(place=place):
            for ref, at in ((mine_ref, place * half), (other_ref, (1 - place) * half)):
                first_ref[0, :, at : at + half] = ref[0].astype(jnp.float32)
                second_ref[0, at : at + half, :] = ref[1].astype(jnp.float32).T


def both_halves(rank, mine, other):
    _, width, half = mine.shape
    vmem = pl.BlockSpec(memory_space=pltpu.VMEM)
    return pl.pallas_call(
        both_kernel,
        in_specs=[pl.BlockSpec(memory_space=pltpu.SMEM), vmem, vmem],
        out_shape=[
            jax.ShapeDtypeStruct((1, width, 2 * half), jnp.float32),
            jax.ShapeDtypeStruct((1, 2 * half, width), jnp.float32),
        ],
        compiler_params=pltpu.CompilerParams(vmem_limit_bytes=48 * 2**20),
        cost_estimate=cost(1000 * half * width),
    )(rank, mine, other)


def inverse_rms(rows):
    return lax.rsqrt(jnp.mean(rows * rows, axis=-1, keepdims=True) + EPSILON)


def norm_backward(grad_normed, gain, normed_hat, inv_scale):
    scaled = grad_normed * gain
    return inv_scale * (scaled - normed_hat * jnp.mean(scaled * normed_hat, axis=-1, keepdims=True))


def swap(array, axis, offset):
    count = lax.axis_size(axis)
    return lax.ppermute(array, axis, [(i, i ^ offset) for i in range(count)])


def trade(array, axis):
    return lax.all_to_all(array, axis, 0, 0, tiled=True)


def low_sum(*arrays):
    return sum(array.astype(jnp.float32) for array in arrays).astype(jnp.bfloat16)


def spread(array, axis):
    return trade(jnp.broadcast_to(array[None], (lax.axis_size(axis),) + array.shape), axis)


def on_device(
    layer_input,
    cotangent,
    norm1_gain,
    w_query,
    w_key,
    w_value,
    w_output,
    bias_table,
    bucket,
    norm2_gain,
    router,
    expert_index,
    w_in,
    w_out,
):
    group_rows, width = layer_input.shape
    tensor_count = lax.axis_size("tensor")
    tensor_rank = lax.axis_index("tensor")
    dp_rank = lax.axis_index("dp")
    own_rows = group_rows // tensor_count
    own_start = tensor_rank * own_rows
    local_heads = bias_table.shape[1]
    inner = local_heads * HEAD_DIM
    experts = router.shape[1]
    capacity = 2 * own_rows // experts
    slots = experts * capacity

    half = w_in.shape[2] // 2
    first_mine = lax.dynamic_slice_in_dim(w_in[0], dp_rank * half, half, 1)
    first_other = lax.dynamic_slice_in_dim(w_in[0], (1 - dp_rank) * half, half, 1)
    second_mine = lax.dynamic_slice_in_dim(w_out[0], dp_rank * half, half, 0)
    second_other = lax.dynamic_slice_in_dim(w_out[0], (1 - dp_rank) * half, half, 0)
    w_joined = jnp.concatenate([w_query.T, w_key.T, w_value.T], axis=0)
    output_full = spread(w_output, "tensor")

    routes = lax.dynamic_slice_in_dim(expert_index[:, 0], own_start, own_rows, 0)
    own_hot = routes[:, None] == jnp.arange(experts, dtype=jnp.int32)[None, :]
    row_ids = jnp.arange(own_rows, dtype=jnp.int32)
    earlier = (row_ids[None, :] < row_ids[:, None]).astype(jnp.bfloat16)
    before = jnp.dot(earlier, own_hot.astype(jnp.bfloat16), preferred_element_type=jnp.float32)
    own_hot = own_hot.astype(jnp.float32)
    slot = jnp.sum(before * own_hot, axis=-1).astype(jnp.int32)
    flat = (routes ^ lax.axis_index("expert")) * capacity + slot
    cot_low = lax.dynamic_slice_in_dim(cotangent, own_start, own_rows, 0)
    place_hot, place_turned, grad_in = place_rows(flat, cot_low, experts, capacity)
    near = experts // 2
    far = near + experts // 4
    grad_in = [grad_in[0]] + [swap(grad_in[k], "expert", k) for k in range(1, far)] + grad_in[far:]

    gain_one = norm1_gain.astype(jnp.float32)
    projected, normed_one = project(layer_input, gain_one[None, :], w_joined, own_rows)
    high_bit = tensor_count // 2
    first_near = swap(first_mine, "tensor", 1)
    second_near = swap(second_mine, "tensor", high_bit)
    first_far = [swap(first_mine, "tensor", high_bit)]
    second_far = [swap(second_mine, "tensor", 1)]
    turned = jnp.concatenate([bucket[::-1], jnp.full((1,), -1, jnp.int32)])
    bucket_hot = jnp.arange(NUM_BUCKETS, dtype=jnp.int32)[:, None] == turned[None, :]
    vectors = dot_tn(bias_table, bucket_hot.astype(jnp.bfloat16))[:, None, :]
    mixed, logs = attend(projected, vectors, own_rows)
    mixed, output_full, first_near, second_near, first_far, second_far, grad_in[1:far] = (
        lax.optimization_barrier(
            (mixed, output_full, first_near, second_near, first_far, second_far, grad_in[1:far])
        )
    )
    output_full = output_full.reshape(tensor_count * inner, width)
    first_far.append(swap(first_near, "tensor", high_bit))
    second_far.append(swap(second_near, "tensor", 1))
    grad_in[far:] = [swap(grad_in[k], "expert", k) for k in range(far, experts)]
    mixed_own = trade(mixed.reshape(tensor_count, inner, own_rows), "tensor").reshape(
        tensor_count * inner, own_rows
    )

    input_own = lax.dynamic_slice_in_dim(layer_input, own_start, own_rows, 0)
    gain_two = norm2_gain.astype(jnp.float32)[None, :]
    router_turned = router.astype(jnp.float32).T
    hot_turned = own_hot.T
    residual, router_probs, gate, sent = send_rows(
        mixed_own, output_full, input_own, gain_two, router_turned, hot_turned, place_hot
    )
    sent, grad_in[far:] = lax.optimization_barrier((sent, grad_in[far:]))
    arrived = [sent[0]] + [swap(sent[k], "expert", k) for k in range(1, experts)]

    first_parts, second_parts = [first_mine, first_other], [second_mine, second_other]
    for first, second in ((first_near, second_far[0]), (first_far[0], second_near)):
        first_parts += [first, swap(first, "dp", 1)]
        second_parts += [second, swap(second, "dp", 1)]
    arrived[1:near], first, second = lax.optimization_barrier(
        (arrived[1:near], first_far[1], second_far[1])
    )
    first_parts += [first, swap(first, "dp", 1)]
    second_parts += [second, swap(second, "dp", 1)]
    arrived[:near], first_parts, second_parts, joined = lax.optimization_barrier(
        (arrived[:near], first_parts, second_parts, w_joined)
    )
    joined_parts = [w_joined] + [swap(joined, "tensor", k) for k in range(1, tensor_count - 1)]
    groups, results, back_got = [], [], []
    for low, high in ((0, near), (near, far), (far, experts)):
        pieces = arrived[low:high]
        if low == near:
            results, pieces, joined, joined_parts = lax.optimization_barrier(
                (results, pieces, joined, joined_parts)
            )
            joined_parts.append(swap(joined, "tensor", tensor_count - 1))
        if low == far:
            results, pieces = lax.optimization_barrier((results, pieces))
        kept, res, back = expert_apply(pieces, grad_in[low:high], first_parts, second_parts)
        groups.append(kept)
        results += res
        back_got += [
            back[k - low] if k == 0 else swap(back[k - low], "expert", k) for k in range(low, high)
        ]
    groups, joined_parts = lax.optimization_barrier((groups, joined_parts))
    first_other, second_other, first_sum, second_sum = expert_weights(groups)
    first_other, second_other, first_sum, second_sum, back_got = lax.optimization_barrier(
        (first_other, second_other, first_sum, second_sum, back_got)
    )
    first_other, second_other = swap(first_other, "dp", 1), swap(second_other, "dp", 1)

    grad_residual, grad_low, grad_heads, grad_router, grad_norm_two = receive_rows(
        residual,
        cot_low,
        gain_two,
        router_turned,
        hot_turned,
        router_probs,
        gate,
        place_hot,
        place_turned,
        output_full,
        back_got,
    )
    heads_got = trade(grad_heads.reshape(tensor_count, inner, own_rows), "tensor")
    grad_wo = dot_nn(mixed_own, grad_low).astype(jnp.bfloat16).reshape(tensor_count, inner, width)
    shared = jnp.concatenate([grad_router, grad_norm_two], axis=0).astype(jnp.bfloat16)
    shared = jnp.pad(shared, ((0, -shared.shape[0] % 8), (0, 0)))
    shared = jnp.broadcast_to(shared[None], (tensor_count,) + shared.shape)
    grad_wo = trade(jnp.concatenate([grad_wo, shared], axis=1), "tensor")
    _, *results = lax.optimization_barrier((grad_low, *results))
    returned = [results[0]] + [swap(results[k], "expert", k) for k in range(1, experts)]

    heads_got, first_other, second_other = lax.optimization_barrier(
        (heads_got, first_other, second_other)
    )
    first_got = swap(low_sum(first_sum[2:], first_other[2:]), "tensor", 1)
    second_got = swap(low_sum(second_sum[2:], second_other[2:]), "tensor", high_bit)
    head_shape = (tensor_count, local_heads, HEAD_DIM, own_rows)
    grad_projected, diagonals = attend_back(
        projected, vectors, mixed, heads_got.reshape(head_shape), logs
    )
    grad_projected = grad_projected.reshape(tensor_count, 3 * inner, own_rows)
    grad_projected, first_got, second_got, returned, grad_wo = lax.optimization_barrier(
        (grad_projected, first_got, second_got, returned, grad_wo)
    )

    grad_got = [lax.dynamic_index_in_dim(grad_projected, tensor_rank, 0, keepdims=False)]
    for k in range(1, tensor_count):
        sent = lax.dynamic_index_in_dim(grad_projected, tensor_rank ^ k, 0, keepdims=False)
        grad_got.append(swap(sent, "tensor", k))

    rank = dp_rank.reshape(1).astype(jnp.int32)
    grad_table = jnp.einsum(
        "br,hr->hb", bucket_hot.astype(jnp.float32), diagonals[:, 0], precision=HIGHEST
    ).reshape(-1)
    table_size = grad_table.shape[0]
    rows, (main_mine, main_other) = joined_halves(
        rank,
        grad_projected,
        normed_one,
        w_joined,
        gain_one[None, :],
        grad_wo,
        jnp.pad(grad_table, (0, width - table_size))[None],
        experts,
    )
    main_other, returned, first_got, second_got = lax.optimization_barrier(
        (swap(main_other, "dp", 1), returned, first_got, second_got)
    )
    main_mine = (main_mine + main_other.astype(jnp.float32)).astype(jnp.bfloat16)
    shares = trade(main_mine.reshape(experts, -1, width), "expert")

    first_pair = low_sum(first_sum[:2], first_other[:2], first_got)
    second_pair = low_sum(second_sum[:2], second_other[:2], second_got)
    first_got = swap(first_pair[1], "tensor", high_bit)
    second_got = swap(second_pair[1], "tensor", 1)
    output = residual + gate[0].astype(jnp.bfloat16).astype(jnp.float32)[:, None] * dot_nn(
        place_turned, jnp.concatenate(returned)
    )
    shares, grad_got, input_own = lax.optimization_barrier((shares, grad_got, input_own))
    main_mine = spread(low_sum(*shares), "expert").reshape(main_mine.shape)
    grad_normed_one = sum(dot_tn(got, part) for got, part in zip(grad_got, joined_parts))
    inv_own = inverse_rms(input_own)
    input_grad = grad_residual + norm_backward(grad_normed_one, gain_one, input_own * inv_own, inv_own)
    main_mine, first_got, second_got = lax.optimization_barrier((main_mine, first_got, second_got))
    pairs = ((first_pair, first_got), (second_pair, second_got))
    total = jnp.stack([low_sum(pair[0], got) for pair, got in pairs])
    grad_first, grad_second = both_halves(rank, total, swap(total, "dp", 1))
    norm_one = main_mine[rows].astype(jnp.float32)
    norm_one = norm_one + sum(swap(norm_one, "tensor", k) for k in range(1, tensor_count))
    grad_query, grad_key, grad_value, grad_output, shared = joined_whole(
        rank, main_mine, swap(main_mine, "dp", 1), rows, inner
    )

    return (
        output,
        input_grad,
        grad_query.T,
        grad_key.T,
        grad_value.T,
        grad_output,
        shared[grad_wo.shape[1] - inner, :table_size].reshape(local_heads, NUM_BUCKETS).T,
        norm_one,
        shared[experts],
        shared[:experts].T,
        grad_first,
        grad_second,
    )


def solution(mesh):
    return jax.shard_map(
        on_device,
        mesh=mesh,
        in_specs=(
            P(("dp", "expert"), None),
            P(("dp", "expert"), None),
            P(),
            P(None, "tensor"),
            P(None, "tensor"),
            P(None, "tensor"),
            P("tensor", None),
            P(None, "tensor"),
            P(),
            P(),
            P(),
            P(("dp", "expert"), None),
            P("expert", None, "tensor"),
            P("expert", "tensor", None),
        ),
        out_specs=(
            P(("dp", "expert", "tensor"), None),
            P(("dp", "expert", "tensor"), None),
            P(None, "tensor"),
            P(None, "tensor"),
            P(None, "tensor"),
            P("tensor", None),
            P(None, "tensor"),
            P(),
            P(),
            P(),
            P("expert", None, "tensor"),
            P("expert", "tensor", None),
        ),
        check_vma=False,
    )
```

```python
import functools
import jax
import jax.numpy as jnp
from jax import lax
from jax.sharding import PartitionSpec as P
from jax.experimental import pallas as pl
from jax.experimental.pallas import tpu as pltpu

HEAD_DIM = 64
NUM_BUCKETS = 32
EPSILON = 1e-06
HIGHEST = lax.Precision.HIGHEST
CHUNK = 512


def cost(work):
    return pl.CostEstimate(flops=work, bytes_accessed=work // 1024, transcendentals=0)

BAND = 128


def dot_nt(a, b):
    return lax.dot_general(a, b, (((1,), (1,)), ((), ())), preferred_element_type=jnp.float32)


def dot_nn(a, b):
    return lax.dot_general(a, b, (((1,), (0,)), ((), ())), preferred_element_type=jnp.float32)


def dot_tn(a, b):
    return lax.dot_general(a, b, (((0,), (0,)), ((), ())), preferred_element_type=jnp.float32)


def fill_band(band, vector):
    span = vector.shape[1]
    rows = jnp.broadcast_to(vector, (8, span))
    rows = pltpu.roll(rows, span - (BAND - 1), 1)
    index = lax.broadcasted_iota(jnp.int32, (8, span), 0)
    for step in (1, 2, 4):
        rows = jnp.where((index & step) != 0, pltpu.roll(rows, step, 1), rows)
    band[0:8, :] = rows
    step = 8
    while step < BAND:
        band[step : 2 * step, :] = pltpu.roll(band[0:step, :], step, 1)
        step *= 2


def fold_band(band):
    span = band.shape[1]
    step = BAND // 2
    while step >= 8:
        band[0:step, :] += pltpu.roll(band[step : 2 * step, :], span - step, 1)
        step //= 2
    rows = band[0:8, :]
    index = lax.broadcasted_iota(jnp.int32, (8, span), 0)
    for step in (1, 2, 4):
        rows = jnp.where((index & step) != 0, pltpu.roll(rows, span - step, 1), rows)
    total = jnp.sum(rows, axis=0, keepdims=True)
    return pltpu.roll(total, BAND - 1, 1)


def attend_kernel(q_ref, k_ref, v_ref, vec_ref, out_ref, log_ref, band):
    seq = k_ref.shape[3]
    own = out_ref.shape[3]

    @pl.when(pl.program_id(1) == 0)
    def _():
        fill_band(band, vec_ref[0])

    keys = k_ref[0, 0].T
    values = v_ref[0, 0]
    for start in range(0, seq, CHUNK):
        queries = q_ref[0, 0, :, start : start + CHUNK] * jnp.bfloat16(HEAD_DIM ** -0.5)
        raw = dot_nn(keys, queries)
        parts = []
        for low in range(0, seq, BAND):
            at = start - low + seq - BAND
            parts.append(raw[low : low + BAND] + band[:, at : at + CHUNK])
        peak = functools.reduce(jnp.maximum, parts)
        peak = jnp.max(peak, axis=0, keepdims=True)
        parts = [jnp.exp(part - peak) for part in parts]
        total = jnp.sum(functools.reduce(jnp.add, parts), axis=0, keepdims=True)
        weights = jnp.concatenate([part.astype(jnp.bfloat16) for part in parts], axis=0)
        mixed = dot_nn(values, weights) / total
        out_ref[start // own, 0, :, start % own : start % own + CHUNK] = mixed.astype(jnp.bfloat16)
        log_ref[0, 0, :, start : start + CHUNK] = peak + jnp.log(total)


def attend(projected, vectors, own):
    heads, seq = vectors.shape[0], vectors.shape[2] // 2
    seqs = projected.shape[1] // seq
    blocks = seq // own
    part = lambda p: pl.BlockSpec((1, 1, HEAD_DIM, seq), lambda h, s, p=p: (p, h, 0, s))
    proj = projected.reshape(3, heads, HEAD_DIM, seqs * seq)
    return pl.pallas_call(
        attend_kernel,
        grid=(heads, seqs),
        in_specs=[part(0), part(1), part(2), pl.BlockSpec((1, 1, 2 * seq), lambda h, s: (h, 0, 0))],
        out_specs=[
            pl.BlockSpec((blocks, 1, HEAD_DIM, own), lambda h, s: (s, h, 0, 0)),
            pl.BlockSpec((1, 1, 1, seq), lambda h, s: (h, s, 0, 0)),
        ],
        out_shape=[
            jax.ShapeDtypeStruct((seqs * blocks, heads, HEAD_DIM, own), jnp.bfloat16),
            jax.ShapeDtypeStruct((heads, seqs, 1, seq), jnp.float32),
        ],
        scratch_shapes=[pltpu.VMEM((BAND, 2 * seq), jnp.float32)],
        compiler_params=pltpu.CompilerParams(vmem_limit_bytes=48 * 2**20),
        cost_estimate=cost(16 * heads * seqs * seq * seq * HEAD_DIM),
    )(proj, proj, proj, vectors)


def attend_back_kernel(q_ref, k_ref, v_ref, o_ref, g_ref, log_ref, vec_ref, out_ref, diag_ref, band, fold, dk, dv):
    seq = k_ref.shape[3]
    own = out_ref.shape[4]
    scale = HEAD_DIM ** -0.5

    @pl.when(pl.program_id(1) == 0)
    def _():
        fill_band(band, vec_ref[0])
        fold[...] = jnp.zeros_like(fold)

    keys_t = k_ref[0, 0]
    keys = keys_t.T
    values = v_ref[0, 0].T
    for start in range(0, seq, CHUNK):
        block, inner = start // own, start % own
        queries = q_ref[0, 0, :, start : start + CHUNK] * jnp.bfloat16(scale)
        grads = g_ref[block, 0, :, inner : inner + CHUNK]
        mixed = o_ref[block, 0, :, inner : inner + CHUNK]
        delta = jnp.sum(grads.astype(jnp.float32) * mixed.astype(jnp.float32), axis=0, keepdims=True)
        logs = log_ref[0, 0, :, start : start + CHUNK]
        raw = dot_nn(keys, queries)
        grad_weights = dot_nn(values, grads)
        low_weights, low_scores = [], []
        for low in range(0, seq, BAND):
            at = start - low + seq - BAND
            weights = jnp.exp(raw[low : low + BAND] + band[:, at : at + CHUNK] - logs)
            scores = weights * (grad_weights[low : low + BAND] - delta)
            fold[:, at : at + CHUNK] += scores
            low_weights.append(weights.astype(jnp.bfloat16))
            low_scores.append(scores.astype(jnp.bfloat16))
        weights = jnp.concatenate(low_weights, axis=0)
        scores = jnp.concatenate(low_scores, axis=0)
        grad_q = dot_nn(keys_t, scores) * scale
        out_ref[block, 0, 0, :, inner : inner + CHUNK] = grad_q.astype(jnp.bfloat16)
        if start == 0:
            dk[...] = dot_nt(queries, scores)
            dv[...] = dot_nt(grads, weights)
        else:
            dk[...] += dot_nt(queries, scores)
            dv[...] += dot_nt(grads, weights)
    for block in range(seq // own):
        out_ref[block, 1, 0] = dk[:, block * own : (block + 1) * own].astype(jnp.bfloat16)
        out_ref[block, 2, 0] = dv[:, block * own : (block + 1) * own].astype(jnp.bfloat16)

    @pl.when(pl.program_id(1) == pl.num_programs(1) - 1)
    def _():
        diag_ref[0] = fold_band(fold)


def attend_back(projected, vectors, mixed, grads, logs):
    heads, seq = vectors.shape[0], vectors.shape[2] // 2
    seqs = projected.shape[1] // seq
    own = mixed.shape[3]
    blocks = seq // own
    part = lambda p: pl.BlockSpec((1, 1, HEAD_DIM, seq), lambda h, s, p=p: (p, h, 0, s))
    side = pl.BlockSpec((blocks, 1, HEAD_DIM, own), lambda h, s: (s, h, 0, 0))
    vec = pl.BlockSpec((1, 1, 2 * seq), lambda h, s: (h, 0, 0))
    proj = projected.reshape(3, heads, HEAD_DIM, seqs * seq)
    return pl.pallas_call(
        attend_back_kernel,
        grid=(heads, seqs),
        in_specs=[part(0), part(1), part(2), side, side,
                  pl.BlockSpec((1, 1, 1, seq), lambda h, s: (h, s, 0, 0)), vec],
        out_specs=[
            pl.BlockSpec((blocks, 3, 1, HEAD_DIM, own), lambda h, s: (s, 0, h, 0, 0)),
            vec,
        ],
        out_shape=[
            jax.ShapeDtypeStruct((seqs * blocks, 3, heads, HEAD_DIM, own), jnp.bfloat16),
            jax.ShapeDtypeStruct((heads, 1, 2 * seq), jnp.float32),
        ],
        scratch_shapes=[
            pltpu.VMEM((BAND, 2 * seq), jnp.float32),
            pltpu.VMEM((BAND, 2 * seq), jnp.float32),
            pltpu.VMEM((HEAD_DIM, seq), jnp.float32),
            pltpu.VMEM((HEAD_DIM, seq), jnp.float32),
        ],
        compiler_params=pltpu.CompilerParams(vmem_limit_bytes=48 * 2**20),
        cost_estimate=cost(32 * heads * seqs * seq * seq * HEAD_DIM),
    )(proj, proj, proj, mixed, grads, logs, vectors)


def dot_exact(a, b, axes):
    return lax.dot_general(
        a, b, ((axes[:1], axes[1:]), ((), ())), precision=HIGHEST, preferred_element_type=jnp.float32
    )


def place_kernel(capacity, row_ref, column_ref, rows_ref, place_ref, turned_ref, *piece_refs):
    flat = row_ref[...]
    column = column_ref[...]
    for k, ref in enumerate(piece_refs):
        span = slice(k * capacity, (k + 1) * capacity)
        index = lax.broadcasted_iota(jnp.int32, (capacity, flat.shape[1]), 0) + k * capacity
        hot = (index == flat).astype(jnp.bfloat16)
        place_ref[span, :] = hot
        ref[...] = dot_nn(hot, rows_ref[...]).astype(jnp.bfloat16)
    index = lax.broadcasted_iota(jnp.int32, turned_ref.shape, 1)
    turned_ref[...] = (index == column).astype(jnp.bfloat16)


def place_rows(flat, rows, pieces, capacity):
    count, width = rows.shape
    outs = pl.pallas_call(
        functools.partial(place_kernel, capacity),
        out_shape=[
            jax.ShapeDtypeStruct((pieces * capacity, count), jnp.bfloat16),
            jax.ShapeDtypeStruct((count, pieces * capacity), jnp.bfloat16),
        ]
        + [jax.ShapeDtypeStruct((capacity, width), jnp.bfloat16)] * pieces,
        compiler_params=pltpu.CompilerParams(vmem_limit_bytes=48 * 2**20),
        cost_estimate=cost(2 * pieces * capacity * count * width),
    )(flat[None, :], flat[:, None], rows)
    return outs[0], outs[1], list(outs[2:])


def second_norm(rows, gain):
    scale = lax.rsqrt(jnp.mean(rows * rows, axis=-1, keepdims=True) + EPSILON)
    hat = rows * scale
    return scale, hat, hat * gain


def send_kernel(capacity, mixed_ref, weight_ref, rows_ref, gain_ref, router_ref, hot_ref, place_ref, *refs):
    residual_ref, probs_ref, gate_ref = refs[:3]
    residual = rows_ref[...] + dot_tn(mixed_ref[...], weight_ref[...])
    residual_ref[...] = residual
    _, _, normed = second_norm(residual, gain_ref[...])
    logits = dot_exact(router_ref[...], normed, (1, 1))
    logits = jnp.exp(logits - jnp.max(logits, axis=0, keepdims=True))
    probs = logits / jnp.sum(logits, axis=0, keepdims=True)
    probs_ref[...] = probs
    gate = jnp.sum(probs * hot_ref[...], axis=0, keepdims=True)
    gate_ref[...] = gate
    low = normed.astype(jnp.bfloat16)
    gates = jnp.broadcast_to(gate.astype(jnp.bfloat16), (8, gate.shape[1]))
    for k, ref in enumerate(refs[3:]):
        place = place_ref[k * capacity : (k + 1) * capacity, :]
        ref[:capacity, :] = dot_nn(place, low).astype(jnp.bfloat16)
        ref[capacity : capacity + 8, :] = jnp.zeros((8, ref.shape[1]), jnp.bfloat16)
        ref[capacity : capacity + 8, :capacity] = dot_nt(gates, place).astype(jnp.bfloat16)


def send_rows(mixed, weight, rows, gain, router, hot, place):
    experts, count = hot.shape
    width = rows.shape[1]
    capacity = place.shape[0] // experts
    outs = pl.pallas_call(
        functools.partial(send_kernel, capacity),
        out_shape=[
            jax.ShapeDtypeStruct((count, width), jnp.float32),
            jax.ShapeDtypeStruct((experts, count), jnp.float32),
            jax.ShapeDtypeStruct((1, count), jnp.float32),
        ]
        + [jax.ShapeDtypeStruct((capacity + 8, width), jnp.bfloat16)] * experts,
        compiler_params=pltpu.CompilerParams(vmem_limit_bytes=48 * 2**20),
        cost_estimate=cost(6 * width * count * width),
    )(mixed, weight, rows, gain, router, hot, place)
    return outs[0], outs[1], outs[2], list(outs[3:])


def receive_kernel(capacity, residual_ref, cot_ref, gain_ref, router_ref, hot_ref, probs_ref, gate_ref, place_ref, turned_ref, weight_ref, *refs):
    backs, (grad_ref, low_ref, heads_ref, router_grad_ref, gain_grad_ref) = refs[:-5], refs[-5:]
    scale, hat, normed = second_norm(residual_ref[...], gain_ref[...])
    grad, pair = 0.0, 0.0
    for k, ref in enumerate(backs):
        span = slice(k * capacity, (k + 1) * capacity)
        grad = grad + dot_nn(turned_ref[:, span], ref[:capacity, :])
        pair = pair + dot_nn(ref[capacity : capacity + 8, :capacity], place_ref[span, :])
    grad_gate = jnp.sum(pair, axis=0, keepdims=True)
    grad_logits = probs_ref[...] * (hot_ref[...] - gate_ref[...]) * grad_gate
    router_grad_ref[...] = dot_exact(grad_logits, normed, (1, 0))
    grad = grad + dot_exact(grad_logits, router_ref[...], (0, 0))
    gain_grad_ref[...] = jnp.sum(grad * hat, axis=0, keepdims=True)
    scaled = grad * gain_ref[...]
    grad = scale * (scaled - hat * jnp.mean(scaled * hat, axis=-1, keepdims=True))
    grad = grad + cot_ref[...].astype(jnp.float32)
    grad_ref[...] = grad
    low = grad.astype(jnp.bfloat16)
    low_ref[...] = low
    heads_ref[...] = dot_nt(weight_ref[...], low).astype(jnp.bfloat16)


def receive_rows(residual, cot, gain, router, hot, probs, gate, place, turned, weight, backs):
    experts, count = hot.shape
    width = residual.shape[1]
    return pl.pallas_call(
        functools.partial(receive_kernel, place.shape[0] // experts),
        out_shape=[
            jax.ShapeDtypeStruct((count, width), jnp.float32),
            jax.ShapeDtypeStruct((count, width), jnp.bfloat16),
            jax.ShapeDtypeStruct((weight.shape[0], count), jnp.bfloat16),
            jax.ShapeDtypeStruct((experts, width), jnp.float32),
            jax.ShapeDtypeStruct((1, width), jnp.float32),
        ],
        compiler_params=pltpu.CompilerParams(vmem_limit_bytes=48 * 2**20),
        cost_estimate=cost(6 * width * count * width),
    )(residual, cot, gain, router, hot, probs, gate, place, turned, weight, *backs)


def project_kernel(x_ref, gain_ref, weight_ref, out_ref, normed_ref):
    rows = x_ref[...]
    scale = lax.rsqrt(jnp.mean(rows * rows, axis=-1, keepdims=True) + EPSILON)
    normed = (rows * scale * gain_ref[...]).astype(jnp.bfloat16)
    normed_ref[...] = normed
    out_ref[...] = dot_nt(weight_ref[...], normed).astype(jnp.bfloat16)


def project(rows, gain, weights, tile):
    count, width = rows.shape
    columns = weights.shape[0]
    return pl.pallas_call(
        project_kernel,
        grid=(count // tile,),
        in_specs=[
            pl.BlockSpec((tile, width), lambda i: (i, 0)),
            pl.BlockSpec((1, width), lambda i: (0, 0)),
            pl.BlockSpec((columns, width), lambda i: (0, 0)),
        ],
        out_specs=[
            pl.BlockSpec((columns, tile), lambda i: (0, i)),
            pl.BlockSpec((tile, width), lambda i: (i, 0)),
        ],
        out_shape=[
            jax.ShapeDtypeStruct((columns, count), jnp.bfloat16),
            jax.ShapeDtypeStruct((count, width), jnp.bfloat16),
        ],
        compiler_params=pltpu.CompilerParams(vmem_limit_bytes=48 * 2**20),
        cost_estimate=cost(4 * count * width * columns),
    )(rows, gain, weights)


def gelu_parts(values):
    root = 0.7978845608028654
    square = values * values
    bend = jnp.tanh(root * values * (1.0 + 0.044715 * square))
    half = 0.5 + 0.5 * bend
    slope = half + half * (1.0 - bend) * values * (root + (3.0 * 0.044715 * root) * square)
    return values * half, slope


def expert_kernel(parts, pieces, *refs):
    row_refs, grad_refs, refs = refs[:pieces], refs[pieces : 2 * pieces], refs[2 * pieces :]
    first_refs, second_refs, refs = refs[:parts], refs[parts : 2 * parts], refs[2 * parts :]
    act_ref, pre_ref, xt_ref, lt_ref = refs[:4]
    res_refs, back_refs = refs[4 : 4 + pieces], refs[4 + pieces : 4 + 2 * pieces]
    rows, low, res_sum, back_sum, firsts, seconds, sems = refs[4 + 2 * pieces :]
    step = pl.program_id(0)
    capacity = grad_refs[0].shape[0]
    width = grad_refs[0].shape[1]
    count = pieces * capacity
    tile = min(count, 256)

    def fetch(j):
        copies = []
        for i in range(2):
            to = (j % 2, i)
            copies.append(pltpu.make_async_copy(first_refs[2 * j + i], firsts.at[to], sems.at[(0,) + to]))
            copies.append(pltpu.make_async_copy(second_refs[2 * j + i], seconds.at[to], sems.at[(1,) + to]))
        return copies

    @pl.when(step == 0)
    def _():
        for copy in fetch(0):
            copy.start()
        for e in range(pieces):
            span = pl.ds(e * capacity, capacity)
            rows[span, :] = row_refs[e][:capacity, :]
            gates = row_refs[e][capacity : capacity + 8, :capacity].astype(jnp.float32).T[:, 0:1]
            low[span, :] = (gates * grad_refs[e][...].astype(jnp.float32)).astype(jnp.bfloat16)
        res_sum[...] = jnp.zeros_like(res_sum)
        back_sum[...] = jnp.zeros_like(back_sum)

    for j in range(parts // 2):

        @pl.when(step == j)
        def _(j=j):
            if j + 1 < parts // 2:
                for copy in fetch(j + 1):
                    copy.start()
            for copy in fetch(j):
                copy.wait()

    @pl.when(step == 0)
    def _():
        xt_ref[...] = rows[...].T
        lt_ref[...] = low[...].T

    slot = step % 2
    spans = [pl.ds(start, tile) for start in range(0, count, tile)]
    chains = [(i, span) for span in spans for i in range(2)]
    values = [dot_nn(rows[span, :], firsts[slot, i]) for i, span in chains]
    grads = [dot_nt(low[span, :], seconds[slot, i]) for i, span in chains]
    for (i, span), value, grad in zip(chains, values, grads):
        active, slope = gelu_parts(value)
        active = active.astype(jnp.bfloat16)
        act_ref[i, span, :] = active
        res_sum[span, :] += dot_nn(active, seconds[slot, i])
        pre = (grad * slope).astype(jnp.bfloat16)
        pre_ref[i, span, :] = pre
        back_sum[span, :] += dot_nt(pre, firsts[slot, i])

    @pl.when(step == parts // 2 - 1)
    def _():
        for e in range(pieces):
            span = pl.ds(e * capacity, capacity)
            res_refs[e][...] = res_sum[span, :].astype(jnp.bfloat16)
            back_refs[e][:capacity, :] = back_sum[span, :].astype(jnp.bfloat16)
            sums = jnp.sum(
                res_sum[span, :] * grad_refs[e][...].astype(jnp.float32), axis=1, keepdims=True
            )
            sums = jnp.broadcast_to(sums, (capacity, 128)).T[0:8, :]
            high = sums.astype(jnp.bfloat16).astype(jnp.float32)
            index = lax.broadcasted_iota(jnp.int32, sums.shape, 0)
            pair = jnp.where(index == 0, high, jnp.where(index == 1, sums - high, 0.0))
            back_refs[e][capacity : capacity + 8, :] = jnp.zeros((8, width), jnp.bfloat16)
            back_refs[e][capacity : capacity + 8, :capacity] = pair.astype(jnp.bfloat16)


MINE = ((0, 4, 2, 6), (0, 2, 4, 6))
OTHER = ((1, 5, 3, 7), (1, 3, 5, 7))


def expert_apply(arrived, grads, firsts, seconds):
    pieces = len(grads)
    capacity, width = grads[0].shape
    count = pieces * capacity
    parts, hidden = len(firsts), firsts[0].shape[1]
    sent = pl.BlockSpec(arrived[0].shape, lambda i: (0, 0))
    whole = pl.BlockSpec((capacity, width), lambda i: (0, 0))
    kept = pl.BlockSpec((2, count, hidden), lambda i: (i, 0, 0))
    turned = pl.BlockSpec((width, count), lambda i: (0, 0))
    outs = pl.pallas_call(
        functools.partial(expert_kernel, parts, pieces),
        grid=(parts // 2,),
        in_specs=[sent] * pieces + [whole] * pieces + [pl.BlockSpec(memory_space=pl.ANY)] * (2 * parts),
        out_specs=[kept, kept, turned, turned] + [whole] * pieces + [sent] * pieces,
        out_shape=[
            jax.ShapeDtypeStruct((parts, count, hidden), jnp.bfloat16),
            jax.ShapeDtypeStruct((parts, count, hidden), jnp.bfloat16),
            jax.ShapeDtypeStruct((width, count), jnp.bfloat16),
            jax.ShapeDtypeStruct((width, count), jnp.bfloat16),
        ]
        + [jax.ShapeDtypeStruct((capacity, width), jnp.bfloat16)] * pieces
        + [jax.ShapeDtypeStruct(arrived[0].shape, jnp.bfloat16)] * pieces,
        scratch_shapes=[
            pltpu.VMEM((count, width), jnp.bfloat16),
            pltpu.VMEM((count, width), jnp.bfloat16),
            pltpu.VMEM((count, width), jnp.float32),
            pltpu.VMEM((count, width), jnp.float32),
            pltpu.VMEM((2, 2, width, hidden), jnp.bfloat16),
            pltpu.VMEM((2, 2, hidden, width), jnp.bfloat16),
            pltpu.SemaphoreType.DMA((2, 2, 2)),
        ],
        compiler_params=pltpu.CompilerParams(vmem_limit_bytes=52 * 2**20),
        cost_estimate=cost(12 * count * width * hidden * parts),
    )(*arrived, *grads, *firsts, *seconds)
    return list(outs[:4]), list(outs[4 : 4 + pieces]), list(outs[4 + pieces :])


def weight_kernel(groups, *refs):
    step = pl.program_id(0)
    outs = refs[4 * groups :]
    steps = pl.num_programs(0) // 2
    for out, (left, right) in enumerate(((2, 1), (3, 0))):
        total = 0.0
        for g in range(groups):
            total = total + dot_nn(refs[4 * g + left][...], refs[4 * g + right][0])
        total = total.astype(jnp.bfloat16)

        @pl.when(step < steps)
        def _():
            outs[out][0] = total

        @pl.when(step >= steps)
        def _():
            outs[2 + out][0] = total


def expert_weights(groups):
    chosen = [OTHER[i] + MINE[i] for i in range(2)]
    steps, hidden = len(chosen[0]), groups[0][0].shape[2]
    width = groups[0][2].shape[0]
    specs, arrays = [], []

    def pick(i, which):
        return sum(jnp.where(i == j, at, 0) for j, at in enumerate(chosen[which]))

    for act, pre, xt, lt in groups:
        block = (1,) + act.shape[1:]
        whole = pl.BlockSpec(xt.shape, lambda i: (0, 0))
        specs += [
            pl.BlockSpec(block, lambda i: (pick(i, 1), 0, 0)),
            pl.BlockSpec(block, lambda i: (pick(i, 0), 0, 0)),
            whole,
            whole,
        ]
        arrays += [act, pre, xt, lt]
    half = steps // 2
    early = pl.BlockSpec((1, width, hidden), lambda i: (jnp.minimum(i, half - 1), 0, 0))
    late = pl.BlockSpec((1, width, hidden), lambda i: (jnp.maximum(i - half, 0), 0, 0))
    count = sum(group[2].shape[1] for group in groups)
    return pl.pallas_call(
        functools.partial(weight_kernel, len(groups)),
        grid=(steps,),
        in_specs=specs,
        out_specs=[early, early, late, late],
        out_shape=[jax.ShapeDtypeStruct((half, width, hidden), jnp.bfloat16)] * 4,
        compiler_params=pltpu.CompilerParams(vmem_limit_bytes=50 * 2**20),
        cost_estimate=cost(6 * count * width * hidden * steps),
    )(*arrays)


def joined_kernel(rank_ref, grads_ref, normed_ref, weight_ref, gain_ref, wo_ref, table_ref, mine_ref, other_ref, main):
    blocks, columns, own = grads_ref.shape
    half = main.shape[0] // 2
    extra = mine_ref.shape[0] - half
    joined = 0.0
    for b in range(blocks):
        joined = joined + dot_nn(grads_ref[b], normed_ref[b * own : (b + 1) * own, :])
    main[:columns, :] = joined
    norm = jnp.sum(joined * weight_ref[...].astype(jnp.float32), axis=0, keepdims=True) / gain_ref[...]
    output = 0.0
    for b in range(blocks):
        output = output + wo_ref[b].astype(jnp.float32)
    end = columns + wo_ref.shape[1]
    main[columns:end, :] = output
    index = lax.broadcasted_iota(jnp.int32, (main.shape[0] - end, main.shape[1]), 0)
    main[end:, :] = jnp.where(index == 0, table_ref[...], 0.0)
    rank = rank_ref[0]
    index = lax.broadcasted_iota(jnp.int32, (extra, main.shape[1]), 0)
    norm = jnp.where(index == 0, norm, 0.0)
    mine_ref[:half, :] = main[pl.ds(pl.multiple_of(rank * half, 8), half), :]
    mine_ref[half:, :] = norm
    other = main[pl.ds(pl.multiple_of((1 - rank) * half, 8), half), :]
    other_ref[:half, :] = other.astype(jnp.bfloat16)
    other_ref[half:, :] = norm.astype(jnp.bfloat16)


def joined_halves(rank, grads, normed, weight, gain, wo, table, experts):
    width = normed.shape[1]
    rows = grads.shape[1] + wo.shape[1] + 1
    half = (rows + 31) // 32 * 16
    unit = max(16, experts)
    total = (half + unit) // unit * unit
    vmem = pl.BlockSpec(memory_space=pltpu.VMEM)
    return half, pl.pallas_call(
        joined_kernel,
        in_specs=[pl.BlockSpec(memory_space=pltpu.SMEM)] + [vmem] * 6,
        out_shape=[
            jax.ShapeDtypeStruct((total, width), jnp.float32),
            jax.ShapeDtypeStruct((total, width), jnp.bfloat16),
        ],
        scratch_shapes=[pltpu.VMEM((2 * half, width), jnp.float32)],
        compiler_params=pltpu.CompilerParams(vmem_limit_bytes=48 * 2**20),
        cost_estimate=cost(4 * rows * width * normed.shape[0]),
    )(rank, grads, normed, weight, gain, wo, table)


def halves_kernel(rank_ref, mine_ref, other_ref, query_ref, key_ref, value_ref, output_ref, rest_ref, main):
    half = main.shape[0] // 2
    rank = rank_ref[0]
    main[pl.ds(pl.multiple_of(rank * half, 8), half), :] = mine_ref[:half, :].astype(jnp.float32)
    main[pl.ds(pl.multiple_of((1 - rank) * half, 8), half), :] = other_ref[:half, :].astype(jnp.float32)
    start = 0
    for ref in (query_ref, key_ref, value_ref, output_ref, rest_ref):
        ref[...] = main[start : start + ref.shape[0], :]
        start += ref.shape[0]


def joined_whole(rank, mine, other, half, inner):
    width = mine.shape[1]
    vmem = pl.BlockSpec(memory_space=pltpu.VMEM)
    part = jax.ShapeDtypeStruct((inner, width), jnp.float32)
    return pl.pallas_call(
        halves_kernel,
        in_specs=[pl.BlockSpec(memory_space=pltpu.SMEM), vmem, vmem],
        out_shape=[part] * 4 + [jax.ShapeDtypeStruct((2 * half - 4 * inner, width), jnp.float32)],
        scratch_shapes=[pltpu.VMEM((2 * half, width), jnp.float32)],
        compiler_params=pltpu.CompilerParams(vmem_limit_bytes=48 * 2**20),
        cost_estimate=cost(1000 * half * width),
    )(rank, mine, other)


def both_kernel(rank_ref, mine_ref, other_ref, first_ref, second_ref):
    half = mine_ref.shape[2]
    rank = rank_ref[0]
    for place in range(2):

        @pl.when(rank == place)
        def _(place=place):
            for ref, at in ((mine_ref, place * half), (other_ref, (1 - place) * half)):
                first_ref[0, :, at : at + half] = ref[0].astype(jnp.float32)
                second_ref[0, at : at + half, :] = ref[1].astype(jnp.float32).T


def both_halves(rank, mine, other):
    _, width, half = mine.shape
    vmem = pl.BlockSpec(memory_space=pltpu.VMEM)
    return pl.pallas_call(
        both_kernel,
        in_specs=[pl.BlockSpec(memory_space=pltpu.SMEM), vmem, vmem],
        out_shape=[
            jax.ShapeDtypeStruct((1, width, 2 * half), jnp.float32),
            jax.ShapeDtypeStruct((1, 2 * half, width), jnp.float32),
        ],
        compiler_params=pltpu.CompilerParams(vmem_limit_bytes=48 * 2**20),
        cost_estimate=cost(1000 * half * width),
    )(rank, mine, other)


def inverse_rms(rows):
    return lax.rsqrt(jnp.mean(rows * rows, axis=-1, keepdims=True) + EPSILON)


def norm_backward(grad_normed, gain, normed_hat, inv_scale):
    scaled = grad_normed * gain
    return inv_scale * (scaled - normed_hat * jnp.mean(scaled * normed_hat, axis=-1, keepdims=True))


def swap(array, axis, offset):
    count = lax.axis_size(axis)
    return lax.ppermute(array, axis, [(i, i ^ offset) for i in range(count)])


def trade(array, axis):
    return lax.all_to_all(array, axis, 0, 0, tiled=True)


def low_sum(*arrays):
    return sum(array.astype(jnp.float32) for array in arrays).astype(jnp.bfloat16)


def spread(array, axis):
    return trade(jnp.broadcast_to(array[None], (lax.axis_size(axis),) + array.shape), axis)


def on_device(
    layer_input,
    cotangent,
    norm1_gain,
    w_query,
    w_key,
    w_value,
    w_output,
    bias_table,
    bucket,
    norm2_gain,
    router,
    expert_index,
    w_in,
    w_out,
):
    group_rows, width = layer_input.shape
    tensor_count = lax.axis_size("tensor")
    tensor_rank = lax.axis_index("tensor")
    dp_rank = lax.axis_index("dp")
    own_rows = group_rows // tensor_count
    own_start = tensor_rank * own_rows
    local_heads = bias_table.shape[1]
    inner = local_heads * HEAD_DIM
    experts = router.shape[1]
    capacity = 2 * own_rows // experts
    slots = experts * capacity

    half = w_in.shape[2] // 2
    first_mine = lax.dynamic_slice_in_dim(w_in[0], dp_rank * half, half, 1)
    first_other = lax.dynamic_slice_in_dim(w_in[0], (1 - dp_rank) * half, half, 1)
    second_mine = lax.dynamic_slice_in_dim(w_out[0], dp_rank * half, half, 0)
    second_other = lax.dynamic_slice_in_dim(w_out[0], (1 - dp_rank) * half, half, 0)
    w_joined = jnp.concatenate([w_query.T, w_key.T, w_value.T], axis=0)
    output_full = spread(w_output, "tensor")

    routes = lax.dynamic_slice_in_dim(expert_index[:, 0], own_start, own_rows, 0)
    own_hot = routes[:, None] == jnp.arange(experts, dtype=jnp.int32)[None, :]
    row_ids = jnp.arange(own_rows, dtype=jnp.int32)
    earlier = (row_ids[None, :] < row_ids[:, None]).astype(jnp.bfloat16)
    before = jnp.dot(earlier, own_hot.astype(jnp.bfloat16), preferred_element_type=jnp.float32)
    own_hot = own_hot.astype(jnp.float32)
    slot = jnp.sum(before * own_hot, axis=-1).astype(jnp.int32)
    flat = (routes ^ lax.axis_index("expert")) * capacity + slot
    cot_low = lax.dynamic_slice_in_dim(cotangent, own_start, own_rows, 0)
    place_hot, place_turned, grad_in = place_rows(flat, cot_low, experts, capacity)
    near = experts // 2
    far = near + experts // 4
    grad_in = [grad_in[0]] + [swap(grad_in[k], "expert", k) for k in range(1, far)] + grad_in[far:]

    gain_one = norm1_gain.astype(jnp.float32)
    projected, normed_one = project(layer_input, gain_one[None, :], w_joined, own_rows)
    high_bit = tensor_count // 2
    first_near = swap(first_mine, "tensor", 1)
    second_near = swap(second_mine, "tensor", high_bit)
    first_far = [swap(first_mine, "tensor", high_bit)]
    second_far = [swap(second_mine, "tensor", 1)]
    turned = jnp.concatenate([bucket[::-1], jnp.full((1,), -1, jnp.int32)])
    bucket_hot = jnp.arange(NUM_BUCKETS, dtype=jnp.int32)[:, None] == turned[None, :]
    vectors = dot_tn(bias_table, bucket_hot.astype(jnp.bfloat16))[:, None, :]
    mixed, logs = attend(projected, vectors, own_rows)
    mixed, output_full, first_near, second_near, first_far, second_far, grad_in[1:far] = (
        lax.optimization_barrier(
            (mixed, output_full, first_near, second_near, first_far, second_far, grad_in[1:far])
        )
    )
    output_full = output_full.reshape(tensor_count * inner, width)
    first_far.append(swap(first_near, "tensor", high_bit))
    second_far.append(swap(second_near, "tensor", 1))
    grad_in[far:] = [swap(grad_in[k], "expert", k) for k in range(far, experts)]
    mixed_own = trade(mixed.reshape(tensor_count, inner, own_rows), "tensor").reshape(
        tensor_count * inner, own_rows
    )

    input_own = lax.dynamic_slice_in_dim(layer_input, own_start, own_rows, 0)
    gain_two = norm2_gain.astype(jnp.float32)[None, :]
    router_turned = router.astype(jnp.float32).T
    hot_turned = own_hot.T
    residual, router_probs, gate, sent = send_rows(
        mixed_own, output_full, input_own, gain_two, router_turned, hot_turned, place_hot
    )
    sent, grad_in[far:] = lax.optimization_barrier((sent, grad_in[far:]))
    arrived = [sent[0]] + [swap(sent[k], "expert", k) for k in range(1, experts)]

    first_parts, second_parts = [first_mine, first_other], [second_mine, second_other]
    for first, second in ((first_near, second_far[0]), (first_far[0], second_near)):
        first_parts += [first, swap(first, "dp", 1)]
        second_parts += [second, swap(second, "dp", 1)]
    arrived[1:near], first, second = lax.optimization_barrier(
        (arrived[1:near], first_far[1], second_far[1])
    )
    first_parts += [first, swap(first, "dp", 1)]
    second_parts += [second, swap(second, "dp", 1)]
    arrived[:near], first_parts, second_parts, joined = lax.optimization_barrier(
        (arrived[:near], first_parts, second_parts, w_joined)
    )
    joined_parts = [w_joined] + [swap(joined, "tensor", k) for k in range(1, tensor_count - 1)]
    groups, results, back_got = [], [], []
    for low, high in ((0, near), (near, far), (far, experts)):
        pieces = arrived[low:high]
        if low == near:
            results, pieces, joined, joined_parts = lax.optimization_barrier(
                (results, pieces, joined, joined_parts)
            )
            joined_parts.append(swap(joined, "tensor", tensor_count - 1))
        if low == far:
            results, pieces = lax.optimization_barrier((results, pieces))
        kept, res, back = expert_apply(pieces, grad_in[low:high], first_parts, second_parts)
        groups.append(kept)
        results += res
        back_got += [
            back[k - low] if k == 0 else swap(back[k - low], "expert", k) for k in range(low, high)
        ]
    groups, joined_parts = lax.optimization_barrier((groups, joined_parts))
    first_other, second_other, first_sum, second_sum = expert_weights(groups)
    first_other, second_other, first_sum, second_sum, back_got = lax.optimization_barrier(
        (first_other, second_other, first_sum, second_sum, back_got)
    )
    first_other, second_other = swap(first_other, "dp", 1), swap(second_other, "dp", 1)

    grad_residual, grad_low, grad_heads, grad_router, grad_norm_two = receive_rows(
        residual,
        cot_low,
        gain_two,
        router_turned,
        hot_turned,
        router_probs,
        gate,
        place_hot,
        place_turned,
        output_full,
        back_got,
    )
    heads_got = trade(grad_heads.reshape(tensor_count, inner, own_rows), "tensor")
    grad_wo = dot_nn(mixed_own, grad_low).astype(jnp.bfloat16).reshape(tensor_count, inner, width)
    shared = jnp.concatenate([grad_router, grad_norm_two], axis=0).astype(jnp.bfloat16)
    shared = jnp.pad(shared, ((0, -shared.shape[0] % 8), (0, 0)))
    shared = jnp.broadcast_to(shared[None], (tensor_count,) + shared.shape)
    grad_wo = trade(jnp.concatenate([grad_wo, shared], axis=1), "tensor")
    _, *results = lax.optimization_barrier((grad_low, *results))
    returned = [results[0]] + [swap(results[k], "expert", k) for k in range(1, experts)]

    heads_got, first_other, second_other = lax.optimization_barrier(
        (heads_got, first_other, second_other)
    )
    first_got = swap(low_sum(first_sum[2:], first_other[2:]), "tensor", 1)
    second_got = swap(low_sum(second_sum[2:], second_other[2:]), "tensor", high_bit)
    head_shape = (tensor_count, local_heads, HEAD_DIM, own_rows)
    grad_projected, diagonals = attend_back(
        projected, vectors, mixed, heads_got.reshape(head_shape), logs
    )
    grad_projected = grad_projected.reshape(tensor_count, 3 * inner, own_rows)
    grad_projected, first_got, second_got, returned, grad_wo = lax.optimization_barrier(
        (grad_projected, first_got, second_got, returned, grad_wo)
    )

    grad_got = [lax.dynamic_index_in_dim(grad_projected, tensor_rank, 0, keepdims=False)]
    for k in range(1, tensor_count):
        sent = lax.dynamic_index_in_dim(grad_projected, tensor_rank ^ k, 0, keepdims=False)
        grad_got.append(swap(sent, "tensor", k))

    rank = dp_rank.reshape(1).astype(jnp.int32)
    grad_table = jnp.einsum(
        "br,hr->hb", bucket_hot.astype(jnp.float32), diagonals[:, 0], precision=HIGHEST
    ).reshape(-1)
    table_size = grad_table.shape[0]
    rows, (main_mine, main_other) = joined_halves(
        rank,
        grad_projected,
        normed_one,
        w_joined,
        gain_one[None, :],
        grad_wo,
        jnp.pad(grad_table, (0, width - table_size))[None],
        experts,
    )
    main_other, returned, first_got, second_got = lax.optimization_barrier(
        (swap(main_other, "dp", 1), returned, first_got, second_got)
    )
    main_mine = (main_mine + main_other.astype(jnp.float32)).astype(jnp.bfloat16)
    shares = trade(main_mine.reshape(experts, -1, width), "expert")

    first_pair = low_sum(first_sum[:2], first_other[:2], first_got)
    second_pair = low_sum(second_sum[:2], second_other[:2], second_got)
    first_got = swap(first_pair[1], "tensor", high_bit)
    second_got = swap(second_pair[1], "tensor", 1)
    output = residual + gate[0].astype(jnp.bfloat16).astype(jnp.float32)[:, None] * dot_nn(
        place_turned, jnp.concatenate(returned)
    )
    shares, grad_got, input_own = lax.optimization_barrier((shares, grad_got, input_own))
    main_mine = spread(low_sum(*shares), "expert").reshape(main_mine.shape)
    grad_normed_one = sum(dot_tn(got, part) for got, part in zip(grad_got, joined_parts))
    inv_own = inverse_rms(input_own)
    input_grad = grad_residual + norm_backward(grad_normed_one, gain_one, input_own * inv_own, inv_own)
    pairs = ((first_pair, first_got), (second_pair, second_got))
    total = jnp.stack([low_sum(pair[0], got) for pair, got in pairs])
    main_mine, total = lax.optimization_barrier((main_mine, total))
    grad_first, grad_second = both_halves(rank, total, swap(total, "dp", 1))
    norm_one = main_mine[rows].astype(jnp.float32)
    norm_one = norm_one + sum(swap(norm_one, "tensor", k) for k in range(1, tensor_count))
    grad_query, grad_key, grad_value, grad_output, shared = joined_whole(
        rank, main_mine, swap(main_mine, "dp", 1), rows, inner
    )

    return (
        output,
        input_grad,
        grad_query.T,
        grad_key.T,
        grad_value.T,
        grad_output,
        shared[grad_wo.shape[1] - inner, :table_size].reshape(local_heads, NUM_BUCKETS).T,
        norm_one,
        shared[experts],
        shared[:experts].T,
        grad_first,
        grad_second,
    )


def solution(mesh):
    return jax.shard_map(
        on_device,
        mesh=mesh,
        in_specs=(
            P(("dp", "expert"), None),
            P(("dp", "expert"), None),
            P(),
            P(None, "tensor"),
            P(None, "tensor"),
            P(None, "tensor"),
            P("tensor", None),
            P(None, "tensor"),
            P(),
            P(),
            P(),
            P(("dp", "expert"), None),
            P("expert", None, "tensor"),
            P("expert", "tensor", None),
        ),
        out_specs=(
            P(("dp", "expert", "tensor"), None),
            P(("dp", "expert", "tensor"), None),
            P(None, "tensor"),
            P(None, "tensor"),
            P(None, "tensor"),
            P("tensor", None),
            P(None, "tensor"),
            P(),
            P(),
            P(),
            P("expert", None, "tensor"),
            P("expert", "tensor", None),
        ),
        check_vma=False,
    )
```
